32 devices in a mesh: shard: 4 (over z), tensor: 4 (over y, x), section: 2 (over core).
Axes of the slice: x: 2, y: 2, z: 4, core: 2. Of those that a mesh axis runs over, the one named last changes fastest.
Arguments:
- grad_parts: bfloat16 [8, 32, 1024, 1024], P(('tensor', 'section'), None, 'shard')
- weights: bfloat16 [32, 1024, 1024], P(None, 'shard', ('tensor', 'section')), may hold values from -6 to 6
- adam_m: float32 [32, 1024, 1024], P(None, 'shard', ('tensor', 'section'))
- adam_v: float32 [32, 1024, 1024], P(None, 'shard', ('tensor', 'section')), may hold values from 0.01 to 1
- left_stat: float32 [96, 1024, 1024], P('shard', None, ('tensor', 'section')), may hold values from -18 to 18
- right_stat: float32 [96, 1024, 1024], P('shard', None, ('tensor', 'section')), may hold values from -18 to 18
- left_root: bfloat16 [32, 1024, 1024], P(None, 'shard', ('tensor', 'section')), as said below
- right_root: bfloat16 [32, 1024, 1024], P(None, 'shard', ('tensor', 'section')), as said below
- block_owner: int32 [32], replicated, may hold values from 0 to 3, as said below
- block_matrix: int32 [32], replicated, may hold values from 0 to 4, as said below
- factors: float32 [832, 2048], P('shard', ('tensor', 'section')), may hold values from -6 to 6
- factor_grad: bfloat16 [832, 2048], P('shard', ('tensor', 'section')), may hold values from -6 to 6
- factor_m: float32 [832, 2048], P('shard', ('tensor', 'section')), may hold values from -3 to 3
- factor_v: float32 [832, 2048], P('shard', ('tensor', 'section')), may hold values from 0.2 to 2
Outputs:
- new_weights: bfloat16 [32, 1024, 1024], P(None, 'shard')
- adam_m_new: float32 [32, 1024, 1024], P(None, 'shard', ('tensor', 'section'))
- adam_v_new: float32 [32, 1024, 1024], P(None, 'shard', ('tensor', 'section'))
- left_new: float32 [96, 1024, 1024], P('shard', None, ('tensor', 'section'))
- right_new: float32 [96, 1024, 1024], P('shard', None, ('tensor', 'section'))
- factors_new: float32 [832, 2048], P('shard', ('tensor', 'section'))
- factor_m_new: float32 [832, 2048], P('shard', ('tensor', 'section'))
- factor_v_new: float32 [832, 2048], P('shard', ('tensor', 'section'))
The draws below stay inside these ranges and needn't reach their ends.
Inputs may be any that keep to these rules, and one draw needn't show every extreme that they name: `block_owner`: no owner holds more than 24 blocks, and some owner holds exactly 24. `block_matrix`: matrices 0 to 3 hold 4 blocks each, all other blocks belong to matrix 4. `left_root`: every block is symmetric. `right_root`: every block is symmetric.
All inputs are finite; a program needn't handle non-finite values.
Results may differ from the reference program's by a relative error of at most 0.014.
Values may be sent and summed in bfloat16 or wider, within the bound.
No kernel may reach another device: no remote copies, remote signals or barrier semaphores. Data moves between devices by JAX's collectives and lax.ppermute only.
A program may use at most 384 MiB of HBM per device.

```python
import math
import jax
import jax.numpy as jnp
from jax import lax

D = 2048
B = 1024
MATS = 5
QD = 4
NBLK = 32
PARTS_SIZE = 8
CAP = 24
SLOTS = 96
ROWS_F = 832
N_SHARD = 4


def log_spread(key, array_shape, high):
    uniform_draw = jax.random.uniform(key, array_shape, jnp.float32)
    return jnp.exp(uniform_draw * math.log(high))


def draw_grad_parts(key, part):
    subkeys = jax.random.split(jax.random.fold_in(key, 3), 6)
    array_shape = (PARTS_SIZE, NBLK, B, B)
    noise_draw = jnp.clip(jax.random.normal(subkeys[0], array_shape, jnp.float32), -6.0, 6.0)
    block_scale = log_spread(subkeys[3], (1, NBLK, 1, 1), 4.0)
    row_scale = log_spread(subkeys[4], (1, NBLK, B, 1), 10.0)
    col_scale = log_spread(subkeys[5], (1, NBLK, 1, B), 10.0)
    return (0.01 / math.sqrt(PARTS_SIZE) * noise_draw * block_scale * row_scale * col_scale).astype(jnp.bfloat16)


def draw_adam_m(key, part):
    subkeys = jax.random.split(jax.random.fold_in(key, 5), 3)
    array_shape = (NBLK, B, B)
    row_place = jnp.arange(B, dtype=jnp.float32).reshape(1, B, 1) / B
    noise_draw = jnp.clip(jax.random.normal(subkeys[0], array_shape, jnp.float32), -6.0, 6.0)
    rising = jnp.exp(math.log(3.0) * row_place)
    row_scale = log_spread(subkeys[1], (NBLK, B, 1), 10.0)
    col_scale = log_spread(subkeys[2], (NBLK, 1, B), 10.0)
    return 0.03 * noise_draw * rising * row_scale * col_scale


def symmetric_root(key):
    subkeys = jax.random.split(key, 2)
    array_shape = (NBLK, B, B)
    raw_draw = jnp.clip(jax.random.normal(subkeys[0], array_shape, jnp.float32), -6.0, 6.0)
    diagonal = jax.random.uniform(subkeys[1], (NBLK, B, 1), jnp.float32, 1.0, 2.0)
    off_diagonal = (raw_draw + jnp.swapaxes(raw_draw, 1, 2)) * (0.4 / math.sqrt(2.0 * B))
    row_ids = jnp.arange(B, dtype=jnp.int32)
    on_diagonal = (row_ids[:, None] == row_ids[None, :])[None, :, :]
    return jnp.where(on_diagonal, diagonal, off_diagonal)


def draw_left_root(key, part):
    return symmetric_root(jax.random.fold_in(key, 7)).astype(jnp.bfloat16)


def draw_right_root(key, part):
    return symmetric_root(jax.random.fold_in(key, 9)).astype(jnp.bfloat16)


def draw_block_owner(key, part):
    subkeys = jax.random.split(jax.random.fold_in(key, 11), 2)
    slot_total = N_SHARD * CAP
    scores = jax.random.permutation(subkeys[0], slot_total).astype(jnp.int32)
    chosen = jax.random.randint(subkeys[1], (), 0, N_SHARD).astype(jnp.int32)
    slot_ids = jnp.arange(slot_total, dtype=jnp.int32)
    scores = jnp.where(slot_ids // CAP == chosen, slot_ids - slot_total, scores)
    ranking = jnp.argsort(scores, stable=True).astype(jnp.int32)
    return (ranking[:NBLK] // CAP).astype(jnp.int32)


def draw_block_matrix(key, part):
    positions = jnp.arange(NBLK, dtype=jnp.int32)
    matrix_ids = jnp.where(positions < 4 * QD, positions // QD, 4).astype(jnp.int32)
    return jax.random.permutation(jax.random.fold_in(key, 13), matrix_ids).astype(jnp.int32)


def shard_levels(own_key, shape, cuts, smallest, high):
    def one(dim, blocks):
        heights = jax.random.uniform(jax.random.fold_in(jax.random.fold_in(own_key, 6), dim), (blocks,), jnp.float32, smallest / len(cuts), high / len(cuts))
        return jnp.repeat(jnp.exp(heights), shape[dim] // blocks).reshape((-1,) + (1,) * (len(shape) - dim - 1))

    factor_of = one(*cuts[0])
    for cut in cuts[1:]:
        factor_of = factor_of * one(*cut)
    return factor_of


def bell_draw(own_key, extent, width, limit, cuts=(), kind=jnp.bfloat16):
    factor_of = shard_levels(own_key, extent, cuts, -0.22, 0.18) if cuts else 1.0
    values = jax.random.normal(own_key, extent, jnp.float32) * width * factor_of
    return jnp.minimum(jnp.maximum(values, -limit), limit).astype(kind)


def setup_inputs(seed: int = 0) -> dict:
    arg_keys = jax.random.split(jax.random.key(seed), 15)
    grad_parts = draw_grad_parts(jax.random.fold_in(arg_keys[14], 71), 0)
    weights = bell_draw(arg_keys[1], (NBLK, B, B), 1.0, 6.0, ((1, 4), (2, 8)))
    adam_m = draw_adam_m(jax.random.fold_in(arg_keys[14], 71), 0)
    adam_v = jnp.clip(jnp.exp(math.log(1.0) - 4.6051702 * jax.random.uniform(arg_keys[3], (NBLK, B, B), jnp.float32) ** shard_levels(arg_keys[3], (NBLK, B, B), ((1, 4), (2, 8)), -0.2, 0.2)), 0.01, 1.0)
    left_stat = bell_draw(arg_keys[4], (SLOTS, B, B), 3.0, 18.0, ((0, 4), (2, 8)), jnp.float32)
    right_stat = bell_draw(arg_keys[5], (SLOTS, B, B), 3.0, 18.0, ((0, 4), (2, 8)), jnp.float32)
    left_root = draw_left_root(jax.random.fold_in(arg_keys[14], 71), 0)
    right_root = draw_right_root(jax.random.fold_in(arg_keys[14], 71), 0)
    block_owner = draw_block_owner(jax.random.fold_in(arg_keys[14], 71), 0)
    block_matrix = draw_block_matrix(jax.random.fold_in(arg_keys[14], 71), 0)
    factors = bell_draw(arg_keys[10], (ROWS_F, D), 1.0, 6.0, ((0, 4), (1, 8)), jnp.float32)
    factor_grad = bell_draw(arg_keys[11], (ROWS_F, D), 1.0, 6.0, ((0, 4), (1, 8)))
    factor_m = bell_draw(arg_keys[12], (ROWS_F, D), 0.5, 3.0, ((0, 4), (1, 8)), jnp.float32)
    factor_v = jnp.clip(jnp.exp(math.log(2.0) - 2.3025851 * jax.random.uniform(arg_keys[13], (ROWS_F, D), jnp.float32) ** shard_levels(arg_keys[13], (ROWS_F, D), ((0, 4), (1, 8)), -0.2, 0.2)), 0.2, 2.0)
    return dict(grad_parts=grad_parts, weights=weights, adam_m=adam_m, adam_v=adam_v, left_stat=left_stat, right_stat=right_stat, left_root=left_root, right_root=right_root, block_owner=block_owner, block_matrix=block_matrix, factors=factors, factor_grad=factor_grad, factor_m=factor_m, factor_v=factor_v)


BETA_ONE = 0.9
BETA_TWO = 0.95
BETA_STAT = 0.95
LEARNING = 0.1
DECAY_RATE = 0.1
EPSILON = 1e-08
FLOOR_RATE = 1e-06
CORRECT_ONE = 1.0 - 0.9 ** 10
CORRECT_TWO = 1.0 - 0.95 ** 10

def adam_direction(grad_float, moment, second):
    moment_new = BETA_ONE * moment + (1.0 - BETA_ONE) * grad_float
    second_new = BETA_TWO * second + (1.0 - BETA_TWO) * grad_float * grad_float
    direction = moment_new / CORRECT_ONE / (jnp.sqrt(second_new / CORRECT_TWO) + EPSILON)
    return (moment_new, second_new, direction)

def slot_numbers(block_owner, capacity):
    positions = jnp.arange(block_owner.shape[0], dtype=jnp.int32)
    earlier = (block_owner[:, None] == block_owner[None, :]) & (positions[None, :] < positions[:, None])
    return (block_owner * capacity + lax.optimization_barrier(jnp.sum(earlier.astype(jnp.int32), axis=1))).astype(jnp.int32)

def reference(grad_parts, weights, adam_m, adam_v, left_stat, right_stat, left_root, right_root, block_owner, block_matrix, factors, factor_grad, factor_m, factor_v):
    gradient = lax.optimization_barrier(jnp.sum(grad_parts.astype(jnp.float32), axis=0)).astype(jnp.bfloat16)
    gradient = lax.optimization_barrier(gradient)
    grad_float = gradient.astype(jnp.float32)
    adam_m_new, adam_v_new, direction = adam_direction(grad_float, adam_m, adam_v)
    onehot = (block_matrix[:, None] == jnp.arange(MATS, dtype=jnp.int32)[None, :]).astype(jnp.float32)
    adam_norm = lax.optimization_barrier(jnp.sum(lax.optimization_barrier(jnp.sum(direction * direction, axis=(1, 2)))[:, None] * onehot, axis=0))

    def per_block(operands):
        block_grad, block_left, block_right = operands
        gram_left = jnp.dot(block_grad, block_grad.T, preferred_element_type=jnp.float32)
        gram_right = jnp.dot(block_grad.T, block_grad, preferred_element_type=jnp.float32)
        mixed = jnp.dot(block_left, block_grad, preferred_element_type=jnp.float32).astype(jnp.bfloat16)
        precond = jnp.dot(mixed, block_right, preferred_element_type=jnp.float32)
        return (gram_left, gram_right, precond)
    gram_left, gram_right, precond = lax.map(per_block, (gradient, left_root, right_root))
    slot = slot_numbers(block_owner, CAP)
    left_new = (BETA_STAT * left_stat).at[slot].set(BETA_STAT * left_stat[slot] + (1.0 - BETA_STAT) * gram_left)
    right_new = (BETA_STAT * right_stat).at[slot].set(BETA_STAT * right_stat[slot] + (1.0 - BETA_STAT) * gram_right)
    shampoo_norm = lax.optimization_barrier(jnp.sum(lax.optimization_barrier(jnp.sum(precond * precond, axis=(1, 2)))[:, None] * onehot, axis=0))
    counts = lax.optimization_barrier(jnp.sum(onehot, axis=0)) * float(B * B)
    graft_scale = jnp.sqrt(adam_norm / (shampoo_norm + FLOOR_RATE * counts))
    block_scale = lax.optimization_barrier(jnp.sum(onehot * graft_scale[None, :], axis=1))
    precond_half = lax.optimization_barrier(precond.astype(jnp.bfloat16)).astype(jnp.float32)
    weights_float = weights.astype(jnp.float32)
    new_weights = (weights_float - LEARNING * (block_scale[:, None, None] * precond_half + DECAY_RATE * weights_float)).astype(jnp.bfloat16)
    factor_m_new, factor_v_new, factor_step = adam_direction(factor_grad.astype(jnp.float32), factor_m, factor_v)
    factors_new = factors - LEARNING * (factor_step + DECAY_RATE * factors)
    return (new_weights, adam_m_new, adam_v_new, left_new, right_new, factors_new, factor_m_new, factor_v_new)
```

```python
import functools

import jax
import jax.numpy as jnp
from jax import lax
from jax.experimental import pallas as pl
from jax.experimental.pallas import tpu as pltpu
from jax.sharding import PartitionSpec as P

MATS = 5

BETA_ONE = 0.9
BETA_TWO = 0.95
BETA_STAT = 0.95
LEARNING = 0.1
DECAY_RATE = 0.1
EPSILON = 1e-08
FLOOR_RATE = 1e-06
CORRECT_ONE = 1.0 - 0.9**10
CORRECT_TWO = 1.0 - 0.95**10

GROUP = ("tensor", "section")
ALL = ("shard", "tensor", "section")
VMEM_LIMIT = 48 * 1024 * 1024
LANES = 128


def params():
    return pltpu.CompilerParams(vmem_limit_bytes=VMEM_LIMIT)


def adam_direction(grad_float, moment, second):
    moment_new = BETA_ONE * moment + (1.0 - BETA_ONE) * grad_float
    second_new = BETA_TWO * second + (1.0 - BETA_TWO) * grad_float * grad_float
    direction = moment_new / CORRECT_ONE / (jnp.sqrt(second_new / CORRECT_TWO) + EPSILON)
    return (moment_new, second_new, direction)


def reorder_kernel(order, block, out):
    out[...] = block[...]


def reorder(blocks, order):
    count = order.shape[0]
    tile = blocks.shape[1:]
    spec = (1,) + tile
    return pl.pallas_call(
        reorder_kernel,
        grid_spec=pltpu.PrefetchScalarGridSpec(
            num_scalar_prefetch=1,
            grid=(count,),
            in_specs=[pl.BlockSpec(spec, lambda i, order: (order[i], 0, 0))],
            out_specs=pl.BlockSpec(spec, lambda i, order: (i, 0, 0)),
        ),
        out_shape=jax.ShapeDtypeStruct((count,) + tile, blocks.dtype),
        compiler_params=params(),
        cost_estimate=pl.CostEstimate(
            flops=0, bytes_accessed=2 * blocks.size * blocks.dtype.itemsize, transcendentals=0
        ),
    )(order, blocks)


def adam_kernel(place, grad, moment, second, moment_out, second_out, total):
    moment_new, second_new, direction = adam_direction(
        grad[0].astype(jnp.float32), moment[0], second[0]
    )
    moment_out[0] = moment_new
    second_out[0] = second_new
    total[0] = jnp.sum(direction * direction, axis=0, keepdims=True)


def adam(grad_tiles, place, moment, second):
    count, rows, cols = moment.shape
    own = pl.BlockSpec((1, rows, cols), lambda i, place: (i, 0, 0))
    return pl.pallas_call(
        adam_kernel,
        grid_spec=pltpu.PrefetchScalarGridSpec(
            num_scalar_prefetch=1,
            grid=(count,),
            in_specs=[
                pl.BlockSpec((1, rows, cols), lambda i, place: (place[i], 0, 0)),
                own,
                own,
            ],
            out_specs=[own, own, pl.BlockSpec((1, 1, cols), lambda i, place: (i, 0, 0))],
        ),
        out_shape=[
            jax.ShapeDtypeStruct(moment.shape, jnp.float32),
            jax.ShapeDtypeStruct(moment.shape, jnp.float32),
            jax.ShapeDtypeStruct((count, 1, cols), jnp.float32),
        ],
        compiler_params=params(),
        cost_estimate=pl.CostEstimate(
            flops=20 * moment.size, bytes_accessed=18 * moment.size, transcendentals=moment.size
        ),
    )(place, grad_tiles, moment, second)


def gram_kernel(chosen, grad, out):
    parts, _, rows, width = grad.shape
    size = parts * rows
    whole = grad[:, 0].reshape(size, width)
    turned = whole.T
    step = 2 * LANES
    for start in range(0, size, step):
        left = lax.dot_general(
            whole,
            whole[start : start + step, :],
            (((1,), (1,)), ((), ())),
            preferred_element_type=jnp.float32,
        ).astype(jnp.bfloat16)
        right = lax.dot_general(
            turned,
            whole[:, start : start + step],
            (((1,), (0,)), ((), ())),
            preferred_element_type=jnp.float32,
        ).astype(jnp.bfloat16)
        for half in range(2):
            slab = start // LANES + half
            out[slab, 0, 0] = left[:, half * LANES : (half + 1) * LANES]
            out[slab, 0, 1] = right[:, half * LANES : (half + 1) * LANES]


def grams(grad_blocks, chosen):
    shards, per, rows, width = grad_blocks.shape
    size = shards * rows
    slabs = size // LANES
    count = chosen.shape[0]
    return pl.pallas_call(
        gram_kernel,
        grid_spec=pltpu.PrefetchScalarGridSpec(
            num_scalar_prefetch=1,
            grid=(count,),
            in_specs=[
                pl.BlockSpec((shards, 1, rows, width), lambda j, chosen: (0, chosen[j], 0, 0))
            ],
            out_specs=pl.BlockSpec(
                (slabs, 1, 2, size, LANES), lambda j, chosen: (0, j, 0, 0, 0)
            ),
        ),
        out_shape=jax.ShapeDtypeStruct((slabs, count, 2, size, LANES), jnp.bfloat16),
        compiler_params=params(),
        cost_estimate=pl.CostEstimate(
            flops=count * 4 * size**3, bytes_accessed=count * 6 * size * size, transcendentals=0
        ),
    )(chosen, grad_blocks)


def stat_kernel(
    source, entry, filled, left_stat, right_stat, left_gram, right_gram, left_out, right_out
):
    full = filled[pl.program_id(0)] > 0
    left = left_gram[0, 0, 0].astype(jnp.float32)
    right = right_gram[0, 0, 0].astype(jnp.float32)
    left_out[0] = BETA_STAT * left_stat[0] + jnp.where(full, (1.0 - BETA_STAT) * left, 0.0)
    right_out[0] = BETA_STAT * right_stat[0] + jnp.where(full, (1.0 - BETA_STAT) * right, 0.0)


def refresh(left_stat, right_stat, received, source, entry, filled):
    slots, size, cols = left_stat.shape
    own = pl.BlockSpec((1, size, cols), lambda r, source, entry, filled: (r, 0, 0))
    gram = (1, 1, 1, size, cols)
    return pl.pallas_call(
        stat_kernel,
        grid_spec=pltpu.PrefetchScalarGridSpec(
            num_scalar_prefetch=3,
            grid=(slots,),
            in_specs=[
                own,
                own,
                pl.BlockSpec(
                    gram, lambda r, source, entry, filled: (source[r], entry[r], 0, 0, 0)
                ),
                pl.BlockSpec(
                    gram, lambda r, source, entry, filled: (source[r], entry[r], 1, 0, 0)
                ),
            ],
            out_specs=[own, own],
        ),
        out_shape=[jax.ShapeDtypeStruct(left_stat.shape, jnp.float32)] * 2,
        compiler_params=params(),
        cost_estimate=pl.CostEstimate(
            flops=6 * left_stat.size, bytes_accessed=20 * left_stat.size, transcendentals=0
        ),
    )(source, entry, filled, left_stat, right_stat, received, received)


def precond_kernel(left, grad, right, out, total):
    slabs, _, rows, cols = left.shape
    parts = grad.shape[0]
    width = grad.shape[3]
    left_rows = jnp.concatenate([left[s, 0] for s in range(slabs)], axis=1)
    whole = grad[:, 0].reshape(parts * rows, width)
    mixed = jnp.dot(left_rows, whole, preferred_element_type=jnp.float32).astype(jnp.bfloat16)
    total[...] = jnp.zeros_like(total)
    step = 2
    for start in range(0, slabs, step):
        columns = jnp.concatenate(
            [right[:, s, 0].reshape(parts * rows, cols) for s in range(start, start + step)], axis=1
        )
        piece = jnp.dot(mixed, columns, preferred_element_type=jnp.float32)
        out[0, :, start * cols : (start + step) * cols] = piece.astype(jnp.bfloat16)
        square = jnp.sum(piece * piece, axis=0, keepdims=True)
        total[0] += square[:, :cols] + square[:, cols:]


def precondition(left, grad_blocks, right):
    shards, per, rows, width = grad_blocks.shape
    slabs, _, _, cols = left.shape
    size = shards * rows
    return pl.pallas_call(
        precond_kernel,
        grid=(per,),
        in_specs=[
            pl.BlockSpec((slabs, 1, rows, cols), lambda m: (0, m, 0, 0)),
            pl.BlockSpec((shards, 1, rows, width), lambda m: (0, m, 0, 0)),
            pl.BlockSpec((shards, slabs, 1, rows, cols), lambda m: (0, 0, m, 0, 0)),
        ],
        out_specs=[
            pl.BlockSpec((1, rows, width), lambda m: (m, 0, 0)),
            pl.BlockSpec((1, 1, cols), lambda m: (m, 0, 0)),
        ],
        out_shape=[
            jax.ShapeDtypeStruct((per, rows, width), jnp.bfloat16),
            jax.ShapeDtypeStruct((per, 1, cols), jnp.float32),
        ],
        compiler_params=params(),
        cost_estimate=pl.CostEstimate(
            flops=per * 4 * rows * size * size,
            bytes_accessed=per * (4 * size * size + 4 * rows * size),
            transcendentals=0,
        ),
    )(left, grad_blocks, right)


def update_kernel(scale, weights, precond, out):
    slabs = weights.shape[0]
    factor = scale[pl.program_id(0)]
    old = jnp.concatenate([weights[s, 0] for s in range(slabs)], axis=1).astype(jnp.float32)
    step = factor * precond[0].astype(jnp.float32) + DECAY_RATE * old
    out[0] = (old - LEARNING * step).astype(jnp.bfloat16)


def update(weights, precond, scale):
    slabs, per, rows, cols = weights.shape
    width = slabs * cols
    own = pl.BlockSpec((1, rows, width), lambda m, scale: (m, 0, 0))
    return pl.pallas_call(
        update_kernel,
        grid_spec=pltpu.PrefetchScalarGridSpec(
            num_scalar_prefetch=1,
            grid=(per,),
            in_specs=[
                pl.BlockSpec((slabs, 1, rows, cols), lambda m, scale: (0, m, 0, 0)),
                own,
            ],
            out_specs=own,
        ),
        out_shape=jax.ShapeDtypeStruct((per, rows, width), jnp.bfloat16),
        compiler_params=params(),
        cost_estimate=pl.CostEstimate(
            flops=5 * weights.size, bytes_accessed=6 * weights.size, transcendentals=0
        ),
    )(scale, weights, precond)


def shards(
    grad_parts,
    weights,
    adam_m,
    adam_v,
    left_stat,
    right_stat,
    left_root,
    right_root,
    block_owner,
    block_matrix,
    factors,
    factor_grad,
    factor_m,
    factor_v,
):
    capacity = left_stat.shape[0]
    blocks, rows, cols = weights.shape
    size = left_stat.shape[1]
    group = size // cols
    per = blocks // group
    sends = -(-capacity // group)
    owner_index = lax.axis_index("shard")
    group_index = lax.axis_index(GROUP)

    ids = jnp.arange(blocks, dtype=jnp.int32)
    before = (block_owner[None, :] < block_owner[:, None]) | (
        (block_owner[None, :] == block_owner[:, None]) & (ids[None, :] < ids[:, None])
    )
    position = jnp.sum(before.astype(jnp.int32), axis=1)
    place = (position % group) * per + position // group
    order = jnp.sum(jnp.where(place[None, :] == ids[:, None], ids[None, :], 0), axis=1)

    first = jnp.sum((block_owner < owner_index).astype(jnp.int32))
    held = jnp.sum((block_owner == owner_index).astype(jnp.int32))
    own_entry = (first - group_index + group - 1) // group
    chosen = jnp.minimum(own_entry + jnp.arange(sends, dtype=jnp.int32), per - 1)
    ranks = jnp.arange(capacity, dtype=jnp.int32)
    source = (first + ranks) % group
    entry = (first + ranks) // group - (first - source + group - 1) // group
    filled = (ranks < held).astype(jnp.int32)
    entry = jnp.where(ranks < held, entry, 0)

    def deal(tiles):
        sent = reorder(tiles, order).reshape(group, per, rows, cols)
        return lax.all_to_all(sent, GROUP, split_axis=0, concat_axis=0, tiled=True)

    partials = reorder(grad_parts[0], order)
    gradient = lax.psum_scatter(partials, GROUP, scatter_dimension=0, tiled=True)
    right_dealt = deal(right_root)
    right_blocks = lax.all_gather(right_dealt, "shard", axis=0)
    left_dealt = deal(left_root)
    weights_dealt = deal(weights)
    grad_blocks = lax.all_gather(gradient, "shard", axis=0)

    tiles = jnp.transpose(gradient.reshape(per, rows, group, cols), (2, 0, 1, 3))
    tiles = lax.all_to_all(tiles, GROUP, split_axis=0, concat_axis=0, tiled=True)
    adam_m_new, adam_v_new, adam_total = adam(
        tiles.reshape(blocks, rows, cols), place, adam_m, adam_v
    )

    precond, precond_total = precondition(left_dealt, grad_blocks, right_blocks)

    matrix_range = jnp.arange(MATS, dtype=jnp.int32)
    onehot = (block_matrix[:, None] == matrix_range[None, :]).astype(jnp.float32)
    own_order = lax.dynamic_slice_in_dim(order, group_index * per, per)
    own_onehot = jnp.sum(
        jnp.where((own_order[:, None] == ids[None, :])[:, :, None], onehot[None, :, :], 0.0), axis=1
    )
    adam_part = jnp.sum(jnp.sum(adam_total, axis=(1, 2))[:, None] * onehot, axis=0)
    shampoo_part = jnp.sum(jnp.sum(precond_total, axis=(1, 2))[:, None] * own_onehot, axis=0)
    adam_norm, shampoo_norm = lax.psum((adam_part, shampoo_part), ALL)
    counts = jnp.sum(onehot, axis=0) * float(size * size)
    graft_scale = jnp.sqrt(adam_norm / (shampoo_norm + FLOOR_RATE * counts))
    block_scale = jnp.sum(own_onehot * graft_scale[None, :], axis=1)

    updated = update(weights_dealt, precond, block_scale)
    gathered = lax.all_gather(updated, GROUP, axis=0, tiled=True)
    new_weights = reorder(gathered, place)

    slabs = grams(grad_blocks, chosen)
    received = lax.all_to_all(slabs, GROUP, split_axis=0, concat_axis=0, tiled=True)
    left_new, right_new = refresh(left_stat, right_stat, received, source, entry, filled)

    factor_m_new, factor_v_new, factor_step = adam_direction(
        factor_grad.astype(jnp.float32), factor_m, factor_v
    )
    factors_new = factors - LEARNING * (factor_step + DECAY_RATE * factors)
    return (
        new_weights,
        adam_m_new,
        adam_v_new,
        left_new,
        right_new,
        factors_new,
        factor_m_new,
        factor_v_new,
    )


def solution(mesh):
    tile = P(None, "shard", GROUP)
    stat = P("shard", None, GROUP)
    factor = P("shard", GROUP)
    in_specs = (P(GROUP, None, "shard", None), tile, tile, tile, stat, stat, tile, tile, P(), P())
    out_specs = (P(None, "shard", None), tile, tile, stat, stat)
    return jax.shard_map(
        shards,
        mesh=mesh,
        in_specs=in_specs + (factor,) * 4,
        out_specs=out_specs + (factor,) * 3,
        check_vma=False,
    )
```

```python
import functools

import jax
import jax.numpy as jnp
from jax import lax
from jax.experimental import pallas as pl
from jax.experimental.pallas import tpu as pltpu
from jax.sharding import PartitionSpec as P

MATS = 5

BETA_ONE = 0.9
BETA_TWO = 0.95
BETA_STAT = 0.95
LEARNING = 0.1
DECAY_RATE = 0.1
EPSILON = 1e-08
FLOOR_RATE = 1e-06
CORRECT_ONE = 1.0 - 0.9**10
CORRECT_TWO = 1.0 - 0.95**10

GROUP = ("tensor", "section")
ALL = ("shard", "tensor", "section")
VMEM_LIMIT = 48 * 1024 * 1024
LANES = 128


def params():
    return pltpu.CompilerParams(vmem_limit_bytes=VMEM_LIMIT)


def adam_direction(grad_float, moment, second):
    moment_new = BETA_ONE * moment + (1.0 - BETA_ONE) * grad_float
    second_new = BETA_TWO * second + (1.0 - BETA_TWO) * grad_float * grad_float
    direction = moment_new / CORRECT_ONE / (jnp.sqrt(second_new / CORRECT_TWO) + EPSILON)
    return (moment_new, second_new, direction)


def reorder_kernel(order, block, out):
    out[...] = block[...]


def reorder(blocks, order):
    count = order.shape[0]
    tile = blocks.shape[1:]
    spec = (1,) + tile
    return pl.pallas_call(
        reorder_kernel,
        grid_spec=pltpu.PrefetchScalarGridSpec(
            num_scalar_prefetch=1,
            grid=(count,),
            in_specs=[pl.BlockSpec(spec, lambda i, order: (order[i], 0, 0))],
            out_specs=pl.BlockSpec(spec, lambda i, order: (i, 0, 0)),
        ),
        out_shape=jax.ShapeDtypeStruct((count,) + tile, blocks.dtype),
        compiler_params=params(),
        cost_estimate=pl.CostEstimate(
            flops=0, bytes_accessed=2 * blocks.size * blocks.dtype.itemsize, transcendentals=0
        ),
    )(order, blocks)


def adam_kernel(place, grad, moment, second, moment_out, second_out, total):
    moment_new, second_new, direction = adam_direction(
        grad[0].astype(jnp.float32), moment[0], second[0]
    )
    moment_out[0] = moment_new
    second_out[0] = second_new
    total[0] = jnp.sum(direction * direction, axis=0, keepdims=True)


def adam(grad_tiles, place, moment, second):
    count, rows, cols = moment.shape
    own = pl.BlockSpec((1, rows, cols), lambda i, place: (i, 0, 0))
    return pl.pallas_call(
        adam_kernel,
        grid_spec=pltpu.PrefetchScalarGridSpec(
            num_scalar_prefetch=1,
            grid=(count,),
            in_specs=[
                pl.BlockSpec((1, rows, cols), lambda i, place: (place[i], 0, 0)),
                own,
                own,
            ],
            out_specs=[own, own, pl.BlockSpec((1, 1, cols), lambda i, place: (i, 0, 0))],
        ),
        out_shape=[
            jax.ShapeDtypeStruct(moment.shape, jnp.float32),
            jax.ShapeDtypeStruct(moment.shape, jnp.float32),
            jax.ShapeDtypeStruct((count, 1, cols), jnp.float32),
        ],
        compiler_params=params(),
        cost_estimate=pl.CostEstimate(
            flops=20 * moment.size, bytes_accessed=18 * moment.size, transcendentals=moment.size
        ),
    )(place, grad_tiles, moment, second)


def gram_kernel(chosen, *refs):
    grads, out, held = refs[:-2], refs[-2], refs[-1]
    size = held.shape[0]
    for index, grad in enumerate(grads):

        @pl.when(chosen[0] == index)
        def _(grad=grad):
            held[...] = grad[...].reshape(size, size)

    whole = held[...]
    turned = whole.T
    step = 2 * LANES
    for start in range(0, size, step):
        left = lax.dot_general(
            whole,
            whole[start : start + step, :],
            (((1,), (1,)), ((), ())),
            preferred_element_type=jnp.float32,
        ).astype(jnp.bfloat16)
        right = lax.dot_general(
            turned,
            whole[:, start : start + step],
            (((1,), (0,)), ((), ())),
            preferred_element_type=jnp.float32,
        ).astype(jnp.bfloat16)
        for half in range(2):
            slab = start // LANES + half
            out[slab, 0] = left[:, half * LANES : (half + 1) * LANES]
            out[slab, 1] = right[:, half * LANES : (half + 1) * LANES]


def grams(candidates, chosen):
    shards, rows, width = candidates[0].shape
    size = shards * rows
    slabs = size // LANES
    return pl.pallas_call(
        gram_kernel,
        grid_spec=pltpu.PrefetchScalarGridSpec(
            num_scalar_prefetch=1,
            grid=(1,),
            in_specs=[pl.BlockSpec((shards, rows, width), lambda j, chosen: (0, 0, 0))]
            * len(candidates),
            out_specs=pl.BlockSpec((slabs, 2, size, LANES), lambda j, chosen: (0, 0, 0, 0)),
            scratch_shapes=[pltpu.VMEM((size, size), jnp.bfloat16)],
        ),
        out_shape=jax.ShapeDtypeStruct((slabs, 2, size, LANES), jnp.bfloat16),
        compiler_params=params(),
        cost_estimate=pl.CostEstimate(
            flops=4 * size**3, bytes_accessed=6 * size * size, transcendentals=0
        ),
    )(chosen.reshape(1), *candidates)


def stat_kernel(base, source, filled, left_stat, right_stat, left_gram, right_gram, *refs):
    left_out, right_out = refs[-2:]
    full = filled[pl.program_id(0)] > 0
    left = left_gram[0, 0].astype(jnp.float32)
    right = right_gram[0, 0].astype(jnp.float32)
    left_out[0] = BETA_STAT * left_stat[0] + jnp.where(full, (1.0 - BETA_STAT) * left, 0.0)
    right_out[0] = BETA_STAT * right_stat[0] + jnp.where(full, (1.0 - BETA_STAT) * right, 0.0)


def refresh(left_stat, right_stat, received, base, source, filled, earlier):
    slots, size, cols = left_stat.shape
    count = source.shape[0]
    own = pl.BlockSpec((1, size, cols), lambda r, base, source, filled: (base[0] + r, 0, 0))
    gram = (1, 1, size, cols)
    shape = jax.ShapeDtypeStruct(left_stat.shape, jnp.float32)
    return pl.pallas_call(
        stat_kernel,
        grid_spec=pltpu.PrefetchScalarGridSpec(
            num_scalar_prefetch=3,
            grid=(count,),
            in_specs=[
                own,
                own,
                pl.BlockSpec(gram, lambda r, base, source, filled: (source[r], 0, 0, 0)),
                pl.BlockSpec(gram, lambda r, base, source, filled: (source[r], 1, 0, 0)),
            ]
            + [pl.BlockSpec(memory_space=pl.ANY)] * len(earlier),
            out_specs=[own, own],
        ),
        out_shape=[shape, shape],
        input_output_aliases={7 + i: i for i in range(len(earlier))},
        compiler_params=params(),
        cost_estimate=pl.CostEstimate(
            flops=6 * count * size * cols, bytes_accessed=20 * count * size * cols, transcendentals=0
        ),
    )(base.reshape(1), source, filled, left_stat, right_stat, received, received, *earlier)


def precond_kernel(left, grad, right, out, total):
    slabs, _, rows, cols = left.shape
    parts, _, width = grad.shape
    left_rows = jnp.concatenate([left[s, 0] for s in range(slabs)], axis=1)
    whole = grad[...].reshape(parts * rows, width)
    mixed = jnp.dot(left_rows, whole, preferred_element_type=jnp.float32).astype(jnp.bfloat16)
    total[...] = jnp.zeros_like(total)
    step = 2
    for start in range(0, slabs, step):
        columns = jnp.concatenate(
            [right[:, s].reshape(parts * rows, cols) for s in range(start, start + step)], axis=1
        )
        piece = jnp.dot(mixed, columns, preferred_element_type=jnp.float32)
        out[:, start * cols : (start + step) * cols] = piece.astype(jnp.bfloat16)
        square = jnp.sum(piece * piece, axis=0, keepdims=True)
        total[...] += square[:, :cols] + square[:, cols:]


def precondition(left, number, grad_block, right):
    shards, rows, width = grad_block.shape
    slabs, _, _, cols = left.shape
    size = shards * rows
    return pl.pallas_call(
        precond_kernel,
        grid=(1,),
        in_specs=[
            pl.BlockSpec((slabs, 1, rows, cols), lambda i: (0, number, 0, 0)),
            pl.BlockSpec((shards, rows, width), lambda i: (0, 0, 0)),
            pl.BlockSpec((shards, slabs, rows, cols), lambda i: (0, 0, 0, 0)),
        ],
        out_specs=[
            pl.BlockSpec((rows, width), lambda i: (0, 0)),
            pl.BlockSpec((1, cols), lambda i: (0, 0)),
        ],
        out_shape=[
            jax.ShapeDtypeStruct((rows, width), jnp.bfloat16),
            jax.ShapeDtypeStruct((1, cols), jnp.float32),
        ],
        compiler_params=params(),
        cost_estimate=pl.CostEstimate(
            flops=4 * rows * size * size,
            bytes_accessed=4 * size * size + 4 * rows * size,
            transcendentals=0,
        ),
    )(left, grad_block, right)


def update_kernel(scale, weights, precond, out):
    slabs = weights.shape[0]
    factor = scale[pl.program_id(0)]
    old = jnp.concatenate([weights[s, 0] for s in range(slabs)], axis=1).astype(jnp.float32)
    step = factor * precond[0].astype(jnp.float32) + DECAY_RATE * old
    out[0] = (old - LEARNING * step).astype(jnp.bfloat16)


def update(weights, precond, scale):
    slabs, per, rows, cols = weights.shape
    width = slabs * cols
    own = pl.BlockSpec((1, rows, width), lambda m, scale: (m, 0, 0))
    return pl.pallas_call(
        update_kernel,
        grid_spec=pltpu.PrefetchScalarGridSpec(
            num_scalar_prefetch=1,
            grid=(per,),
            in_specs=[
                pl.BlockSpec((slabs, 1, rows, cols), lambda m, scale: (0, m, 0, 0)),
                own,
            ],
            out_specs=own,
        ),
        out_shape=jax.ShapeDtypeStruct((per, rows, width), jnp.bfloat16),
        compiler_params=params(),
        cost_estimate=pl.CostEstimate(
            flops=5 * weights.size, bytes_accessed=6 * weights.size, transcendentals=0
        ),
    )(scale, weights, precond)


def pair_kernel(picked, first, second, third, fourth, received, send_a, keep_a, send_b, keep_b):
    half = first.shape[1] // 2
    added = [
        (own[0].astype(jnp.float32) + received[u].astype(jnp.float32)).astype(jnp.bfloat16)
        for u, own in enumerate((first, second, third, fourth))
    ]
    for ref, chosen, start in (
        (send_a, (1, 3), 0),
        (keep_a, (0, 2), 0),
        (send_b, (2, 3), half),
        (keep_b, (0, 1), half),
    ):
        for i, u in enumerate(chosen):
            ref[i] = added[u][start : start + half]


def add_pair(partials, received, picked):
    _, rows, width = partials.shape
    half = jax.ShapeDtypeStruct((2, rows // 2, width), partials.dtype)

    def own(u):
        return pl.BlockSpec((1, rows, width), lambda i, picked: (picked[u], 0, 0))

    return pl.pallas_call(
        pair_kernel,
        grid_spec=pltpu.PrefetchScalarGridSpec(
            num_scalar_prefetch=1,
            grid=(1,),
            in_specs=[own(0), own(1), own(2), own(3)]
            + [pl.BlockSpec((4, rows, width), lambda i, picked: (0, 0, 0))],
            out_specs=[pl.BlockSpec(half.shape, lambda i, picked: (0, 0, 0))] * 4,
        ),
        out_shape=[half] * 4,
        compiler_params=params(),
        cost_estimate=pl.CostEstimate(
            flops=4 * rows * width, bytes_accessed=24 * rows * width, transcendentals=0
        ),
    )(picked, partials, partials, partials, partials, received)


def add(one, two):
    return (one.astype(jnp.float32) + two.astype(jnp.float32)).astype(jnp.bfloat16)


def swap(array, bit):
    devices = lax.axis_size("tensor")
    return lax.ppermute(array, "tensor", [(t, t ^ bit) for t in range(devices)])


def sum_blocks(partials, picked):
    tensors, cores = lax.axis_size("tensor"), lax.axis_size("section")
    if (tensors, cores) != (4, 2):
        return lax.psum_scatter(reorder(partials, picked), GROUP, scatter_dimension=0)
    core = lax.axis_index("section")
    relative = jnp.arange(tensors, dtype=jnp.int32) ^ lax.axis_index("tensor")
    mine = jnp.take(picked, relative * cores + core)
    other = jnp.take(picked, relative * cores + 1 - core)
    received = lax.ppermute(reorder(partials, other), "section", [(0, 1), (1, 0)])
    send_a, keep_a, send_b, keep_b = add_pair(partials, received, mine)
    sum_a = add(keep_a, swap(send_a, 1))
    sum_b = add(keep_b, swap(send_b, 2))
    last_a = add(sum_a[0], swap(sum_a[1], 2))
    last_b = add(sum_b[0], swap(sum_b[1], 1))
    return jnp.concatenate([last_a, last_b], axis=0)


def shards(
    grad_parts,
    weights,
    adam_m,
    adam_v,
    left_stat,
    right_stat,
    left_root,
    right_root,
    block_owner,
    block_matrix,
    factors,
    factor_grad,
    factor_m,
    factor_v,
):
    capacity = left_stat.shape[0]
    blocks, rows, cols = weights.shape
    size = left_stat.shape[1]
    group = size // cols
    per = blocks // group
    sends = -(-capacity // group)
    owner_index = lax.axis_index("shard")
    group_index = lax.axis_index(GROUP)
    owner_count = lax.axis_size("shard")

    ids = jnp.arange(blocks, dtype=jnp.int32)
    owners = jnp.arange(owner_count, dtype=jnp.int32)
    loads = jnp.sum((block_owner[None, :] == owners[:, None]).astype(jnp.int32), axis=1)
    heavy = jnp.min(jnp.where(loads == jnp.max(loads), owners, owner_count))
    turn = (block_owner - heavy) % owner_count
    own_turn = (owner_index - heavy) % owner_count
    before = (turn[None, :] < turn[:, None]) | (
        (turn[None, :] == turn[:, None]) & (ids[None, :] < ids[:, None])
    )
    position = jnp.sum(before.astype(jnp.int32), axis=1)
    place = (position % group) * per + position // group
    order = jnp.sum(jnp.where(place[None, :] == ids[:, None], ids[None, :], 0), axis=1)

    first = jnp.sum((turn < own_turn).astype(jnp.int32))
    held = jnp.sum((turn == own_turn).astype(jnp.int32))
    early = sends - 1 if blocks - capacity <= group else 0
    is_heavy = own_turn == 0
    own_entry = (first - group_index + group - 1) // group

    def deal(tiles):
        sent = reorder(tiles, order).reshape(group, per, rows, cols)
        return lax.all_to_all(sent, GROUP, split_axis=0, concat_axis=0, tiled=True)

    right_dealt = deal(right_root)
    by_entry = order.reshape(group, per)
    steps = list(range(early)) + list(range(early + 1, per)) + [early]
    gradient, grad_blocks = {}, {}
    for m in steps:
        gradient[m] = sum_blocks(grad_parts[0], by_entry[:, m])
        grad_blocks[m] = lax.all_gather(gradient[m], "shard", axis=0)
    right_blocks = [lax.all_gather(right_dealt[:, m], "shard", axis=0) for m in range(per)]
    left_dealt = deal(left_root)
    weights_dealt = deal(weights)

    tiles = jnp.stack([gradient[m].reshape(rows, group, cols) for m in range(per)])
    tiles = jnp.transpose(tiles, (2, 0, 1, 3))
    tiles = lax.all_to_all(tiles, GROUP, split_axis=0, concat_axis=0, tiled=True)
    adam_m_new, adam_v_new, adam_total = adam(
        tiles.reshape(blocks, rows, cols), place, adam_m, adam_v
    )

    stats = ()
    for j in range(early):
        slabs = grams([grad_blocks[j]], jnp.int32(0))
        received = lax.all_to_all(slabs, GROUP, split_axis=0, concat_axis=0, tiled=True)
        base = jnp.where(is_heavy, j, j + 1) * group
        source = jnp.arange(group, dtype=jnp.int32)
        filled = jnp.where(is_heavy, 1, 0) * jnp.ones_like(source)
        stats = refresh(left_stat, right_stat, received, base, source, filled, stats)
    rest = [grad_blocks[m] for m in range(early, per)]
    entry = jnp.where(is_heavy, early, own_entry) - early
    slabs = grams(rest, jnp.clip(entry, 0, per - 1 - early))
    received = lax.all_to_all(slabs, GROUP, split_axis=0, concat_axis=0, tiled=True)
    base = jnp.where(is_heavy, early, 0) * group
    ranks = base + jnp.arange(capacity - early * group, dtype=jnp.int32)
    source = (first + ranks) % group
    filled = (ranks < held).astype(jnp.int32)
    stats = refresh(left_stat, right_stat, received, base, source, filled, stats)
    left_new, right_new = stats

    pieces = [
        precondition(left_dealt, m, grad_blocks[m], right_blocks[m]) for m in range(per)
    ]
    precond = jnp.stack([piece for piece, _ in pieces])
    precond_total = jnp.stack([total for _, total in pieces])

    matrix_range = jnp.arange(MATS, dtype=jnp.int32)
    onehot = (block_matrix[:, None] == matrix_range[None, :]).astype(jnp.float32)
    own_order = lax.dynamic_slice_in_dim(order, group_index * per, per)
    own_onehot = jnp.sum(
        jnp.where((own_order[:, None] == ids[None, :])[:, :, None], onehot[None, :, :], 0.0), axis=1
    )
    adam_part = jnp.sum(jnp.sum(adam_total, axis=(1, 2))[:, None] * onehot, axis=0)
    shampoo_part = jnp.sum(jnp.sum(precond_total, axis=(1, 2))[:, None] * own_onehot, axis=0)
    adam_norm, shampoo_norm = lax.psum((adam_part, shampoo_part), ALL)
    counts = jnp.sum(onehot, axis=0) * float(size * size)
    graft_scale = jnp.sqrt(adam_norm / (shampoo_norm + FLOOR_RATE * counts))
    block_scale = jnp.sum(own_onehot * graft_scale[None, :], axis=1)

    updated = update(weights_dealt, precond, block_scale)
    gathered = lax.all_gather(updated, GROUP, axis=0, tiled=True)
    new_weights = reorder(gathered, place)

    factor_m_new, factor_v_new, factor_step = adam_direction(
        factor_grad.astype(jnp.float32), factor_m, factor_v
    )
    factors_new = factors - LEARNING * (factor_step + DECAY_RATE * factors)
    return (
        new_weights,
        adam_m_new,
        adam_v_new,
        left_new,
        right_new,
        factors_new,
        factor_m_new,
        factor_v_new,
    )


def solution(mesh):
    tile = P(None, "shard", GROUP)
    stat = P("shard", None, GROUP)
    factor = P("shard", GROUP)
    in_specs = (P(GROUP, None, "shard", None), tile, tile, tile, stat, stat, tile, tile, P(), P())
    out_specs = (P(None, "shard", None), tile, tile, stat, stat)
    return jax.shard_map(
        shards,
        mesh=mesh,
        in_specs=in_specs + (factor,) * 4,
        out_specs=out_specs + (factor,) * 3,
        check_vma=False,
    )
```

```python
import functools

import jax
import jax.numpy as jnp
from jax import lax
from jax.experimental import pallas as pl
from jax.experimental.pallas import tpu as pltpu
from jax.sharding import PartitionSpec as P

MATS = 5

BETA_ONE = 0.9
BETA_TWO = 0.95
BETA_STAT = 0.95
LEARNING = 0.1
DECAY_RATE = 0.1
EPSILON = 1e-08
FLOOR_RATE = 1e-06
CORRECT_ONE = 1.0 - 0.9**10
CORRECT_TWO = 1.0 - 0.95**10

GROUP = ("tensor", "section")
ALL = ("shard", "tensor", "section")
VMEM_LIMIT = 48 * 1024 * 1024
LANES = 128


def params():
    return pltpu.CompilerParams(vmem_limit_bytes=VMEM_LIMIT)


def adam_direction(grad_float, moment, second):
    moment_new = BETA_ONE * moment + (1.0 - BETA_ONE) * grad_float
    second_new = BETA_TWO * second + (1.0 - BETA_TWO) * grad_float * grad_float
    direction = moment_new / CORRECT_ONE / (jnp.sqrt(second_new / CORRECT_TWO) + EPSILON)
    return (moment_new, second_new, direction)


def reorder_kernel(order, blocks, out, done):
    copies = [
        pltpu.make_async_copy(blocks.at[order[i]], out.at[i], done.at[i])
        for i in range(out.shape[0])
    ]
    for copy in copies:
        copy.start()
    for copy in copies:
        copy.wait()


def reorder(blocks, order):
    count = order.shape[0]
    out = jax.ShapeDtypeStruct((count,) + blocks.shape[1:], blocks.dtype)
    return pl.pallas_call(
        reorder_kernel,
        grid_spec=pltpu.PrefetchScalarGridSpec(
            num_scalar_prefetch=1,
            grid=(1,),
            in_specs=[pl.BlockSpec(memory_space=pl.ANY)],
            out_specs=pl.BlockSpec(memory_space=pl.ANY),
            scratch_shapes=[pltpu.SemaphoreType.DMA((count,))],
        ),
        out_shape=out,
        compiler_params=params(),
        cost_estimate=pl.CostEstimate(
            flops=0, bytes_accessed=2 * out.size * out.dtype.itemsize, transcendentals=0
        ),
    )(order, blocks)


def place_kernel(sources, target, *refs):
    done, out = refs[-1], refs[-2]
    copies = []
    for ref in refs[:sources]:
        for i in range(ref.shape[0]):
            place = target[len(copies)]
            copies.append(
                pltpu.make_async_copy(ref.at[i], out.at[place], done.at[len(copies)])
            )
    for copy in copies:
        copy.start()
    for copy in copies:
        copy.wait()


def place_blocks(arrays, target, total, earlier):
    tile, kind = arrays[0].shape[1:], arrays[0].dtype
    count = target.shape[0]
    inputs = list(arrays) + list(earlier)
    return pl.pallas_call(
        functools.partial(place_kernel, len(arrays)),
        grid_spec=pltpu.PrefetchScalarGridSpec(
            num_scalar_prefetch=1,
            grid=(1,),
            in_specs=[pl.BlockSpec(memory_space=pl.ANY)] * len(inputs),
            out_specs=pl.BlockSpec(memory_space=pl.ANY),
            scratch_shapes=[pltpu.SemaphoreType.DMA((count,))],
        ),
        out_shape=jax.ShapeDtypeStruct((total,) + tile, kind),
        input_output_aliases={1 + len(arrays) + i: i for i in range(len(earlier))},
        compiler_params=params(),
        cost_estimate=pl.CostEstimate(
            flops=0, bytes_accessed=4 * count * tile[0] * tile[1], transcendentals=0
        ),
    )(target, *inputs)


def adam_kernel(place, grad, moment, second, moment_out, second_out, total):
    moment_new, second_new, direction = adam_direction(
        grad[0].astype(jnp.float32), moment[0], second[0]
    )
    moment_out[0] = moment_new
    second_out[0] = second_new
    total[0] = jnp.sum(direction * direction, axis=0, keepdims=True)


def adam(grad_tiles, place, moment, second):
    count, rows, cols = moment.shape
    own = pl.BlockSpec((1, rows, cols), lambda i, place: (i, 0, 0))
    return pl.pallas_call(
        adam_kernel,
        grid_spec=pltpu.PrefetchScalarGridSpec(
            num_scalar_prefetch=1,
            grid=(count,),
            in_specs=[
                pl.BlockSpec((1, rows, cols), lambda i, place: (place[i], 0, 0)),
                own,
                own,
            ],
            out_specs=[own, own, pl.BlockSpec((1, 1, cols), lambda i, place: (i, 0, 0))],
        ),
        out_shape=[
            jax.ShapeDtypeStruct(moment.shape, jnp.float32),
            jax.ShapeDtypeStruct(moment.shape, jnp.float32),
            jax.ShapeDtypeStruct((count, 1, cols), jnp.float32),
        ],
        compiler_params=params(),
        cost_estimate=pl.CostEstimate(
            flops=20 * moment.size, bytes_accessed=18 * moment.size, transcendentals=moment.size
        ),
    )(place, grad_tiles, moment, second)


def gram_kernel(chosen, grad, out):
    parts, _, rows, width = grad.shape
    size = parts * rows
    whole = grad[:, 0].reshape(size, width)
    turned = whole.T
    step = 2 * LANES
    for start in range(0, size, step):
        left = lax.dot_general(
            whole,
            whole[start : start + step, :],
            (((1,), (1,)), ((), ())),
            preferred_element_type=jnp.float32,
        ).astype(jnp.bfloat16)
        right = lax.dot_general(
            turned,
            whole[:, start : start + step],
            (((1,), (0,)), ((), ())),
            preferred_element_type=jnp.float32,
        ).astype(jnp.bfloat16)
        for half in range(2):
            slab = start // LANES + half
            out[slab, 0, 0] = left[:, half * LANES : (half + 1) * LANES]
            out[slab, 0, 1] = right[:, half * LANES : (half + 1) * LANES]


def grams(grad_blocks, chosen):
    shards, per, rows, width = grad_blocks.shape
    size = shards * rows
    slabs = size // LANES
    count = chosen.shape[0]
    return pl.pallas_call(
        gram_kernel,
        grid_spec=pltpu.PrefetchScalarGridSpec(
            num_scalar_prefetch=1,
            grid=(count,),
            in_specs=[
                pl.BlockSpec((shards, 1, rows, width), lambda j, chosen: (0, chosen[j], 0, 0))
            ],
            out_specs=pl.BlockSpec(
                (slabs, 1, 2, size, LANES), lambda j, chosen: (0, j, 0, 0, 0)
            ),
        ),
        out_shape=jax.ShapeDtypeStruct((slabs, count, 2, size, LANES), jnp.bfloat16),
        compiler_params=params(),
        cost_estimate=pl.CostEstimate(
            flops=count * 4 * size**3, bytes_accessed=count * 6 * size * size, transcendentals=0
        ),
    )(chosen, grad_blocks)


def stat_kernel(
    base, source, entry, filled, left_stat, right_stat, left_gram, right_gram, *refs
):
    left_out, right_out = refs[-2:]
    full = filled[pl.program_id(0)] > 0
    left = left_gram[0, 0, 0].astype(jnp.float32)
    right = right_gram[0, 0, 0].astype(jnp.float32)
    left_out[0] = BETA_STAT * left_stat[0] + jnp.where(full, (1.0 - BETA_STAT) * left, 0.0)
    right_out[0] = BETA_STAT * right_stat[0] + jnp.where(full, (1.0 - BETA_STAT) * right, 0.0)


def refresh(left_stat, right_stat, received, base, source, entry, filled, earlier):
    slots, size, cols = left_stat.shape
    count = source.shape[0]
    own = pl.BlockSpec((1, size, cols), lambda r, base, source, entry, filled: (base[0] + r, 0, 0))
    gram = (1, 1, 1, size, cols)
    shape = jax.ShapeDtypeStruct(left_stat.shape, jnp.float32)
    return pl.pallas_call(
        stat_kernel,
        grid_spec=pltpu.PrefetchScalarGridSpec(
            num_scalar_prefetch=4,
            grid=(count,),
            in_specs=[
                own,
                own,
                pl.BlockSpec(
                    gram, lambda r, base, source, entry, filled: (source[r], entry[r], 0, 0, 0)
                ),
                pl.BlockSpec(
                    gram, lambda r, base, source, entry, filled: (source[r], entry[r], 1, 0, 0)
                ),
            ]
            + [pl.BlockSpec(memory_space=pl.ANY)] * len(earlier),
            out_specs=[own, own],
        ),
        out_shape=[shape, shape],
        input_output_aliases={8 + i: i for i in range(len(earlier))},
        compiler_params=params(),
        cost_estimate=pl.CostEstimate(
            flops=6 * count * size * cols, bytes_accessed=20 * count * size * cols, transcendentals=0
        ),
    )(
        base.reshape(1), source, entry, filled, left_stat, right_stat, received, received, *earlier
    )


def left_product(left, grad):
    slabs, _, rows, _ = left.shape
    left_rows = jnp.concatenate([left[s, 0] for s in range(slabs)], axis=1)
    whole = grad[:, 0].reshape(grad.shape[0] * rows, grad.shape[3])
    return jnp.dot(left_rows, whole, preferred_element_type=jnp.float32).astype(jnp.bfloat16)


def precond_kernel(left, grad, right, out, total):
    slabs, _, rows, cols = left.shape
    parts = grad.shape[0]
    mixed = left_product(left, grad)
    total[...] = jnp.zeros_like(total)
    step = 2
    for start in range(0, slabs, step):
        columns = jnp.concatenate(
            [right[:, s, 0].reshape(parts * rows, cols) for s in range(start, start + step)], axis=1
        )
        piece = jnp.dot(mixed, columns, preferred_element_type=jnp.float32)
        out[0, :, start * cols : (start + step) * cols] = piece.astype(jnp.bfloat16)
        square = jnp.sum(piece * piece, axis=0, keepdims=True)
        total[0] += square[:, :cols] + square[:, cols:]


def tile_sources(mine, count, spread):
    found = {(mine, b): (0, spread * b) for b in range(count)}
    for hop in range(1, count):
        for i in range(count - hop):
            if mine + hop < count:
                found[mine + hop, (mine + hop + i) % count] = (hop, spread * i)
            if mine - hop >= 0:
                found[mine - hop, (mine - hop - i) % count] = (count - 1 + hop, spread * i)
    return found


def precond_tiles_kernel(me, left, grad, *refs):
    rights, out, total = refs[:-2], refs[-2], refs[-1]
    slabs, _, rows, cols = left.shape
    parts = grad.shape[0]
    spread = slabs // parts
    mixed = left_product(left, grad)
    total[...] = jnp.zeros_like(total)
    for mine in range(parts):

        @pl.when(me[0] == mine)
        def _(mine=mine):
            found = tile_sources(mine, parts, spread)
            for b in range(parts):
                piece = jnp.zeros((rows, spread * cols), jnp.float32)
                for a in range(parts):
                    turned = (a, b) not in found
                    array, first = found[(b, a) if turned else (a, b)]
                    tile = jnp.concatenate(
                        [rights[array][first + s, 0] for s in range(spread)], axis=1
                    )
                    piece += lax.dot_general(
                        mixed[:, a * rows : (a + 1) * rows],
                        tile,
                        (((1,), (1 if turned else 0,)), ((), ())),
                        preferred_element_type=jnp.float32,
                    )
                out[0, :, b * rows : (b + 1) * rows] = piece.astype(jnp.bfloat16)
                square = jnp.sum(piece * piece, axis=0, keepdims=True)
                total[0] += sum(square[:, s * cols : (s + 1) * cols] for s in range(spread))


def gather_roots(right):
    slabs, per, rows, cols = right.shape
    count, me = lax.axis_size("shard"), lax.axis_index("shard")
    if count != 4 or slabs % count or rows * count != slabs * cols:
        return [lax.all_gather(right, "shard", axis=0)]
    spread = slabs // count
    down = [(a, a - 1) for a in range(1, count)]
    up = [(a, a + 1) for a in range(count - 1)]
    lane = jnp.arange(spread * (count - 1), dtype=jnp.int32)
    parts = [right]
    for pairs, sign in ((down, 1), (up, -1)):
        tiles = (me + sign * (lane // spread)) % count
        moving = reorder(
            right.reshape(slabs, per * rows, cols), tiles * spread + lane % spread
        ).reshape(lane.shape[0], per, rows, cols)
        for hop in range(1, count):
            moving = lax.ppermute(moving, "shard", pairs)
            parts.append(moving)
            moving = moving[: spread * (count - 1 - hop)]
    return parts


def precondition(left, start, grad_blocks, rights):
    shards, count, rows, width = grad_blocks.shape
    slabs, _, _, cols = left.shape
    size = shards * rows
    whole = len(rights) == 1
    if whole:
        right_specs = [pl.BlockSpec((shards, slabs, 1, rows, cols), lambda m, me: (0, 0, start + m, 0, 0))]
    else:
        right_specs = [
            pl.BlockSpec((right.shape[0], 1, rows, cols), lambda m, me: (0, start + m, 0, 0))
            for right in rights
        ]
    body = precond_tiles_kernel
    if whole:
        body = lambda me, *refs: precond_kernel(*refs)
    return pl.pallas_call(
        body,
        grid_spec=pltpu.PrefetchScalarGridSpec(
            num_scalar_prefetch=1,
            grid=(count,),
            in_specs=[
                pl.BlockSpec((slabs, 1, rows, cols), lambda m, me: (0, start + m, 0, 0)),
                pl.BlockSpec((shards, 1, rows, width), lambda m, me: (0, m, 0, 0)),
            ]
            + right_specs,
            out_specs=[
                pl.BlockSpec((1, rows, width), lambda m, me: (m, 0, 0)),
                pl.BlockSpec((1, 1, cols), lambda m, me: (m, 0, 0)),
            ],
        ),
        out_shape=[
            jax.ShapeDtypeStruct((count, rows, width), jnp.bfloat16),
            jax.ShapeDtypeStruct((count, 1, cols), jnp.float32),
        ],
        compiler_params=params(),
        cost_estimate=pl.CostEstimate(
            flops=count * 4 * rows * size * size,
            bytes_accessed=count * (4 * size * size + 4 * rows * size),
            transcendentals=0,
        ),
    )(lax.axis_index("shard").reshape(1), left, grad_blocks, *rights)


def update_kernel(scale, weights, precond, out):
    slabs = weights.shape[0]
    factor = scale[pl.program_id(0)]
    old = jnp.concatenate([weights[s, 0] for s in range(slabs)], axis=1).astype(jnp.float32)
    step = factor * precond[0].astype(jnp.float32) + DECAY_RATE * old
    out[0] = (old - LEARNING * step).astype(jnp.bfloat16)


def update(weights, start, precond, scale):
    slabs, _, rows, cols = weights.shape
    count = precond.shape[0]
    width = slabs * cols
    own = pl.BlockSpec((1, rows, width), lambda m, scale: (m, 0, 0))
    return pl.pallas_call(
        update_kernel,
        grid_spec=pltpu.PrefetchScalarGridSpec(
            num_scalar_prefetch=1,
            grid=(count,),
            in_specs=[
                pl.BlockSpec((slabs, 1, rows, cols), lambda m, scale: (0, start + m, 0, 0)),
                own,
            ],
            out_specs=own,
        ),
        out_shape=jax.ShapeDtypeStruct((count, rows, width), jnp.bfloat16),
        compiler_params=params(),
        cost_estimate=pl.CostEstimate(
            flops=5 * precond.size, bytes_accessed=6 * precond.size, transcendentals=0
        ),
    )(scale, weights, precond)


def pair_kernel(picked, first, second, third, fourth, received, send_a, keep_a, send_b, keep_b):
    half = first.shape[1] // 2
    added = [
        (own[0].astype(jnp.float32) + received[u].astype(jnp.float32)).astype(jnp.bfloat16)
        for u, own in enumerate((first, second, third, fourth))
    ]
    for ref, chosen, start in (
        (send_a, (1, 3), 0),
        (keep_a, (0, 2), 0),
        (send_b, (2, 3), half),
        (keep_b, (0, 1), half),
    ):
        for i, u in enumerate(chosen):
            ref[i, 0] = added[u][start : start + half]


def add_pair(partials, received, picked):
    _, rows, width = partials.shape
    count = received.shape[0] // 4
    half = jax.ShapeDtypeStruct((2, count, rows // 2, width), partials.dtype)

    def own(u):
        return pl.BlockSpec((1, rows, width), lambda i, picked: (picked[4 * i + u], 0, 0))

    return pl.pallas_call(
        pair_kernel,
        grid_spec=pltpu.PrefetchScalarGridSpec(
            num_scalar_prefetch=1,
            grid=(count,),
            in_specs=[own(0), own(1), own(2), own(3)]
            + [pl.BlockSpec((4, rows, width), lambda i, picked: (i, 0, 0))],
            out_specs=[pl.BlockSpec((2, 1, rows // 2, width), lambda i, picked: (0, i, 0, 0))] * 4,
        ),
        out_shape=[half] * 4,
        compiler_params=params(),
        cost_estimate=pl.CostEstimate(
            flops=4 * count * rows * width,
            bytes_accessed=24 * count * rows * width,
            transcendentals=0,
        ),
    )(picked, partials, partials, partials, partials, received)


def add(one, two):
    return (one.astype(jnp.float32) + two.astype(jnp.float32)).astype(jnp.bfloat16)


def swap(array, bit):
    devices = lax.axis_size("tensor")
    return lax.ppermute(array, "tensor", [(t, t ^ bit) for t in range(devices)])


def swap_core(array):
    return lax.ppermute(array, "section", [(0, 1), (1, 0)])


def by_bits():
    return (lax.axis_size("tensor"), lax.axis_size("section")) == (4, 2)


def sum_blocks(partials, picked):
    count = picked.shape[1]
    if not by_bits():
        ordered = reorder(partials, picked.reshape(-1))
        return lax.psum_scatter(ordered, GROUP, scatter_dimension=0, tiled=True)
    core = lax.axis_index("section")
    relative = jnp.arange(4, dtype=jnp.int32) ^ lax.axis_index("tensor")
    mine = jnp.take(picked, relative * 2 + core, axis=0).T.reshape(-1)
    other = jnp.take(picked, relative * 2 + 1 - core, axis=0).T.reshape(-1)
    received = swap_core(reorder(partials, other))
    send_a, keep_a, send_b, keep_b = add_pair(partials, received, mine)
    sum_a = add(keep_a, swap(send_a, 1))
    sum_b = add(keep_b, swap(send_b, 2))
    last_a = add(sum_a[0], swap(sum_a[1], 2))
    last_b = add(sum_b[0], swap(sum_b[1], 1))
    return jnp.concatenate([last_a, last_b], axis=1)


def gather_blocks(first, second, by_entry):
    total = by_entry.size
    if not by_bits():
        mine = jnp.concatenate([first, second], axis=0)
        gathered = lax.all_gather(mine, GROUP, axis=0, tiled=True)
        return place_blocks([gathered], by_entry.reshape(-1), total, [])
    cut = first.shape[0]
    tensor, core = lax.axis_index("tensor"), lax.axis_index("section")
    x_first, y_second = swap(first, 1), swap(second, 2)
    y_first, x_second = swap(first, 2), swap(second, 1)
    d_first, d_second = swap(x_first, 2), swap(y_second, 1)

    def targets(bits, core):
        places = [by_entry[(tensor ^ bit) * 2 + core] for bit in bits]
        return [piece for place in places for piece in (place[:cut], place[cut:])]

    near = [first, second, x_first, x_second, y_first, y_second]
    near_target = targets((0, 1, 2), core) + targets((0, 1, 2), 1 - core)
    near = near + [swap_core(piece) for piece in near]
    far = [d_first, d_second]
    far_target = targets((3,), core) + targets((3,), 1 - core)
    far = far + [swap_core(piece) for piece in far]
    placed = place_blocks(near, jnp.concatenate(near_target), total, [])
    return place_blocks(far, jnp.concatenate(far_target), total, [placed])


def shards(
    grad_parts,
    weights,
    adam_m,
    adam_v,
    left_stat,
    right_stat,
    left_root,
    right_root,
    block_owner,
    block_matrix,
    factors,
    factor_grad,
    factor_m,
    factor_v,
):
    capacity = left_stat.shape[0]
    blocks, rows, cols = weights.shape
    size = left_stat.shape[1]
    group = size // cols
    per = blocks // group
    sends = -(-capacity // group)
    owner_index = lax.axis_index("shard")
    group_index = lax.axis_index(GROUP)
    owner_count = lax.axis_size("shard")

    ids = jnp.arange(blocks, dtype=jnp.int32)
    owners = jnp.arange(owner_count, dtype=jnp.int32)
    loads = jnp.sum((block_owner[None, :] == owners[:, None]).astype(jnp.int32), axis=1)
    heavy = jnp.min(jnp.where(loads == jnp.max(loads), owners, owner_count))
    turn = (block_owner - heavy) % owner_count
    own_turn = (owner_index - heavy) % owner_count
    before = (turn[None, :] < turn[:, None]) | (
        (turn[None, :] == turn[:, None]) & (ids[None, :] < ids[:, None])
    )
    position = jnp.sum(before.astype(jnp.int32), axis=1)
    place = (position % group) * per + position // group
    order = jnp.sum(jnp.where(place[None, :] == ids[:, None], ids[None, :], 0), axis=1)

    first = jnp.sum((turn < own_turn).astype(jnp.int32))
    held = jnp.sum((turn == own_turn).astype(jnp.int32))
    early = sends - 1 if blocks - capacity <= group else 0
    is_heavy = own_turn == 0
    own_entry = (first - group_index + group - 1) // group

    def deal(tiles):
        sent = reorder(tiles, order).reshape(group, per, rows, cols)
        return lax.all_to_all(sent, GROUP, split_axis=0, concat_axis=0, tiled=True)

    by_entry = order.reshape(group, per)
    right_dealt = deal(right_root)
    cuts = [(0, early), (early, per)] if early else [(0, per)]
    gradient = [sum_blocks(grad_parts[0], by_entry[:, a:b]) for a, b in cuts]
    grad_blocks = [lax.all_gather(part, "shard", axis=0) for part in gradient]
    rights = gather_roots(right_dealt)
    left_dealt = deal(left_root)
    weights_dealt = deal(weights)

    tiles = jnp.concatenate(gradient, axis=0).reshape(per, rows, group, cols)
    tiles = jnp.transpose(tiles, (2, 0, 1, 3))
    tiles = lax.all_to_all(tiles, GROUP, split_axis=0, concat_axis=0, tiled=True)
    adam_m_new, adam_v_new, adam_total = adam(
        tiles.reshape(blocks, rows, cols), place, adam_m, adam_v
    )

    if early:
        slabs = grams(grad_blocks[0], jnp.arange(early, dtype=jnp.int32))
        slabs, left_dealt = lax.optimization_barrier((slabs, left_dealt))
        received = lax.all_to_all(slabs, GROUP, split_axis=0, concat_axis=0, tiled=True)
    entry = jnp.where(is_heavy, early, own_entry) - early
    last_slabs = grams(grad_blocks[-1], jnp.clip(entry, 0, per - 1 - early).reshape(1))
    pieces = [
        precondition(left_dealt, a, part, rights) for (a, _), part in zip(cuts, grad_blocks)
    ]
    precond_total = jnp.concatenate([total for _, total in pieces], axis=0)

    matrix_range = jnp.arange(MATS, dtype=jnp.int32)
    onehot = (block_matrix[:, None] == matrix_range[None, :]).astype(jnp.float32)
    own_order = lax.dynamic_slice_in_dim(order, group_index * per, per)
    own_onehot = jnp.sum(
        jnp.where((own_order[:, None] == ids[None, :])[:, :, None], onehot[None, :, :], 0.0), axis=1
    )
    adam_part = jnp.sum(jnp.sum(adam_total, axis=(1, 2))[:, None] * onehot, axis=0)
    shampoo_part = jnp.sum(jnp.sum(precond_total, axis=(1, 2))[:, None] * own_onehot, axis=0)
    parts = jnp.pad(jnp.stack([adam_part, shampoo_part]), ((0, 6), (0, LANES - MATS)))
    if early:
        received, last_slabs, parts = lax.optimization_barrier((received, last_slabs, parts))
    devices = owner_count * group
    parts = lax.all_to_all(
        jnp.broadcast_to(parts[None], (devices,) + parts.shape), ALL, 0, 0, tiled=True
    )
    adam_norm, shampoo_norm = jnp.sum(parts, axis=0)[:2, :MATS]
    counts = jnp.sum(onehot, axis=0) * float(size * size)
    graft_scale = jnp.sqrt(adam_norm / (shampoo_norm + FLOOR_RATE * counts))
    block_scale = jnp.sum(own_onehot * graft_scale[None, :], axis=1)

    last = lax.all_to_all(last_slabs, GROUP, split_axis=0, concat_axis=0, tiled=True)
    stats = ()
    if early:
        ranks = jnp.arange(early * group, dtype=jnp.int32)
        base = jnp.where(is_heavy, 0, capacity - early * group)
        filled = jnp.where(is_heavy, 1, 0) * jnp.ones_like(ranks)
        stats = refresh(
            left_stat, right_stat, received, base, ranks % group, ranks // group, filled, stats
        )
    base = jnp.where(is_heavy, early * group, 0)
    ranks = base + jnp.arange(capacity - early * group, dtype=jnp.int32)
    filled = (ranks < held).astype(jnp.int32)
    source = (first + ranks) % group
    stats = refresh(
        left_stat, right_stat, last, base, source, jnp.zeros_like(ranks), filled, stats
    )
    left_new, right_new = stats

    updated = [
        update(weights_dealt, a, piece, block_scale[a:b])
        for (a, b), (piece, _) in zip(cuts, pieces)
    ]
    if len(updated) == 1:
        updated = [updated[0][: per // 2], updated[0][per // 2 :]]
    new_weights = gather_blocks(updated[0], updated[1], by_entry)

    factor_m_new, factor_v_new, factor_step = adam_direction(
        factor_grad.astype(jnp.float32), factor_m, factor_v
    )
    factors_new = factors - LEARNING * (factor_step + DECAY_RATE * factors)
    return (
        new_weights,
        adam_m_new,
        adam_v_new,
        left_new,
        right_new,
        factors_new,
        factor_m_new,
        factor_v_new,
    )


def solution(mesh):
    tile = P(None, "shard", GROUP)
    stat = P("shard", None, GROUP)
    factor = P("shard", GROUP)
    in_specs = (P(GROUP, None, "shard", None), tile, tile, tile, stat, stat, tile, tile, P(), P())
    out_specs = (P(None, "shard", None), tile, tile, stat, stat)
    return jax.shard_map(
        shards,
        mesh=mesh,
        in_specs=in_specs + (factor,) * 4,
        out_specs=out_specs + (factor,) * 3,
        check_vma=False,
    )
```

```python
import functools

import jax
import jax.numpy as jnp
from jax import lax
from jax.experimental import pallas as pl
from jax.experimental.pallas import tpu as pltpu
from jax.sharding import PartitionSpec as P

MATS = 5

BETA_ONE = 0.9
BETA_TWO = 0.95
BETA_STAT = 0.95
LEARNING = 0.1
DECAY_RATE = 0.1
EPSILON = 1e-08
FLOOR_RATE = 1e-06
CORRECT_ONE = 1.0 - 0.9**10
CORRECT_TWO = 1.0 - 0.95**10

GROUP = ("tensor", "section")
ALL = ("shard", "tensor", "section")
VMEM_LIMIT = 48 * 1024 * 1024
LANES = 128
SMALL = pl.CostEstimate(flops=0, bytes_accessed=0, transcendentals=0)


def params():
    return pltpu.CompilerParams(vmem_limit_bytes=VMEM_LIMIT)


def adam_direction(grad_float, moment, second):
    moment_new = BETA_ONE * moment + (1.0 - BETA_ONE) * grad_float
    second_new = BETA_TWO * second + (1.0 - BETA_TWO) * grad_float * grad_float
    direction = moment_new / CORRECT_ONE / (jnp.sqrt(second_new / CORRECT_TWO) + EPSILON)
    return (moment_new, second_new, direction)


def copy_blocks(pairs, held, arrived, left):
    into = [
        pltpu.make_async_copy(source, held.at[i], arrived.at[i])
        for i, (source, _) in enumerate(pairs)
    ]
    out_of = [
        pltpu.make_async_copy(held.at[i], target, left.at[i]) for i, (_, target) in enumerate(pairs)
    ]
    for copy in into:
        copy.start()
    for arrival, copy in zip(into, out_of):
        arrival.wait()
        copy.start()
    for copy in out_of:
        copy.wait()


def copy_scratch(count, tile, kind):
    return [
        pltpu.VMEM((count,) + tile, kind),
        pltpu.SemaphoreType.DMA((count,)),
        pltpu.SemaphoreType.DMA((count,)),
    ]


def reorder_kernel(order, blocks, out, held, arrived, left):
    pairs = [(blocks.at[order[i]], out.at[i]) for i in range(out.shape[0])]
    copy_blocks(pairs, held, arrived, left)


def reorder(blocks, order):
    count, tile = order.shape[0], blocks.shape[1:]
    return pl.pallas_call(
        reorder_kernel,
        grid_spec=pltpu.PrefetchScalarGridSpec(
            num_scalar_prefetch=1,
            grid=(1,),
            in_specs=[pl.BlockSpec(memory_space=pl.ANY)],
            out_specs=pl.BlockSpec(memory_space=pl.ANY),
            scratch_shapes=copy_scratch(count, tile, blocks.dtype),
        ),
        out_shape=jax.ShapeDtypeStruct((count,) + tile, blocks.dtype),
        compiler_params=params(),
        cost_estimate=SMALL,
    )(order, blocks)


def place_kernel(sources, target, *refs):
    out, held, arrived, left = refs[-4:]
    blocks = [ref.at[i] for ref in refs[:sources] for i in range(ref.shape[0])]
    pairs = [(block, out.at[target[i]]) for i, block in enumerate(blocks)]
    copy_blocks(pairs, held, arrived, left)


def place_blocks(arrays, target, total, earlier):
    tile, kind = arrays[0].shape[1:], arrays[0].dtype
    inputs = list(arrays) + list(earlier)
    return pl.pallas_call(
        functools.partial(place_kernel, len(arrays)),
        grid_spec=pltpu.PrefetchScalarGridSpec(
            num_scalar_prefetch=1,
            grid=(1,),
            in_specs=[pl.BlockSpec(memory_space=pl.ANY)] * len(inputs),
            out_specs=pl.BlockSpec(memory_space=pl.ANY),
            scratch_shapes=copy_scratch(target.shape[0], tile, kind),
        ),
        out_shape=jax.ShapeDtypeStruct((total,) + tile, kind),
        input_output_aliases={1 + len(arrays) + i: i for i in range(len(earlier))},
        compiler_params=params(),
        cost_estimate=SMALL,
    )(target, *inputs)


def adam_kernel(place, grad, moment, second, moment_out, second_out, total):
    moment_new, second_new, direction = adam_direction(
        grad[0].astype(jnp.float32), moment[0], second[0]
    )
    moment_out[0] = moment_new
    second_out[0] = second_new
    total[0] = jnp.sum(direction * direction, axis=0, keepdims=True)


def adam(grad_tiles, place, moment, second):
    count, rows, cols = moment.shape
    own = pl.BlockSpec((1, rows, cols), lambda i, place: (i, 0, 0))
    return pl.pallas_call(
        adam_kernel,
        grid_spec=pltpu.PrefetchScalarGridSpec(
            num_scalar_prefetch=1,
            grid=(count,),
            in_specs=[
                pl.BlockSpec((1, rows, cols), lambda i, place: (place[i], 0, 0)),
                own,
                own,
            ],
            out_specs=[own, own, pl.BlockSpec((1, 1, cols), lambda i, place: (i, 0, 0))],
        ),
        out_shape=[
            jax.ShapeDtypeStruct(moment.shape, jnp.float32),
            jax.ShapeDtypeStruct(moment.shape, jnp.float32),
            jax.ShapeDtypeStruct((count, 1, cols), jnp.float32),
        ],
        compiler_params=params(),
        cost_estimate=SMALL,
    )(place, grad_tiles, moment, second)


def gram_kernel(chosen, grad, out):
    parts, _, rows, width = grad.shape
    size = parts * rows
    whole = grad[:, 0].reshape(size, width)
    turned = whole.T
    step = 2 * LANES
    for start in range(0, size, step):
        left = lax.dot_general(
            whole,
            whole[start : start + step, :],
            (((1,), (1,)), ((), ())),
            preferred_element_type=jnp.float32,
        ).astype(jnp.bfloat16)
        right = lax.dot_general(
            turned,
            whole[:, start : start + step],
            (((1,), (0,)), ((), ())),
            preferred_element_type=jnp.float32,
        ).astype(jnp.bfloat16)
        for half in range(2):
            slab = start // LANES + half
            out[slab, 0, 0] = left[:, half * LANES : (half + 1) * LANES]
            out[slab, 0, 1] = right[:, half * LANES : (half + 1) * LANES]


def grams(grad_blocks, chosen):
    shards, per, rows, width = grad_blocks.shape
    size = shards * rows
    slabs = size // LANES
    count = chosen.shape[0]
    return pl.pallas_call(
        gram_kernel,
        grid_spec=pltpu.PrefetchScalarGridSpec(
            num_scalar_prefetch=1,
            grid=(count,),
            in_specs=[
                pl.BlockSpec((shards, 1, rows, width), lambda j, chosen: (0, chosen[j], 0, 0))
            ],
            out_specs=pl.BlockSpec(
                (slabs, 1, 2, size, LANES), lambda j, chosen: (0, j, 0, 0, 0)
            ),
        ),
        out_shape=jax.ShapeDtypeStruct((slabs, count, 2, size, LANES), jnp.bfloat16),
        compiler_params=params(),
        cost_estimate=SMALL,
    )(chosen, grad_blocks)


def stat_kernel(
    base, source, entry, filled, left_stat, right_stat, left_gram, right_gram, *refs
):
    left_out, right_out = refs[-2:]
    full = filled[pl.program_id(0)] > 0
    left = left_gram[0, 0, 0].astype(jnp.float32)
    right = right_gram[0, 0, 0].astype(jnp.float32)
    left_out[0] = BETA_STAT * left_stat[0] + jnp.where(full, (1.0 - BETA_STAT) * left, 0.0)
    right_out[0] = BETA_STAT * right_stat[0] + jnp.where(full, (1.0 - BETA_STAT) * right, 0.0)


def refresh(left_stat, right_stat, received, base, source, entry, filled, earlier):
    slots, size, cols = left_stat.shape
    count = source.shape[0]
    own = pl.BlockSpec((1, size, cols), lambda r, base, source, entry, filled: (base[0] + r, 0, 0))
    gram = (1, 1, 1, size, cols)
    shape = jax.ShapeDtypeStruct(left_stat.shape, jnp.float32)
    return pl.pallas_call(
        stat_kernel,
        grid_spec=pltpu.PrefetchScalarGridSpec(
            num_scalar_prefetch=4,
            grid=(count,),
            in_specs=[
                own,
                own,
                pl.BlockSpec(
                    gram, lambda r, base, source, entry, filled: (source[r], entry[r], 0, 0, 0)
                ),
                pl.BlockSpec(
                    gram, lambda r, base, source, entry, filled: (source[r], entry[r], 1, 0, 0)
                ),
            ]
            + [pl.BlockSpec(memory_space=pl.ANY)] * len(earlier),
            out_specs=[own, own],
        ),
        out_shape=[shape, shape],
        input_output_aliases={8 + i: i for i in range(len(earlier))},
        compiler_params=params(),
        cost_estimate=SMALL,
    )(
        base.reshape(1), source, entry, filled, left_stat, right_stat, received, received, *earlier
    )


def left_product(left, grad):
    slabs, _, rows, _ = left.shape
    left_rows = jnp.concatenate([left[s, 0] for s in range(slabs)], axis=1)
    whole = grad[:, 0].reshape(grad.shape[0] * rows, grad.shape[3])
    return jnp.dot(left_rows, whole, preferred_element_type=jnp.float32).astype(jnp.bfloat16)


def precond_kernel(left, grad, right, out, total):
    slabs, _, rows, cols = left.shape
    parts = grad.shape[0]
    mixed = left_product(left, grad)
    total[...] = jnp.zeros_like(total)
    step = 2
    for start in range(0, slabs, step):
        columns = jnp.concatenate(
            [right[:, s, 0].reshape(parts * rows, cols) for s in range(start, start + step)], axis=1
        )
        piece = jnp.dot(mixed, columns, preferred_element_type=jnp.float32)
        out[0, :, start * cols : (start + step) * cols] = piece.astype(jnp.bfloat16)
        square = jnp.sum(piece * piece, axis=0, keepdims=True)
        total[0] += square[:, :cols] + square[:, cols:]


def tile_sources(mine, count, spread):
    found = {(mine, b): (0, spread * b) for b in range(count)}
    for hop in range(1, count):
        for i in range(count - hop):
            if mine + hop < count:
                found[mine + hop, (mine + hop + i) % count] = (hop, spread * i)
            if mine - hop >= 0:
                found[mine - hop, (mine - hop - i) % count] = (count - 1 + hop, spread * i)
    return found


def precond_tiles_kernel(me, left, grad, *refs):
    rights, out, total = refs[:-2], refs[-2], refs[-1]
    slabs, _, rows, cols = left.shape
    parts = grad.shape[0]
    spread = slabs // parts
    mixed = left_product(left, grad)
    total[...] = jnp.zeros_like(total)
    for mine in range(parts):

        @pl.when(me[0] == mine)
        def _(mine=mine):
            found = tile_sources(mine, parts, spread)
            for b in range(parts):
                piece = jnp.zeros((rows, spread * cols), jnp.float32)
                for a in range(parts):
                    turned = (a, b) not in found
                    array, first = found[(b, a) if turned else (a, b)]
                    tile = jnp.concatenate(
                        [rights[array][first + s, 0] for s in range(spread)], axis=1
                    )
                    piece += lax.dot_general(
                        mixed[:, a * rows : (a + 1) * rows],
                        tile,
                        (((1,), (1 if turned else 0,)), ((), ())),
                        preferred_element_type=jnp.float32,
                    )
                out[0, :, b * rows : (b + 1) * rows] = piece.astype(jnp.bfloat16)
                square = jnp.sum(piece * piece, axis=0, keepdims=True)
                total[0] += sum(square[:, s * cols : (s + 1) * cols] for s in range(spread))


def gather_roots(right):
    slabs, per, rows, cols = right.shape
    count, me = lax.axis_size("shard"), lax.axis_index("shard")
    if count != 4 or slabs % count or rows * count != slabs * cols:
        return [lax.all_gather(right, "shard", axis=0)]
    spread = slabs // count
    down = [(a, a - 1) for a in range(1, count)]
    up = [(a, a + 1) for a in range(count - 1)]
    lane = jnp.arange(spread * (count - 1), dtype=jnp.int32)
    parts = [right]
    for pairs, sign in ((down, 1), (up, -1)):
        tiles = (me + sign * (lane // spread)) % count
        moving = reorder(
            right.reshape(slabs, per * rows, cols), tiles * spread + lane % spread
        ).reshape(lane.shape[0], per, rows, cols)
        for hop in range(1, count):
            moving = lax.ppermute(moving, "shard", pairs)
            parts.append(moving)
            moving = moving[: spread * (count - 1 - hop)]
    return parts


def precondition(left, start, grad_blocks, rights):
    shards, count, rows, width = grad_blocks.shape
    slabs, _, _, cols = left.shape
    size = shards * rows
    whole = len(rights) == 1
    if whole:
        right_specs = [pl.BlockSpec((shards, slabs, 1, rows, cols), lambda m, me: (0, 0, start + m, 0, 0))]
    else:
        right_specs = [
            pl.BlockSpec((right.shape[0], 1, rows, cols), lambda m, me: (0, start + m, 0, 0))
            for right in rights
        ]
    body = precond_tiles_kernel
    if whole:
        body = lambda me, *refs: precond_kernel(*refs)
    return pl.pallas_call(
        body,
        grid_spec=pltpu.PrefetchScalarGridSpec(
            num_scalar_prefetch=1,
            grid=(count,),
            in_specs=[
                pl.BlockSpec((slabs, 1, rows, cols), lambda m, me: (0, start + m, 0, 0)),
                pl.BlockSpec((shards, 1, rows, width), lambda m, me: (0, m, 0, 0)),
            ]
            + right_specs,
            out_specs=[
                pl.BlockSpec((1, rows, width), lambda m, me: (m, 0, 0)),
                pl.BlockSpec((1, 1, cols), lambda m, me: (m, 0, 0)),
            ],
        ),
        out_shape=[
            jax.ShapeDtypeStruct((count, rows, width), jnp.bfloat16),
            jax.ShapeDtypeStruct((count, 1, cols), jnp.float32),
        ],
        compiler_params=params(),
        cost_estimate=SMALL,
    )(lax.axis_index("shard").reshape(1), left, grad_blocks, *rights)


def update_kernel(scale, weights, precond, out):
    slabs = weights.shape[0]
    factor = scale[pl.program_id(0)]
    old = jnp.concatenate([weights[s, 0] for s in range(slabs)], axis=1).astype(jnp.float32)
    step = factor * precond[0].astype(jnp.float32) + DECAY_RATE * old
    out[0] = (old - LEARNING * step).astype(jnp.bfloat16)


def update(weights, start, precond, scale):
    slabs, _, rows, cols = weights.shape
    count = precond.shape[0]
    width = slabs * cols
    own = pl.BlockSpec((1, rows, width), lambda m, scale: (m, 0, 0))
    return pl.pallas_call(
        update_kernel,
        grid_spec=pltpu.PrefetchScalarGridSpec(
            num_scalar_prefetch=1,
            grid=(count,),
            in_specs=[
                pl.BlockSpec((slabs, 1, rows, cols), lambda m, scale: (0, start + m, 0, 0)),
                own,
            ],
            out_specs=own,
        ),
        out_shape=jax.ShapeDtypeStruct((count, rows, width), jnp.bfloat16),
        compiler_params=params(),
        cost_estimate=SMALL,
    )(scale, weights, precond)


def pair_kernel(picked, first, second, third, fourth, received, send_a, keep_a, send_b, keep_b):
    half = first.shape[1] // 2
    added = [
        (own[0].astype(jnp.float32) + received[u].astype(jnp.float32)).astype(jnp.bfloat16)
        for u, own in enumerate((first, second, third, fourth))
    ]
    for ref, chosen, start in (
        (send_a, (1, 3), 0),
        (keep_a, (0, 2), 0),
        (send_b, (2, 3), half),
        (keep_b, (0, 1), half),
    ):
        for i, u in enumerate(chosen):
            ref[i, 0] = added[u][start : start + half]


def add_pair(partials, received, picked):
    _, rows, width = partials.shape
    count = received.shape[0] // 4
    half = jax.ShapeDtypeStruct((2, count, rows // 2, width), partials.dtype)

    def own(u):
        return pl.BlockSpec((1, rows, width), lambda i, picked: (picked[4 * i + u], 0, 0))

    return pl.pallas_call(
        pair_kernel,
        grid_spec=pltpu.PrefetchScalarGridSpec(
            num_scalar_prefetch=1,
            grid=(count,),
            in_specs=[own(0), own(1), own(2), own(3)]
            + [pl.BlockSpec((4, rows, width), lambda i, picked: (i, 0, 0))],
            out_specs=[pl.BlockSpec((2, 1, rows // 2, width), lambda i, picked: (0, i, 0, 0))] * 4,
        ),
        out_shape=[half] * 4,
        compiler_params=params(),
        cost_estimate=SMALL,
    )(picked, partials, partials, partials, partials, received)


def add(one, two):
    return (one.astype(jnp.float32) + two.astype(jnp.float32)).astype(jnp.bfloat16)


def swap(array, bit):
    devices = lax.axis_size("tensor")
    return lax.ppermute(array, "tensor", [(t, t ^ bit) for t in range(devices)])


def swap_core(array):
    return lax.ppermute(array, "section", [(0, 1), (1, 0)])


def by_bits():
    return (lax.axis_size("tensor"), lax.axis_size("section")) == (4, 2)


def sum_blocks(partials, picked, after=()):
    count = picked.shape[1]
    if not by_bits():
        ordered = reorder(partials, picked.reshape(-1))
        return lax.psum_scatter(ordered, GROUP, scatter_dimension=0, tiled=True), after
    core = lax.axis_index("section")
    relative = jnp.arange(4, dtype=jnp.int32) ^ lax.axis_index("tensor")
    mine = jnp.take(picked, relative * 2 + core, axis=0).T.reshape(-1)
    other = jnp.take(picked, relative * 2 + 1 - core, axis=0).T.reshape(-1)
    received = swap_core(reorder(partials, other))
    send_a, keep_a, send_b, keep_b = add_pair(partials, received, mine)
    sum_a = add(keep_a, swap(send_a, 1))
    sum_b = add(keep_b, swap(send_b, 2))
    if after:
        sum_a, sum_b, after = lax.optimization_barrier((sum_a, sum_b, after))
    last_a = add(sum_a[0], swap(sum_a[1], 2))
    last_b = add(sum_b[0], swap(sum_b[1], 1))
    return jnp.concatenate([last_a, last_b], axis=1), after


def gather_blocks(first, second, by_entry, early_work, finish):
    total = by_entry.size
    if not by_bits():
        mine = jnp.concatenate([first, second], axis=0)
        gathered = lax.all_gather(mine, GROUP, axis=0, tiled=True)
        return place_blocks([gathered], by_entry.reshape(-1), total, []), finish(early_work)
    cut = first.shape[0]
    tensor, core = lax.axis_index("tensor"), lax.axis_index("section")
    x_first, y_second = swap(first, 1), swap(second, 2)
    y_first, x_second = swap(first, 2), swap(second, 1)
    x_first, y_second, early_work = lax.optimization_barrier((x_first, y_second, early_work))
    d_first, d_second = swap(x_first, 2), swap(y_second, 1)

    def targets(bits, core):
        places = [by_entry[(tensor ^ bit) * 2 + core] for bit in bits]
        return [piece for place in places for piece in (place[:cut], place[cut:])]

    near = [first, second, x_first, x_second, y_first, y_second]
    near_target = targets((0, 1, 2), core) + targets((0, 1, 2), 1 - core)
    near = near + [swap_core(piece) for piece in near]
    far = [d_first, d_second]
    far_target = targets((3,), core) + targets((3,), 1 - core)
    far = far + [swap_core(piece) for piece in far]
    placed = place_blocks(near, jnp.concatenate(near_target), total, [])
    placed, late_work = lax.optimization_barrier((placed, finish(early_work)))
    return place_blocks(far, jnp.concatenate(far_target), total, [placed]), late_work


def shards(
    grad_parts,
    weights,
    adam_m,
    adam_v,
    left_stat,
    right_stat,
    left_root,
    right_root,
    block_owner,
    block_matrix,
    factors,
    factor_grad,
    factor_m,
    factor_v,
):
    capacity = left_stat.shape[0]
    blocks, rows, cols = weights.shape
    size = left_stat.shape[1]
    group = size // cols
    per = blocks // group
    sends = -(-capacity // group)
    owner_index = lax.axis_index("shard")
    group_index = lax.axis_index(GROUP)
    owner_count = lax.axis_size("shard")

    ids = jnp.arange(blocks, dtype=jnp.int32)
    owners = jnp.arange(owner_count, dtype=jnp.int32)
    loads = jnp.sum((block_owner[None, :] == owners[:, None]).astype(jnp.int32), axis=1)
    heavy = jnp.min(jnp.where(loads == jnp.max(loads), owners, owner_count))
    turn = (block_owner - heavy) % owner_count
    own_turn = (owner_index - heavy) % owner_count
    before = (turn[None, :] < turn[:, None]) | (
        (turn[None, :] == turn[:, None]) & (ids[None, :] < ids[:, None])
    )
    position = jnp.sum(before.astype(jnp.int32), axis=1)
    place = (position % group) * per + position // group
    order = jnp.sum(jnp.where(place[None, :] == ids[:, None], ids[None, :], 0), axis=1)

    first = jnp.sum((turn < own_turn).astype(jnp.int32))
    held = jnp.sum((turn == own_turn).astype(jnp.int32))
    early = sends - 1 if blocks - capacity <= group else 0
    is_heavy = own_turn == 0
    own_entry = (first - group_index + group - 1) // group

    def deal(tiles):
        return lax.all_to_all(
            tiles.reshape(group, per, rows, cols), GROUP, split_axis=0, concat_axis=0, tiled=True
        )

    by_entry = order.reshape(group, per)
    partials = grad_parts[0]
    right_sent = reorder(right_root, order)
    right_sent, by_entry = lax.optimization_barrier((right_sent, by_entry))
    right_dealt = deal(right_sent)
    cuts = [(0, early), (early, per)] if early else [(0, per)]
    if early:
        gradient = [sum_blocks(partials, by_entry[:, :early])[0]]
        right_dealt, last_entries = lax.optimization_barrier((right_dealt, by_entry[:, early:]))
        rights = gather_roots(right_dealt)
        last_gradient, rights[1::3] = sum_blocks(partials, last_entries, rights[1::3])
        gradient.append(last_gradient)
    else:
        gradient = [sum_blocks(partials, by_entry)[0]]
        rights = gather_roots(right_dealt)
    grad_blocks = [lax.all_gather(part, "shard", axis=0) for part in gradient]
    left_dealt = deal(reorder(left_root, order))
    weights_dealt = deal(reorder(weights, order))
    tiles = jnp.concatenate(gradient, axis=0).reshape(per, rows, group, cols)
    tiles = deal(jnp.transpose(tiles, (2, 0, 1, 3)))

    if early:
        grad_blocks[0], rights, left_dealt, weights_dealt, tiles = lax.optimization_barrier(
            (grad_blocks[0], rights, left_dealt, weights_dealt, tiles)
        )
        slabs = grams(grad_blocks[0], jnp.arange(early, dtype=jnp.int32))
        slabs, left_dealt, tiles = lax.optimization_barrier((slabs, left_dealt, tiles))
        received = lax.all_to_all(slabs, GROUP, split_axis=0, concat_axis=0, tiled=True)
    adam_m_new, adam_v_new, adam_total = adam(
        tiles.reshape(blocks, rows, cols), place, adam_m, adam_v
    )
    entry = jnp.where(is_heavy, early, own_entry) - early
    last_slabs = grams(grad_blocks[-1], jnp.clip(entry, 0, per - 1 - early).reshape(1))
    pieces = [
        precondition(left_dealt, a, part, rights) for (a, _), part in zip(cuts, grad_blocks)
    ]
    precond_total = jnp.concatenate([total for _, total in pieces], axis=0)

    matrix_range = jnp.arange(MATS, dtype=jnp.int32)
    onehot = (block_matrix[:, None] == matrix_range[None, :]).astype(jnp.float32)
    own_order = lax.dynamic_slice_in_dim(order, group_index * per, per)
    own_onehot = jnp.sum(
        jnp.where((own_order[:, None] == ids[None, :])[:, :, None], onehot[None, :, :], 0.0), axis=1
    )
    adam_part = jnp.sum(jnp.sum(adam_total, axis=(1, 2))[:, None] * onehot, axis=0)
    shampoo_part = jnp.sum(jnp.sum(precond_total, axis=(1, 2))[:, None] * own_onehot, axis=0)
    parts = jnp.pad(jnp.stack([adam_part, shampoo_part]), ((0, 6), (0, LANES - MATS)))
    if early:
        received, last_slabs, parts = lax.optimization_barrier((received, last_slabs, parts))
    devices = owner_count * group
    parts = lax.all_to_all(
        jnp.broadcast_to(parts[None], (devices,) + parts.shape), ALL, 0, 0, tiled=True
    )
    adam_norm, shampoo_norm = jnp.sum(parts, axis=0)[:2, :MATS]
    counts = jnp.sum(onehot, axis=0) * float(size * size)
    graft_scale = jnp.sqrt(adam_norm / (shampoo_norm + FLOOR_RATE * counts))
    block_scale = jnp.sum(own_onehot * graft_scale[None, :], axis=1)

    last = lax.all_to_all(last_slabs, GROUP, split_axis=0, concat_axis=0, tiled=True)
    updated = [
        update(weights_dealt, a, piece, block_scale[a:b])
        for (a, b), (piece, _) in zip(cuts, pieces)
    ]
    if len(updated) == 1:
        updated = [updated[0][: per // 2], updated[0][per // 2 :]]
    stats = ()
    if early:
        ranks = jnp.arange(early * group, dtype=jnp.int32)
        base = jnp.where(is_heavy, 0, capacity - early * group)
        filled = jnp.where(is_heavy, 1, 0) * jnp.ones_like(ranks)
        stats = refresh(
            left_stat, right_stat, received, base, ranks % group, ranks // group, filled, stats
        )
    base = jnp.where(is_heavy, early * group, 0)
    ranks = base + jnp.arange(capacity - early * group, dtype=jnp.int32)
    filled = (ranks < held).astype(jnp.int32)
    source = (first + ranks) % group
    nothing = jnp.zeros_like(ranks)
    finish = lambda earlier: refresh(
        left_stat, right_stat, last, base, source, nothing, filled, earlier
    )
    new_weights, (left_new, right_new) = gather_blocks(*updated, by_entry, stats, finish)

    factor_m_new, factor_v_new, factor_step = adam_direction(
        factor_grad.astype(jnp.float32), factor_m, factor_v
    )
    factors_new = factors - LEARNING * (factor_step + DECAY_RATE * factors)
    return (
        new_weights,
        adam_m_new,
        adam_v_new,
        left_new,
        right_new,
        factors_new,
        factor_m_new,
        factor_v_new,
    )


def solution(mesh):
    tile = P(None, "shard", GROUP)
    stat = P("shard", None, GROUP)
    factor = P("shard", GROUP)
    in_specs = (P(GROUP, None, "shard", None), tile, tile, tile, stat, stat, tile, tile, P(), P())
    out_specs = (P(None, "shard", None), tile, tile, stat, stat)
    return jax.shard_map(
        shards,
        mesh=mesh,
        in_specs=in_specs + (factor,) * 4,
        out_specs=out_specs + (factor,) * 3,
        check_vma=False,
    )
```

```python
import functools

import jax
import jax.numpy as jnp
from jax import lax
from jax.experimental import pallas as pl
from jax.experimental.pallas import tpu as pltpu
from jax.sharding import PartitionSpec as P

MATS = 5

BETA_ONE = 0.9
BETA_TWO = 0.95
BETA_STAT = 0.95
LEARNING = 0.1
DECAY_RATE = 0.1
EPSILON = 1e-08
FLOOR_RATE = 1e-06
CORRECT_ONE = 1.0 - 0.9**10
CORRECT_TWO = 1.0 - 0.95**10

GROUP = ("tensor", "section")
ALL = ("shard", "tensor", "section")
VMEM_LIMIT = 48 * 1024 * 1024
LANES = 128
SMALL = pl.CostEstimate(flops=0, bytes_accessed=0, transcendentals=0)


def params():
    return pltpu.CompilerParams(vmem_limit_bytes=VMEM_LIMIT)


def adam_direction(grad_float, moment, second):
    moment_new = BETA_ONE * moment + (1.0 - BETA_ONE) * grad_float
    second_new = BETA_TWO * second + (1.0 - BETA_TWO) * grad_float * grad_float
    direction = moment_new / CORRECT_ONE / (jnp.sqrt(second_new / CORRECT_TWO) + EPSILON)
    return (moment_new, second_new, direction)


def copy_blocks(pairs, held, arrived, left):
    into = [
        pltpu.make_async_copy(source, held.at[i], arrived.at[i])
        for i, (source, _) in enumerate(pairs)
    ]
    out_of = [
        pltpu.make_async_copy(held.at[i], target, left.at[i]) for i, (_, target) in enumerate(pairs)
    ]
    for copy in into:
        copy.start()
    for arrival, copy in zip(into, out_of):
        arrival.wait()
        copy.start()
    for copy in out_of:
        copy.wait()


def copy_scratch(count, tile, kind):
    return [
        pltpu.VMEM((count,) + tile, kind),
        pltpu.SemaphoreType.DMA((count,)),
        pltpu.SemaphoreType.DMA((count,)),
    ]


def reorder_kernel(order, blocks, out, held, arrived, left):
    pairs = [(blocks.at[order[i]], out.at[i]) for i in range(out.shape[0])]
    copy_blocks(pairs, held, arrived, left)


def reorder(blocks, order):
    count, tile = order.shape[0], blocks.shape[1:]
    return pl.pallas_call(
        reorder_kernel,
        grid_spec=pltpu.PrefetchScalarGridSpec(
            num_scalar_prefetch=1,
            grid=(1,),
            in_specs=[pl.BlockSpec(memory_space=pl.ANY)],
            out_specs=pl.BlockSpec(memory_space=pl.ANY),
            scratch_shapes=copy_scratch(count, tile, blocks.dtype),
        ),
        out_shape=jax.ShapeDtypeStruct((count,) + tile, blocks.dtype),
        compiler_params=params(),
        cost_estimate=SMALL,
    )(order, blocks)


def place_kernel(sources, target, *refs):
    out, held, arrived, left = refs[-4:]
    blocks = [ref.at[i] for ref in refs[:sources] for i in range(ref.shape[0])]
    pairs = [(block, out.at[target[i]]) for i, block in enumerate(blocks)]
    copy_blocks(pairs, held, arrived, left)


def place_blocks(arrays, target, total, earlier):
    tile, kind = arrays[0].shape[1:], arrays[0].dtype
    inputs = list(arrays) + list(earlier)
    return pl.pallas_call(
        functools.partial(place_kernel, len(arrays)),
        grid_spec=pltpu.PrefetchScalarGridSpec(
            num_scalar_prefetch=1,
            grid=(1,),
            in_specs=[pl.BlockSpec(memory_space=pl.ANY)] * len(inputs),
            out_specs=pl.BlockSpec(memory_space=pl.ANY),
            scratch_shapes=copy_scratch(target.shape[0], tile, kind),
        ),
        out_shape=jax.ShapeDtypeStruct((total,) + tile, kind),
        input_output_aliases={1 + len(arrays) + i: i for i in range(len(earlier))},
        compiler_params=params(),
        cost_estimate=SMALL,
    )(target, *inputs)


def adam_kernel(place, grad, moment, second, moment_out, second_out, total):
    moment_new, second_new, direction = adam_direction(
        grad[0].astype(jnp.float32), moment[0], second[0]
    )
    moment_out[0] = moment_new
    second_out[0] = second_new
    total[0] = jnp.sum(direction * direction, axis=0, keepdims=True)


def adam(grad_tiles, place, moment, second):
    count, rows, cols = moment.shape
    own = pl.BlockSpec((1, rows, cols), lambda i, place: (i, 0, 0))
    return pl.pallas_call(
        adam_kernel,
        grid_spec=pltpu.PrefetchScalarGridSpec(
            num_scalar_prefetch=1,
            grid=(count,),
            in_specs=[
                pl.BlockSpec((1, rows, cols), lambda i, place: (place[i], 0, 0)),
                own,
                own,
            ],
            out_specs=[own, own, pl.BlockSpec((1, 1, cols), lambda i, place: (i, 0, 0))],
        ),
        out_shape=[
            jax.ShapeDtypeStruct(moment.shape, jnp.float32),
            jax.ShapeDtypeStruct(moment.shape, jnp.float32),
            jax.ShapeDtypeStruct((count, 1, cols), jnp.float32),
        ],
        compiler_params=params(),
        cost_estimate=SMALL,
    )(place, grad_tiles, moment, second)


def gram_kernel(chosen, grad, out):
    parts, _, rows, width = grad.shape
    size = parts * rows
    whole = grad[:, 0].reshape(size, width)
    turned = whole.T
    step = 2 * LANES
    for start in range(0, size, step):
        left = lax.dot_general(
            whole,
            whole[start : start + step, :],
            (((1,), (1,)), ((), ())),
            preferred_element_type=jnp.float32,
        ).astype(jnp.bfloat16)
        right = lax.dot_general(
            turned,
            whole[:, start : start + step],
            (((1,), (0,)), ((), ())),
            preferred_element_type=jnp.float32,
        ).astype(jnp.bfloat16)
        for half in range(2):
            slab = start // LANES + half
            out[slab, 0, 0] = left[:, half * LANES : (half + 1) * LANES]
            out[slab, 0, 1] = right[:, half * LANES : (half + 1) * LANES]


def grams(grad_blocks, chosen):
    shards, per, rows, width = grad_blocks.shape
    size = shards * rows
    slabs = size // LANES
    count = chosen.shape[0]
    return pl.pallas_call(
        gram_kernel,
        grid_spec=pltpu.PrefetchScalarGridSpec(
            num_scalar_prefetch=1,
            grid=(count,),
            in_specs=[
                pl.BlockSpec((shards, 1, rows, width), lambda j, chosen: (0, chosen[j], 0, 0))
            ],
            out_specs=pl.BlockSpec(
                (slabs, 1, 2, size, LANES), lambda j, chosen: (0, j, 0, 0, 0)
            ),
        ),
        out_shape=jax.ShapeDtypeStruct((slabs, count, 2, size, LANES), jnp.bfloat16),
        compiler_params=params(),
        cost_estimate=SMALL,
    )(chosen, grad_blocks)


def stat_kernel(
    base, source, entry, filled, left_stat, right_stat, left_gram, right_gram, *refs
):
    left_out, right_out = refs[-2:]
    full = filled[pl.program_id(0)] > 0
    left = left_gram[0, 0, 0].astype(jnp.float32)
    right = right_gram[0, 0, 0].astype(jnp.float32)
    left_out[0] = BETA_STAT * left_stat[0] + jnp.where(full, (1.0 - BETA_STAT) * left, 0.0)
    right_out[0] = BETA_STAT * right_stat[0] + jnp.where(full, (1.0 - BETA_STAT) * right, 0.0)


def refresh(left_stat, right_stat, received, base, source, entry, filled, earlier):
    slots, size, cols = left_stat.shape
    count = source.shape[0]
    own = pl.BlockSpec((1, size, cols), lambda r, base, source, entry, filled: (base[0] + r, 0, 0))
    gram = (1, 1, 1, size, cols)
    shape = jax.ShapeDtypeStruct(left_stat.shape, jnp.float32)
    return pl.pallas_call(
        stat_kernel,
        grid_spec=pltpu.PrefetchScalarGridSpec(
            num_scalar_prefetch=4,
            grid=(count,),
            in_specs=[
                own,
                own,
                pl.BlockSpec(
                    gram, lambda r, base, source, entry, filled: (source[r], entry[r], 0, 0, 0)
                ),
                pl.BlockSpec(
                    gram, lambda r, base, source, entry, filled: (source[r], entry[r], 1, 0, 0)
                ),
            ]
            + [pl.BlockSpec(memory_space=pl.ANY)] * len(earlier),
            out_specs=[own, own],
        ),
        out_shape=[shape, shape],
        input_output_aliases={8 + i: i for i in range(len(earlier))},
        compiler_params=params(),
        cost_estimate=SMALL,
    )(
        base.reshape(1), source, entry, filled, left_stat, right_stat, received, received, *earlier
    )


def left_product(left, grad):
    slabs, _, rows, _ = left.shape
    left_rows = jnp.concatenate([left[s, 0] for s in range(slabs)], axis=1)
    whole = grad[:, 0].reshape(grad.shape[0] * rows, grad.shape[3])
    return jnp.dot(left_rows, whole, preferred_element_type=jnp.float32).astype(jnp.bfloat16)


def precond_kernel(left, grad, right, out, total):
    slabs, _, rows, cols = left.shape
    parts = grad.shape[0]
    mixed = left_product(left, grad)
    total[...] = jnp.zeros_like(total)
    step = 2
    for start in range(0, slabs, step):
        columns = jnp.concatenate(
            [right[:, s, 0].reshape(parts * rows, cols) for s in range(start, start + step)], axis=1
        )
        piece = jnp.dot(mixed, columns, preferred_element_type=jnp.float32)
        out[0, :, start * cols : (start + step) * cols] = piece.astype(jnp.bfloat16)
        square = jnp.sum(piece * piece, axis=0, keepdims=True)
        total[0] += square[:, :cols] + square[:, cols:]


def tile_sources(mine, count, spread):
    found = {(mine, b): (0, spread * b) for b in range(count)}
    for hop in range(1, count):
        for i in range(count - hop):
            if mine + hop < count:
                found[mine + hop, (mine + hop + i) % count] = (hop, spread * i)
            if mine - hop >= 0:
                found[mine - hop, (mine - hop - i) % count] = (count - 1 + hop, spread * i)
    return found


def precond_tiles_kernel(me, left, grad, *refs):
    rights, out, total = refs[:-2], refs[-2], refs[-1]
    slabs, _, rows, cols = left.shape
    parts = grad.shape[0]
    spread = slabs // parts
    mixed = left_product(left, grad)
    total[...] = jnp.zeros_like(total)
    for mine in range(parts):

        @pl.when(me[0] == mine)
        def _(mine=mine):
            found = tile_sources(mine, parts, spread)
            for b in range(parts):
                piece = jnp.zeros((rows, spread * cols), jnp.float32)
                for a in range(parts):
                    turned = (a, b) not in found
                    array, first = found[(b, a) if turned else (a, b)]
                    tile = jnp.concatenate(
                        [rights[array][first + s, 0] for s in range(spread)], axis=1
                    )
                    piece += lax.dot_general(
                        mixed[:, a * rows : (a + 1) * rows],
                        tile,
                        (((1,), (1 if turned else 0,)), ((), ())),
                        preferred_element_type=jnp.float32,
                    )
                out[0, :, b * rows : (b + 1) * rows] = piece.astype(jnp.bfloat16)
                square = jnp.sum(piece * piece, axis=0, keepdims=True)
                total[0] += sum(square[:, s * cols : (s + 1) * cols] for s in range(spread))


def first_hop(right):
    slabs, per, rows, cols = right.shape
    count, me = lax.axis_size("shard"), lax.axis_index("shard")
    spread = slabs // count
    lane = jnp.arange(spread * (count - 1), dtype=jnp.int32)
    moved = []
    for sign in (1, -1):
        tiles = (me + sign * (lane // spread)) % count
        picked = reorder(right.reshape(slabs, per * rows, cols), tiles * spread + lane % spread)
        moved.append(picked.reshape(lane.shape[0], per, rows, cols))
    return hop(moved)


def hop(moved):
    count = lax.axis_size("shard")
    down = [(a, a - 1) for a in range(1, count)]
    up = [(a, a + 1) for a in range(count - 1)]
    return lax.ppermute(moved[0], "shard", down), lax.ppermute(moved[1], "shard", up)


def next_hop(moved, spread):
    return hop([part[: part.shape[0] - spread] for part in moved])


def precondition(left, start, grad_blocks, rights):
    shards, count, rows, width = grad_blocks.shape
    slabs, _, _, cols = left.shape
    size = shards * rows
    whole = len(rights) == 1
    if whole:
        right_specs = [pl.BlockSpec((shards, slabs, 1, rows, cols), lambda m, me: (0, 0, start + m, 0, 0))]
    else:
        right_specs = [
            pl.BlockSpec((right.shape[0], 1, rows, cols), lambda m, me: (0, start + m, 0, 0))
            for right in rights
        ]
    body = precond_tiles_kernel
    if whole:
        body = lambda me, *refs: precond_kernel(*refs)
    return pl.pallas_call(
        body,
        grid_spec=pltpu.PrefetchScalarGridSpec(
            num_scalar_prefetch=1,
            grid=(count,),
            in_specs=[
                pl.BlockSpec((slabs, 1, rows, cols), lambda m, me: (0, start + m, 0, 0)),
                pl.BlockSpec((shards, 1, rows, width), lambda m, me: (0, m, 0, 0)),
            ]
            + right_specs,
            out_specs=[
                pl.BlockSpec((1, rows, width), lambda m, me: (m, 0, 0)),
                pl.BlockSpec((1, 1, cols), lambda m, me: (m, 0, 0)),
            ],
        ),
        out_shape=[
            jax.ShapeDtypeStruct((count, rows, width), jnp.bfloat16),
            jax.ShapeDtypeStruct((count, 1, cols), jnp.float32),
        ],
        compiler_params=params(),
        cost_estimate=SMALL,
    )(lax.axis_index("shard").reshape(1), left, grad_blocks, *rights)


def update_kernel(scale, weights, precond, out):
    slabs = weights.shape[0]
    factor = scale[pl.program_id(0)]
    old = jnp.concatenate([weights[s, 0] for s in range(slabs)], axis=1).astype(jnp.float32)
    step = factor * precond[0].astype(jnp.float32) + DECAY_RATE * old
    out[0] = (old - LEARNING * step).astype(jnp.bfloat16)


def update(weights, start, precond, scale):
    slabs, _, rows, cols = weights.shape
    count = precond.shape[0]
    width = slabs * cols
    own = pl.BlockSpec((1, rows, width), lambda m, scale: (m, 0, 0))
    return pl.pallas_call(
        update_kernel,
        grid_spec=pltpu.PrefetchScalarGridSpec(
            num_scalar_prefetch=1,
            grid=(count,),
            in_specs=[
                pl.BlockSpec((slabs, 1, rows, cols), lambda m, scale: (0, start + m, 0, 0)),
                own,
            ],
            out_specs=own,
        ),
        out_shape=jax.ShapeDtypeStruct((count, rows, width), jnp.bfloat16),
        compiler_params=params(),
        cost_estimate=SMALL,
    )(scale, weights, precond)


def pair_kernel(picked, first, second, third, fourth, received, send_a, keep_a, send_b, keep_b):
    half = first.shape[1] // 2
    added = [
        (own[0].astype(jnp.float32) + received[u].astype(jnp.float32)).astype(jnp.bfloat16)
        for u, own in enumerate((first, second, third, fourth))
    ]
    for ref, chosen, start in (
        (send_a, (1, 3), 0),
        (keep_a, (0, 2), 0),
        (send_b, (2, 3), half),
        (keep_b, (0, 1), half),
    ):
        for i, u in enumerate(chosen):
            ref[i, 0] = added[u][start : start + half]


def add_pair(partials, received, picked):
    _, rows, width = partials.shape
    count = received.shape[0] // 4
    half = jax.ShapeDtypeStruct((2, count, rows // 2, width), partials.dtype)

    def own(u):
        return pl.BlockSpec((1, rows, width), lambda i, picked: (picked[4 * i + u], 0, 0))

    return pl.pallas_call(
        pair_kernel,
        grid_spec=pltpu.PrefetchScalarGridSpec(
            num_scalar_prefetch=1,
            grid=(count,),
            in_specs=[own(0), own(1), own(2), own(3)]
            + [pl.BlockSpec((4, rows, width), lambda i, picked: (i, 0, 0))],
            out_specs=[pl.BlockSpec((2, 1, rows // 2, width), lambda i, picked: (0, i, 0, 0))] * 4,
        ),
        out_shape=[half] * 4,
        compiler_params=params(),
        cost_estimate=SMALL,
    )(picked, partials, partials, partials, partials, received)


def add(one, two):
    return (one.astype(jnp.float32) + two.astype(jnp.float32)).astype(jnp.bfloat16)


def swap(array, bit):
    devices = lax.axis_size("tensor")
    return lax.ppermute(array, "tensor", [(t, t ^ bit) for t in range(devices)])


def swap_core(array):
    return lax.ppermute(array, "section", [(0, 1), (1, 0)])


def pick(picked):
    core = lax.axis_index("section")
    relative = jnp.arange(4, dtype=jnp.int32) ^ lax.axis_index("tensor")
    mine = jnp.take(picked, relative * 2 + core, axis=0).T.reshape(-1)
    other = jnp.take(picked, relative * 2 + 1 - core, axis=0).T.reshape(-1)
    return mine, other


def first_sums(partials, sent, mine):
    received = swap_core(sent)
    send_a, keep_a, send_b, keep_b = add_pair(partials, received, mine)
    return add(keep_a, swap(send_a, 1)), add(keep_b, swap(send_b, 2))


def last_sums(sum_a, sum_b):
    last_a = add(sum_a[0], swap(sum_a[1], 2))
    last_b = add(sum_b[0], swap(sum_b[1], 1))
    return jnp.concatenate([last_a, last_b], axis=1)


def gather_blocks(first, second, by_entry, early_work, finish):
    total = by_entry.size
    cut = first.shape[0]
    tensor, core = lax.axis_index("tensor"), lax.axis_index("section")
    x_first, y_second = swap(first, 1), swap(second, 2)
    y_first, x_second = swap(first, 2), swap(second, 1)
    x_first, y_second, early_work = lax.optimization_barrier((x_first, y_second, early_work))
    d_first, d_second = swap(x_first, 2), swap(y_second, 1)

    def targets(bits, core):
        places = [by_entry[(tensor ^ bit) * 2 + core] for bit in bits]
        return [piece for place in places for piece in (place[:cut], place[cut:])]

    near = [first, second, x_first, x_second, y_first, y_second]
    near_target = targets((0, 1, 2), core) + targets((0, 1, 2), 1 - core)
    near = near + [swap_core(piece) for piece in near]
    placed = place_blocks(near, jnp.concatenate(near_target), total, [])
    late_work = finish(early_work)
    d_first, d_second, placed, late_work = lax.optimization_barrier(
        (d_first, d_second, placed, late_work)
    )
    far = [d_first, d_second]
    far_target = targets((3,), core) + targets((3,), 1 - core)
    far = far + [swap_core(piece) for piece in far]
    return place_blocks(far, jnp.concatenate(far_target), total, [placed]), late_work


def shards(
    grad_parts,
    weights,
    adam_m,
    adam_v,
    left_stat,
    right_stat,
    left_root,
    right_root,
    block_owner,
    block_matrix,
    factors,
    factor_grad,
    factor_m,
    factor_v,
):
    capacity = left_stat.shape[0]
    blocks, rows, cols = weights.shape
    size = left_stat.shape[1]
    group = size // cols
    per = blocks // group
    sends = -(-capacity // group)
    owner_index = lax.axis_index("shard")
    group_index = lax.axis_index(GROUP)
    owner_count = lax.axis_size("shard")

    ids = jnp.arange(blocks, dtype=jnp.int32)
    owners = jnp.arange(owner_count, dtype=jnp.int32)
    loads = jnp.sum((block_owner[None, :] == owners[:, None]).astype(jnp.int32), axis=1)
    heavy = jnp.min(jnp.where(loads == jnp.max(loads), owners, owner_count))
    turn = (block_owner - heavy) % owner_count
    own_turn = (owner_index - heavy) % owner_count
    before = (turn[None, :] < turn[:, None]) | (
        (turn[None, :] == turn[:, None]) & (ids[None, :] < ids[:, None])
    )
    position = jnp.sum(before.astype(jnp.int32), axis=1)
    place = (position % group) * per + position // group
    order = jnp.sum(jnp.where(place[None, :] == ids[:, None], ids[None, :], 0), axis=1)

    first = jnp.sum((turn < own_turn).astype(jnp.int32))
    held = jnp.sum((turn == own_turn).astype(jnp.int32))
    early = sends - 1 if blocks - capacity <= group else 0
    is_heavy = own_turn == 0
    own_entry = (first - group_index + group - 1) // group

    def deal(tiles):
        return lax.all_to_all(
            tiles.reshape(group, per, rows, cols), GROUP, split_axis=0, concat_axis=0, tiled=True
        )

    by_entry = order.reshape(group, per)
    partials = grad_parts[0]
    cuts = [(0, early), (early, per)] if early else [(0, per)]
    orders = [pick(by_entry[:, a:b]) for a, b in cuts]
    right_dealt = deal(reorder(right_root, order))
    sent = [reorder(partials, other) for _, other in orders]
    right_dealt, sent[-1] = lax.optimization_barrier((right_dealt, sent[-1]))
    if early and owner_count == 4 and rows * owner_count == size:
        spread = group // owner_count
        near = first_hop(right_dealt)
        sums = first_sums(partials, sent[0], orders[0][0])
        sums, near = lax.optimization_barrier((sums, near))
        gradient = [last_sums(*sums)]
        middle = next_hop(near, spread)
        sums = first_sums(partials, sent[1], orders[1][0])
        sums, middle = lax.optimization_barrier((sums, middle))
        gradient.append(last_sums(*sums))
        far = next_hop(middle, spread)
        downs, ups = zip(near, middle, far)
        rights = [right_dealt, *downs, *ups]
    else:
        gradient = [
            last_sums(*first_sums(partials, part, mine)) for part, (mine, _) in zip(sent, orders)
        ]
        rights = [lax.all_gather(right_dealt, "shard", axis=0)]
    gradient = [lax.optimization_barrier(part) for part in gradient]
    grad_blocks = [lax.all_gather(part, "shard", axis=0) for part in gradient]
    left_dealt = deal(reorder(left_root, order))
    weights_dealt = deal(reorder(weights, order))
    tiles = jnp.concatenate(gradient, axis=0).reshape(per, rows, group, cols)
    tiles = deal(jnp.transpose(tiles, (2, 0, 1, 3)))

    if early:
        grad_blocks[0], left_dealt, weights_dealt, tiles = lax.optimization_barrier(
            (grad_blocks[0], left_dealt, weights_dealt, tiles)
        )
        slabs = grams(grad_blocks[0], jnp.arange(early, dtype=jnp.int32))
        slabs, left_dealt, tiles = lax.optimization_barrier((slabs, left_dealt, tiles))
        received = lax.all_to_all(slabs, GROUP, split_axis=0, concat_axis=0, tiled=True)
    adam_m_new, adam_v_new, adam_total = adam(
        tiles.reshape(blocks, rows, cols), place, adam_m, adam_v
    )
    pieces = [precondition(left_dealt, 0, grad_blocks[0], rights)]
    if early:
        grad_blocks[1], adam_total, pieces[0] = lax.optimization_barrier(
            (grad_blocks[1], adam_total, pieces[0])
        )
        pieces.append(precondition(left_dealt, early, grad_blocks[1], rights))
    entry = jnp.where(is_heavy, early, own_entry) - early
    last_slabs = grams(grad_blocks[-1], jnp.clip(entry, 0, per - 1 - early).reshape(1))
    precond_total = jnp.concatenate([total for _, total in pieces], axis=0)

    matrix_range = jnp.arange(MATS, dtype=jnp.int32)
    onehot = (block_matrix[:, None] == matrix_range[None, :]).astype(jnp.float32)
    own_order = lax.dynamic_slice_in_dim(order, group_index * per, per)
    own_onehot = jnp.sum(
        jnp.where((own_order[:, None] == ids[None, :])[:, :, None], onehot[None, :, :], 0.0), axis=1
    )
    adam_part = jnp.sum(jnp.sum(adam_total, axis=(1, 2))[:, None] * onehot, axis=0)
    shampoo_part = jnp.sum(jnp.sum(precond_total, axis=(1, 2))[:, None] * own_onehot, axis=0)
    parts = jnp.pad(jnp.stack([adam_part, shampoo_part]), ((0, 6), (0, LANES - MATS)))
    if early:
        received, last_slabs, parts = lax.optimization_barrier((received, last_slabs, parts))
    devices = owner_count * group
    parts = lax.all_to_all(
        jnp.broadcast_to(parts[None], (devices,) + parts.shape), ALL, 0, 0, tiled=True
    )
    adam_norm, shampoo_norm = jnp.sum(parts, axis=0)[:2, :MATS]
    counts = jnp.sum(onehot, axis=0) * float(size * size)
    graft_scale = jnp.sqrt(adam_norm / (shampoo_norm + FLOOR_RATE * counts))
    block_scale = jnp.sum(own_onehot * graft_scale[None, :], axis=1)

    last = lax.all_to_all(last_slabs, GROUP, split_axis=0, concat_axis=0, tiled=True)
    updated = [
        update(weights_dealt, a, piece, block_scale[a:b])
        for (a, b), (piece, _) in zip(cuts, pieces)
    ]
    if len(updated) == 1:
        updated = [updated[0][: per // 2], updated[0][per // 2 :]]
    stats = ()
    if early:
        ranks = jnp.arange(early * group, dtype=jnp.int32)
        base = jnp.where(is_heavy, 0, capacity - early * group)
        filled = jnp.where(is_heavy, 1, 0) * jnp.ones_like(ranks)
        stats = refresh(
            left_stat, right_stat, received, base, ranks % group, ranks // group, filled, stats
        )
    base = jnp.where(is_heavy, early * group, 0)
    ranks = base + jnp.arange(capacity - early * group, dtype=jnp.int32)
    filled = (ranks < held).astype(jnp.int32)
    source = (first + ranks) % group
    nothing = jnp.zeros_like(ranks)
    finish = lambda earlier: refresh(
        left_stat, right_stat, last, base, source, nothing, filled, earlier
    )
    new_weights, (left_new, right_new) = gather_blocks(*updated, by_entry, stats, finish)

    factor_m_new, factor_v_new, factor_step = adam_direction(
        factor_grad.astype(jnp.float32), factor_m, factor_v
    )
    factors_new = factors - LEARNING * (factor_step + DECAY_RATE * factors)
    return (
        new_weights,
        adam_m_new,
        adam_v_new,
        left_new,
        right_new,
        factors_new,
        factor_m_new,
        factor_v_new,
    )


def solution(mesh):
    tile = P(None, "shard", GROUP)
    stat = P("shard", None, GROUP)
    factor = P("shard", GROUP)
    in_specs = (P(GROUP, None, "shard", None), tile, tile, tile, stat, stat, tile, tile, P(), P())
    out_specs = (P(None, "shard", None), tile, tile, stat, stat)
    return jax.shard_map(
        shards,
        mesh=mesh,
        in_specs=in_specs + (factor,) * 4,
        out_specs=out_specs + (factor,) * 3,
        check_vma=False,
    )
```

```python
import functools

import jax
import jax.numpy as jnp
from jax import lax
from jax.experimental import pallas as pl
from jax.experimental.pallas import tpu as pltpu
from jax.sharding import PartitionSpec as P

MATS = 5

BETA_ONE = 0.9
BETA_TWO = 0.95
BETA_STAT = 0.95
LEARNING = 0.1
DECAY_RATE = 0.1
EPSILON = 1e-08
FLOOR_RATE = 1e-06
CORRECT_ONE = 1.0 - 0.9**10
CORRECT_TWO = 1.0 - 0.95**10

GROUP = ("tensor", "section")
ALL = ("shard", "tensor", "section")
VMEM_LIMIT = 48 * 1024 * 1024
LANES = 128
SMALL = pl.CostEstimate(flops=0, bytes_accessed=0, transcendentals=0)


def params():
    return pltpu.CompilerParams(vmem_limit_bytes=VMEM_LIMIT)


def adam_direction(grad_float, moment, second):
    moment_new = BETA_ONE * moment + (1.0 - BETA_ONE) * grad_float
    second_new = BETA_TWO * second + (1.0 - BETA_TWO) * grad_float * grad_float
    direction = moment_new / CORRECT_ONE / (jnp.sqrt(second_new / CORRECT_TWO) + EPSILON)
    return (moment_new, second_new, direction)


def copy_blocks(pairs, held, arrived, left):
    into = [
        pltpu.make_async_copy(source, held.at[i], arrived.at[i])
        for i, (source, _) in enumerate(pairs)
    ]
    out_of = [
        pltpu.make_async_copy(held.at[i], target, left.at[i]) for i, (_, target) in enumerate(pairs)
    ]
    for copy in into:
        copy.start()
    for arrival, copy in zip(into, out_of):
        arrival.wait()
        copy.start()
    for copy in out_of:
        copy.wait()


def copy_scratch(count, tile, kind):
    return [
        pltpu.VMEM((count,) + tile, kind),
        pltpu.SemaphoreType.DMA((count,)),
        pltpu.SemaphoreType.DMA((count,)),
    ]


def reorder_kernel(order, blocks, out, held, arrived, left):
    pairs = [(blocks.at[order[i]], out.at[i]) for i in range(out.shape[0])]
    copy_blocks(pairs, held, arrived, left)


def reorder(blocks, order):
    count, tile = order.shape[0], blocks.shape[1:]
    return pl.pallas_call(
        reorder_kernel,
        grid_spec=pltpu.PrefetchScalarGridSpec(
            num_scalar_prefetch=1,
            grid=(1,),
            in_specs=[pl.BlockSpec(memory_space=pl.ANY)],
            out_specs=pl.BlockSpec(memory_space=pl.ANY),
            scratch_shapes=copy_scratch(count, tile, blocks.dtype),
        ),
        out_shape=jax.ShapeDtypeStruct((count,) + tile, blocks.dtype),
        compiler_params=params(),
        cost_estimate=SMALL,
    )(order, blocks)


def place_kernel(sources, target, *refs):
    out, held, arrived, left = refs[-4:]
    blocks = [ref.at[i] for ref in refs[:sources] for i in range(ref.shape[0])]
    pairs = [(block, out.at[target[i]]) for i, block in enumerate(blocks)]
    copy_blocks(pairs, held, arrived, left)


def place_blocks(arrays, target, total, earlier):
    tile, kind = arrays[0].shape[1:], arrays[0].dtype
    inputs = list(arrays) + list(earlier)
    return pl.pallas_call(
        functools.partial(place_kernel, len(arrays)),
        grid_spec=pltpu.PrefetchScalarGridSpec(
            num_scalar_prefetch=1,
            grid=(1,),
            in_specs=[pl.BlockSpec(memory_space=pl.ANY)] * len(inputs),
            out_specs=pl.BlockSpec(memory_space=pl.ANY),
            scratch_shapes=copy_scratch(target.shape[0], tile, kind),
        ),
        out_shape=jax.ShapeDtypeStruct((total,) + tile, kind),
        input_output_aliases={1 + len(arrays) + i: i for i in range(len(earlier))},
        compiler_params=params(),
        cost_estimate=SMALL,
    )(target, *inputs)


def adam_kernel(place, grad, moment, second, moment_out, second_out, total):
    moment_new, second_new, direction = adam_direction(
        grad[0].astype(jnp.float32), moment[0], second[0]
    )
    moment_out[0] = moment_new
    second_out[0] = second_new
    total[0] = jnp.sum(direction * direction, axis=0, keepdims=True)


def adam(grad_tiles, place, moment, second):
    count, rows, cols = moment.shape
    own = pl.BlockSpec((1, rows, cols), lambda i, place: (i, 0, 0))
    return pl.pallas_call(
        adam_kernel,
        grid_spec=pltpu.PrefetchScalarGridSpec(
            num_scalar_prefetch=1,
            grid=(count,),
            in_specs=[
                pl.BlockSpec((1, rows, cols), lambda i, place: (place[i], 0, 0)),
                own,
                own,
            ],
            out_specs=[own, own, pl.BlockSpec((1, 1, cols), lambda i, place: (i, 0, 0))],
        ),
        out_shape=[
            jax.ShapeDtypeStruct(moment.shape, jnp.float32),
            jax.ShapeDtypeStruct(moment.shape, jnp.float32),
            jax.ShapeDtypeStruct((count, 1, cols), jnp.float32),
        ],
        compiler_params=params(),
        cost_estimate=SMALL,
    )(place, grad_tiles, moment, second)


def gram_kernel(chosen, grad, out):
    parts, _, rows, width = grad.shape
    size = parts * rows
    whole = grad[:, 0].reshape(size, width)
    turned = whole.T
    step = 2 * LANES
    for start in range(0, size, step):
        left = lax.dot_general(
            whole,
            whole[start : start + step, :],
            (((1,), (1,)), ((), ())),
            preferred_element_type=jnp.float32,
        ).astype(jnp.bfloat16)
        right = lax.dot_general(
            turned,
            whole[:, start : start + step],
            (((1,), (0,)), ((), ())),
            preferred_element_type=jnp.float32,
        ).astype(jnp.bfloat16)
        for half in range(2):
            slab = start // LANES + half
            out[slab, 0, 0] = left[:, half * LANES : (half + 1) * LANES]
            out[slab, 0, 1] = right[:, half * LANES : (half + 1) * LANES]


def grams(grad_blocks, chosen):
    shards, per, rows, width = grad_blocks.shape
    size = shards * rows
    slabs = size // LANES
    count = chosen.shape[0]
    return pl.pallas_call(
        gram_kernel,
        grid_spec=pltpu.PrefetchScalarGridSpec(
            num_scalar_prefetch=1,
            grid=(count,),
            in_specs=[
                pl.BlockSpec((shards, 1, rows, width), lambda j, chosen: (0, chosen[j], 0, 0))
            ],
            out_specs=pl.BlockSpec(
                (slabs, 1, 2, size, LANES), lambda j, chosen: (0, j, 0, 0, 0)
            ),
        ),
        out_shape=jax.ShapeDtypeStruct((slabs, count, 2, size, LANES), jnp.bfloat16),
        compiler_params=params(),
        cost_estimate=SMALL,
    )(chosen, grad_blocks)


def stat_kernel(
    base, source, entry, filled, left_stat, right_stat, left_gram, right_gram, *refs
):
    left_out, right_out = refs[-2:]
    full = filled[pl.program_id(0)] > 0
    left = left_gram[0, 0, 0].astype(jnp.float32)
    right = right_gram[0, 0, 0].astype(jnp.float32)
    left_out[0] = BETA_STAT * left_stat[0] + jnp.where(full, (1.0 - BETA_STAT) * left, 0.0)
    right_out[0] = BETA_STAT * right_stat[0] + jnp.where(full, (1.0 - BETA_STAT) * right, 0.0)


def refresh(left_stat, right_stat, received, base, source, entry, filled, earlier):
    slots, size, cols = left_stat.shape
    count = source.shape[0]
    own = pl.BlockSpec((1, size, cols), lambda r, base, source, entry, filled: (base[0] + r, 0, 0))
    gram = (1, 1, 1, size, cols)
    shape = jax.ShapeDtypeStruct(left_stat.shape, jnp.float32)
    return pl.pallas_call(
        stat_kernel,
        grid_spec=pltpu.PrefetchScalarGridSpec(
            num_scalar_prefetch=4,
            grid=(count,),
            in_specs=[
                own,
                own,
                pl.BlockSpec(
                    gram, lambda r, base, source, entry, filled: (source[r], entry[r], 0, 0, 0)
                ),
                pl.BlockSpec(
                    gram, lambda r, base, source, entry, filled: (source[r], entry[r], 1, 0, 0)
                ),
            ]
            + [pl.BlockSpec(memory_space=pl.ANY)] * len(earlier),
            out_specs=[own, own],
        ),
        out_shape=[shape, shape],
        input_output_aliases={8 + i: i for i in range(len(earlier))},
        compiler_params=params(),
        cost_estimate=SMALL,
    )(
        base.reshape(1), source, entry, filled, left_stat, right_stat, received, received, *earlier
    )


def left_product(left, grad):
    slabs, _, rows, _ = left.shape
    left_rows = jnp.concatenate([left[s, 0] for s in range(slabs)], axis=1)
    whole = grad[:, 0].reshape(grad.shape[0] * rows, grad.shape[3])
    return jnp.dot(left_rows, whole, preferred_element_type=jnp.float32).astype(jnp.bfloat16)


def precond_kernel(left, grad, right, out, total):
    slabs, _, rows, cols = left.shape
    parts = grad.shape[0]
    mixed = left_product(left, grad)
    total[...] = jnp.zeros_like(total)
    step = 2
    for start in range(0, slabs, step):
        columns = jnp.concatenate(
            [right[:, s, 0].reshape(parts * rows, cols) for s in range(start, start + step)], axis=1
        )
        piece = jnp.dot(mixed, columns, preferred_element_type=jnp.float32)
        out[0, :, start * cols : (start + step) * cols] = piece.astype(jnp.bfloat16)
        square = jnp.sum(piece * piece, axis=0, keepdims=True)
        total[0] += square[:, :cols] + square[:, cols:]


def tile_sources(mine, count, spread):
    found = {(mine, b): (0, spread * b) for b in range(count)}
    for hop in range(1, count):
        for i in range(count - hop):
            if mine + hop < count:
                found[mine + hop, (mine + hop + i) % count] = (hop, spread * i)
            if mine - hop >= 0:
                found[mine - hop, (mine - hop - i) % count] = (count - 1 + hop, spread * i)
    return found


def precond_tiles_kernel(me, left, grad, *refs):
    rights, out, total = refs[:-2], refs[-2], refs[-1]
    slabs, _, rows, cols = left.shape
    parts = grad.shape[0]
    spread = slabs // parts
    mixed = left_product(left, grad)
    total[...] = jnp.zeros_like(total)
    for mine in range(parts):

        @pl.when(me[0] == mine)
        def _(mine=mine):
            found = tile_sources(mine, parts, spread)
            for b in range(parts):
                piece = jnp.zeros((rows, spread * cols), jnp.float32)
                for a in range(parts):
                    turned = (a, b) not in found
                    array, first = found[(b, a) if turned else (a, b)]
                    tile = jnp.concatenate(
                        [rights[array][first + s, 0] for s in range(spread)], axis=1
                    )
                    piece += lax.dot_general(
                        mixed[:, a * rows : (a + 1) * rows],
                        tile,
                        (((1,), (1 if turned else 0,)), ((), ())),
                        preferred_element_type=jnp.float32,
                    )
                out[0, :, b * rows : (b + 1) * rows] = piece.astype(jnp.bfloat16)
                square = jnp.sum(piece * piece, axis=0, keepdims=True)
                total[0] += sum(square[:, s * cols : (s + 1) * cols] for s in range(spread))


def first_hop(right):
    slabs, per, rows, cols = right.shape
    count, me = lax.axis_size("shard"), lax.axis_index("shard")
    spread = slabs // count
    lane = jnp.arange(spread * (count - 1), dtype=jnp.int32)
    moved = []
    for sign in (1, -1):
        tiles = (me + sign * (lane // spread)) % count
        picked = reorder(right.reshape(slabs, per * rows, cols), tiles * spread + lane % spread)
        moved.append(picked.reshape(lane.shape[0], per, rows, cols))
    return hop(moved)


def hop(moved):
    count = lax.axis_size("shard")
    down = [(a, a - 1) for a in range(1, count)]
    up = [(a, a + 1) for a in range(count - 1)]
    return lax.ppermute(moved[0], "shard", down), lax.ppermute(moved[1], "shard", up)


def next_hop(moved, spread):
    return hop([part[: part.shape[0] - spread] for part in moved])


def precondition(left, start, grad_blocks, rights):
    shards, count, rows, width = grad_blocks.shape
    slabs, _, _, cols = left.shape
    size = shards * rows
    whole = len(rights) == 1
    if whole:
        right_specs = [pl.BlockSpec((shards, slabs, 1, rows, cols), lambda m, me: (0, 0, start + m, 0, 0))]
    else:
        right_specs = [
            pl.BlockSpec((right.shape[0], 1, rows, cols), lambda m, me: (0, start + m, 0, 0))
            for right in rights
        ]
    body = precond_tiles_kernel
    if whole:
        body = lambda me, *refs: precond_kernel(*refs)
    return pl.pallas_call(
        body,
        grid_spec=pltpu.PrefetchScalarGridSpec(
            num_scalar_prefetch=1,
            grid=(count,),
            in_specs=[
                pl.BlockSpec((slabs, 1, rows, cols), lambda m, me: (0, start + m, 0, 0)),
                pl.BlockSpec((shards, 1, rows, width), lambda m, me: (0, m, 0, 0)),
            ]
            + right_specs,
            out_specs=[
                pl.BlockSpec((1, rows, width), lambda m, me: (m, 0, 0)),
                pl.BlockSpec((1, 1, cols), lambda m, me: (m, 0, 0)),
            ],
        ),
        out_shape=[
            jax.ShapeDtypeStruct((count, rows, width), jnp.bfloat16),
            jax.ShapeDtypeStruct((count, 1, cols), jnp.float32),
        ],
        compiler_params=params(),
        cost_estimate=SMALL,
    )(lax.axis_index("shard").reshape(1), left, grad_blocks, *rights)


def update_kernel(scale, weights, precond, out):
    slabs = weights.shape[0]
    factor = scale[pl.program_id(0)]
    old = jnp.concatenate([weights[s, 0] for s in range(slabs)], axis=1).astype(jnp.float32)
    step = factor * precond[0].astype(jnp.float32) + DECAY_RATE * old
    out[0] = (old - LEARNING * step).astype(jnp.bfloat16)


def update(weights, start, precond, scale):
    slabs, _, rows, cols = weights.shape
    count = precond.shape[0]
    width = slabs * cols
    own = pl.BlockSpec((1, rows, width), lambda m, scale: (m, 0, 0))
    return pl.pallas_call(
        update_kernel,
        grid_spec=pltpu.PrefetchScalarGridSpec(
            num_scalar_prefetch=1,
            grid=(count,),
            in_specs=[
                pl.BlockSpec((slabs, 1, rows, cols), lambda m, scale: (0, start + m, 0, 0)),
                own,
            ],
            out_specs=own,
        ),
        out_shape=jax.ShapeDtypeStruct((count, rows, width), jnp.bfloat16),
        compiler_params=params(),
        cost_estimate=SMALL,
    )(scale, weights, precond)


def pair_kernel(picked, first, second, third, fourth, received, send_a, keep_a, send_b, keep_b):
    half = first.shape[1] // 2
    added = [
        (own[0].astype(jnp.float32) + received[u].astype(jnp.float32)).astype(jnp.bfloat16)
        for u, own in enumerate((first, second, third, fourth))
    ]
    for ref, chosen, start in (
        (send_a, (1, 3), 0),
        (keep_a, (0, 2), 0),
        (send_b, (2, 3), half),
        (keep_b, (0, 1), half),
    ):
        for i, u in enumerate(chosen):
            ref[i, 0] = added[u][start : start + half]


def add_pair(partials, received, picked):
    _, rows, width = partials.shape
    count = received.shape[0] // 4
    half = jax.ShapeDtypeStruct((2, count, rows // 2, width), partials.dtype)

    def own(u):
        return pl.BlockSpec((1, rows, width), lambda i, picked: (picked[4 * i + u], 0, 0))

    return pl.pallas_call(
        pair_kernel,
        grid_spec=pltpu.PrefetchScalarGridSpec(
            num_scalar_prefetch=1,
            grid=(count,),
            in_specs=[own(0), own(1), own(2), own(3)]
            + [pl.BlockSpec((4, rows, width), lambda i, picked: (i, 0, 0))],
            out_specs=[pl.BlockSpec((2, 1, rows // 2, width), lambda i, picked: (0, i, 0, 0))] * 4,
        ),
        out_shape=[half] * 4,
        compiler_params=params(),
        cost_estimate=SMALL,
    )(picked, partials, partials, partials, partials, received)


def add(one, two):
    return (one.astype(jnp.float32) + two.astype(jnp.float32)).astype(jnp.bfloat16)


def swap(array, bit):
    devices = lax.axis_size("tensor")
    return lax.ppermute(array, "tensor", [(t, t ^ bit) for t in range(devices)])


def swap_core(array):
    return lax.ppermute(array, "section", [(0, 1), (1, 0)])


def pick(picked):
    core = lax.axis_index("section")
    relative = jnp.arange(4, dtype=jnp.int32) ^ lax.axis_index("tensor")
    mine = jnp.take(picked, relative * 2 + core, axis=0).T.reshape(-1)
    other = jnp.take(picked, relative * 2 + 1 - core, axis=0).T.reshape(-1)
    return mine, other


def pair_sums(partials, sent, mine):
    return add_pair(partials, swap_core(sent), mine)


def first_sums(send_a, keep_a, send_b, keep_b):
    return add(keep_a, swap(send_a, 1)), add(keep_b, swap(send_b, 2))


def last_sums(sum_a, sum_b):
    last_a = add(sum_a[0], swap(sum_a[1], 2))
    last_b = add(sum_b[0], swap(sum_b[1], 1))
    return jnp.concatenate([last_a, last_b], axis=1)


def gather_blocks(first, second, by_entry, early_work, finish):
    total = by_entry.size
    cut = first.shape[0]
    tensor, core = lax.axis_index("tensor"), lax.axis_index("section")
    x_first, y_second = swap(first, 1), swap(second, 2)
    y_first, x_second = swap(first, 2), swap(second, 1)
    x_first, y_second, early_work = lax.optimization_barrier((x_first, y_second, early_work))
    d_first, d_second = swap(x_first, 2), swap(y_second, 1)

    def targets(bits, core):
        places = [by_entry[(tensor ^ bit) * 2 + core] for bit in bits]
        return [piece for place in places for piece in (place[:cut], place[cut:])]

    near = [first, second, x_first, x_second, y_first, y_second]
    near_target = targets((0, 1, 2), core) + targets((0, 1, 2), 1 - core)
    near = near + [swap_core(piece) for piece in near]
    placed = place_blocks(near, jnp.concatenate(near_target), total, [])
    late_work = finish(early_work)
    d_first, d_second, placed, late_work = lax.optimization_barrier(
        (d_first, d_second, placed, late_work)
    )
    far = [d_first, d_second]
    far_target = targets((3,), core) + targets((3,), 1 - core)
    far = far + [swap_core(piece) for piece in far]
    return place_blocks(far, jnp.concatenate(far_target), total, [placed]), late_work


def shards(
    grad_parts,
    weights,
    adam_m,
    adam_v,
    left_stat,
    right_stat,
    left_root,
    right_root,
    block_owner,
    block_matrix,
    factors,
    factor_grad,
    factor_m,
    factor_v,
):
    capacity = left_stat.shape[0]
    blocks, rows, cols = weights.shape
    size = left_stat.shape[1]
    group = size // cols
    per = blocks // group
    sends = -(-capacity // group)
    owner_index = lax.axis_index("shard")
    group_index = lax.axis_index(GROUP)
    owner_count = lax.axis_size("shard")

    ids = jnp.arange(blocks, dtype=jnp.int32)
    owners = jnp.arange(owner_count, dtype=jnp.int32)
    loads = jnp.sum((block_owner[None, :] == owners[:, None]).astype(jnp.int32), axis=1)
    heavy = jnp.min(jnp.where(loads == jnp.max(loads), owners, owner_count))
    turn = (block_owner - heavy) % owner_count
    own_turn = (owner_index - heavy) % owner_count
    before = (turn[None, :] < turn[:, None]) | (
        (turn[None, :] == turn[:, None]) & (ids[None, :] < ids[:, None])
    )
    position = jnp.sum(before.astype(jnp.int32), axis=1)
    place = (position % group) * per + position // group
    order = jnp.sum(jnp.where(place[None, :] == ids[:, None], ids[None, :], 0), axis=1)

    first = jnp.sum((turn < own_turn).astype(jnp.int32))
    held = jnp.sum((turn == own_turn).astype(jnp.int32))
    early = sends - 1 if blocks - capacity <= group else 0
    is_heavy = own_turn == 0
    own_entry = (first - group_index + group - 1) // group

    def deal(tiles):
        return lax.all_to_all(
            tiles.reshape(group, per, rows, cols), GROUP, split_axis=0, concat_axis=0, tiled=True
        )

    by_entry = order.reshape(group, per)
    partials = grad_parts[0]
    cuts = [(0, early), (early, per)] if early else [(0, per)]
    orders = [pick(by_entry[:, a:b]) for a, b in cuts]
    right_dealt = deal(reorder(right_root, order))
    sent = [reorder(partials, other) for _, other in orders]
    right_dealt, sent[-1] = lax.optimization_barrier((right_dealt, sent[-1]))
    if early and owner_count == 4 and rows * owner_count == size:
        spread = group // owner_count
        near = first_hop(right_dealt)
        sums = first_sums(*pair_sums(partials, sent[0], orders[0][0]))
        pairs = pair_sums(partials, sent[1], orders[1][0])
        sums, near, pairs = lax.optimization_barrier((sums, near, pairs))
        gradient = [last_sums(*sums)]
        middle = next_hop(near, spread)
        sums = first_sums(*pairs)
        sums, middle = lax.optimization_barrier((sums, middle))
        gradient.append(last_sums(*sums))
        far = next_hop(middle, spread)
        downs, ups = zip(near, middle, far)
        rights = [right_dealt, *downs, *ups]
    else:
        gradient = [
            last_sums(*first_sums(*pair_sums(partials, part, mine)))
            for part, (mine, _) in zip(sent, orders)
        ]
        rights = [lax.all_gather(right_dealt, "shard", axis=0)]
    gradient = [lax.optimization_barrier(part) for part in gradient]
    grad_blocks = [lax.all_gather(part, "shard", axis=0) for part in gradient]
    left_dealt = deal(reorder(left_root, order))
    weights_dealt = deal(reorder(weights, order))
    tiles = jnp.concatenate(gradient, axis=0).reshape(per, rows, group, cols)
    tiles = jnp.transpose(tiles, (2, 0, 1, 3)).reshape(group, per * rows, cols)
    partners = jnp.arange(group, dtype=jnp.int32) ^ group_index
    tiles = reorder(tiles, partners)
    tiles = jnp.concatenate(
        [tiles[:1]]
        + [
            lax.ppermute(tiles[k : k + 1], GROUP, [(g, g ^ k) for g in range(group)])
            for k in range(1, group)
        ]
    )
    tile_place = ((place // per) ^ group_index) * per + place % per

    if early:
        grad_blocks[0], left_dealt, weights_dealt = lax.optimization_barrier(
            (grad_blocks[0], left_dealt, weights_dealt)
        )
        slabs = grams(grad_blocks[0], jnp.arange(early, dtype=jnp.int32))
        slabs, left_dealt, tile_place = lax.optimization_barrier((slabs, left_dealt, tile_place))
        received = lax.all_to_all(slabs, GROUP, split_axis=0, concat_axis=0, tiled=True)
    adam_m_new, adam_v_new, adam_total = adam(
        tiles.reshape(blocks, rows, cols), tile_place, adam_m, adam_v
    )
    pieces = [precondition(left_dealt, 0, grad_blocks[0], rights)]
    if early:
        grad_blocks[1], adam_total, pieces[0] = lax.optimization_barrier(
            (grad_blocks[1], adam_total, pieces[0])
        )
        pieces.append(precondition(left_dealt, early, grad_blocks[1], rights))
    entry = jnp.where(is_heavy, early, own_entry) - early
    last_slabs = grams(grad_blocks[-1], jnp.clip(entry, 0, per - 1 - early).reshape(1))
    precond_total = jnp.concatenate([total for _, total in pieces], axis=0)

    matrix_range = jnp.arange(MATS, dtype=jnp.int32)
    onehot = (block_matrix[:, None] == matrix_range[None, :]).astype(jnp.float32)
    own_order = lax.dynamic_slice_in_dim(order, group_index * per, per)
    own_onehot = jnp.sum(
        jnp.where((own_order[:, None] == ids[None, :])[:, :, None], onehot[None, :, :], 0.0), axis=1
    )
    adam_part = jnp.sum(jnp.sum(adam_total, axis=(1, 2))[:, None] * onehot, axis=0)
    shampoo_part = jnp.sum(jnp.sum(precond_total, axis=(1, 2))[:, None] * own_onehot, axis=0)
    parts = jnp.pad(jnp.stack([adam_part, shampoo_part]), ((0, 6), (0, LANES - MATS)))
    if early:
        received, last_slabs, parts = lax.optimization_barrier((received, last_slabs, parts))
    devices = owner_count * group
    parts = lax.all_to_all(
        jnp.broadcast_to(parts[None], (devices,) + parts.shape), ALL, 0, 0, tiled=True
    )
    adam_norm, shampoo_norm = jnp.sum(parts, axis=0)[:2, :MATS]
    counts = jnp.sum(onehot, axis=0) * float(size * size)
    graft_scale = jnp.sqrt(adam_norm / (shampoo_norm + FLOOR_RATE * counts))
    block_scale = jnp.sum(own_onehot * graft_scale[None, :], axis=1)

    last = lax.all_to_all(last_slabs, GROUP, split_axis=0, concat_axis=0, tiled=True)
    updated = [
        update(weights_dealt, a, piece, block_scale[a:b])
        for (a, b), (piece, _) in zip(cuts, pieces)
    ]
    if len(updated) == 1:
        updated = [updated[0][: per // 2], updated[0][per // 2 :]]
    stats = ()
    if early:
        ranks = jnp.arange(early * group, dtype=jnp.int32)
        base = jnp.where(is_heavy, 0, capacity - early * group)
        filled = jnp.where(is_heavy, 1, 0) * jnp.ones_like(ranks)
        stats = refresh(
            left_stat, right_stat, received, base, ranks % group, ranks // group, filled, stats
        )
    base = jnp.where(is_heavy, early * group, 0)
    ranks = base + jnp.arange(capacity - early * group, dtype=jnp.int32)
    filled = (ranks < held).astype(jnp.int32)
    source = (first + ranks) % group
    nothing = jnp.zeros_like(ranks)
    finish = lambda earlier: refresh(
        left_stat, right_stat, last, base, source, nothing, filled, earlier
    )
    new_weights, (left_new, right_new) = gather_blocks(*updated, by_entry, stats, finish)

    factor_m_new, factor_v_new, factor_step = adam_direction(
        factor_grad.astype(jnp.float32), factor_m, factor_v
    )
    factors_new = factors - LEARNING * (factor_step + DECAY_RATE * factors)
    return (
        new_weights,
        adam_m_new,
        adam_v_new,
        left_new,
        right_new,
        factors_new,
        factor_m_new,
        factor_v_new,
    )


def solution(mesh):
    tile = P(None, "shard", GROUP)
    stat = P("shard", None, GROUP)
    factor = P("shard", GROUP)
    in_specs = (P(GROUP, None, "shard", None), tile, tile, tile, stat, stat, tile, tile, P(), P())
    out_specs = (P(None, "shard", None), tile, tile, stat, stat)
    return jax.shard_map(
        shards,
        mesh=mesh,
        in_specs=in_specs + (factor,) * 4,
        out_specs=out_specs + (factor,) * 3,
        check_vma=False,
    )
```

```python
import functools

import jax
import jax.numpy as jnp
from jax import lax
from jax.experimental import pallas as pl
from jax.experimental.pallas import tpu as pltpu
from jax.sharding import PartitionSpec as P

MATS = 5

BETA_ONE = 0.9
BETA_TWO = 0.95
BETA_STAT = 0.95
LEARNING = 0.1
DECAY_RATE = 0.1
EPSILON = 1e-08
FLOOR_RATE = 1e-06
CORRECT_ONE = 1.0 - 0.9**10
CORRECT_TWO = 1.0 - 0.95**10

GROUP = ("tensor", "section")
ALL = ("shard", "tensor", "section")
VMEM_LIMIT = 48 * 1024 * 1024
LANES = 128
SMALL = pl.CostEstimate(flops=0, bytes_accessed=0, transcendentals=0)


def params():
    return pltpu.CompilerParams(vmem_limit_bytes=VMEM_LIMIT)


def adam_direction(grad_float, moment, second):
    moment_new = BETA_ONE * moment + (1.0 - BETA_ONE) * grad_float
    second_new = BETA_TWO * second + (1.0 - BETA_TWO) * grad_float * grad_float
    direction = moment_new / CORRECT_ONE / (jnp.sqrt(second_new / CORRECT_TWO) + EPSILON)
    return (moment_new, second_new, direction)


def copy_blocks(pairs, held, arrived, left):
    into = [
        pltpu.make_async_copy(source, held.at[i], arrived.at[i])
        for i, (source, _) in enumerate(pairs)
    ]
    out_of = [
        pltpu.make_async_copy(held.at[i], target, left.at[i]) for i, (_, target) in enumerate(pairs)
    ]
    for copy in into:
        copy.start()
    for arrival, copy in zip(into, out_of):
        arrival.wait()
        copy.start()
    for copy in out_of:
        copy.wait()


def copy_scratch(count, tile, kind):
    return [
        pltpu.VMEM((count,) + tile, kind),
        pltpu.SemaphoreType.DMA((count,)),
        pltpu.SemaphoreType.DMA((count,)),
    ]


def reorder_kernel(order, blocks, out, held, arrived, left):
    pairs = [(blocks.at[order[i]], out.at[i]) for i in range(out.shape[0])]
    copy_blocks(pairs, held, arrived, left)


def reorder(blocks, order):
    count, tile = order.shape[0], blocks.shape[1:]
    return pl.pallas_call(
        reorder_kernel,
        grid_spec=pltpu.PrefetchScalarGridSpec(
            num_scalar_prefetch=1,
            grid=(1,),
            in_specs=[pl.BlockSpec(memory_space=pl.ANY)],
            out_specs=pl.BlockSpec(memory_space=pl.ANY),
            scratch_shapes=copy_scratch(count, tile, blocks.dtype),
        ),
        out_shape=jax.ShapeDtypeStruct((count,) + tile, blocks.dtype),
        compiler_params=params(),
        cost_estimate=SMALL,
    )(order, blocks)


def place_kernel(sources, target, *refs):
    out, held, arrived, left = refs[-4:]
    blocks = [ref.at[i] for ref in refs[:sources] for i in range(ref.shape[0])]
    pairs = [(block, out.at[target[i]]) for i, block in enumerate(blocks)]
    copy_blocks(pairs, held, arrived, left)


def place_blocks(arrays, target, total, earlier):
    tile, kind = arrays[0].shape[1:], arrays[0].dtype
    inputs = list(arrays) + list(earlier)
    return pl.pallas_call(
        functools.partial(place_kernel, len(arrays)),
        grid_spec=pltpu.PrefetchScalarGridSpec(
            num_scalar_prefetch=1,
            grid=(1,),
            in_specs=[pl.BlockSpec(memory_space=pl.ANY)] * len(inputs),
            out_specs=pl.BlockSpec(memory_space=pl.ANY),
            scratch_shapes=copy_scratch(target.shape[0], tile, kind),
        ),
        out_shape=jax.ShapeDtypeStruct((total,) + tile, kind),
        input_output_aliases={1 + len(arrays) + i: i for i in range(len(earlier))},
        compiler_params=params(),
        cost_estimate=SMALL,
    )(target, *inputs)


def adam_kernel(place, grad, moment, second, moment_out, second_out, total):
    moment_new, second_new, direction = adam_direction(
        grad[0].astype(jnp.float32), moment[0], second[0]
    )
    moment_out[0] = moment_new
    second_out[0] = second_new
    total[0] = jnp.sum(direction * direction, axis=0, keepdims=True)


def adam(grad_tiles, place, moment, second):
    count, rows, cols = moment.shape
    own = pl.BlockSpec((1, rows, cols), lambda i, place: (i, 0, 0))
    return pl.pallas_call(
        adam_kernel,
        grid_spec=pltpu.PrefetchScalarGridSpec(
            num_scalar_prefetch=1,
            grid=(count,),
            in_specs=[
                pl.BlockSpec((1, rows, cols), lambda i, place: (place[i], 0, 0)),
                own,
                own,
            ],
            out_specs=[own, own, pl.BlockSpec((1, 1, cols), lambda i, place: (i, 0, 0))],
        ),
        out_shape=[
            jax.ShapeDtypeStruct(moment.shape, jnp.float32),
            jax.ShapeDtypeStruct(moment.shape, jnp.float32),
            jax.ShapeDtypeStruct((count, 1, cols), jnp.float32),
        ],
        compiler_params=params(),
        cost_estimate=SMALL,
    )(place, grad_tiles, moment, second)


def gram_kernel(chosen, grad, out):
    parts, _, rows, width = grad.shape
    size = parts * rows
    whole = grad[:, 0].reshape(size, width)
    turned = whole.T
    step = 2 * LANES
    for start in range(0, size, step):
        left = lax.dot_general(
            whole,
            whole[start : start + step, :],
            (((1,), (1,)), ((), ())),
            preferred_element_type=jnp.float32,
        ).astype(jnp.bfloat16)
        right = lax.dot_general(
            turned,
            whole[:, start : start + step],
            (((1,), (0,)), ((), ())),
            preferred_element_type=jnp.float32,
        ).astype(jnp.bfloat16)
        for half in range(2):
            slab = start // LANES + half
            out[slab, 0, 0] = left[:, half * LANES : (half + 1) * LANES]
            out[slab, 0, 1] = right[:, half * LANES : (half + 1) * LANES]


def grams(grad_blocks, chosen):
    shards, per, rows, width = grad_blocks.shape
    size = shards * rows
    slabs = size // LANES
    count = chosen.shape[0]
    return pl.pallas_call(
        gram_kernel,
        grid_spec=pltpu.PrefetchScalarGridSpec(
            num_scalar_prefetch=1,
            grid=(count,),
            in_specs=[
                pl.BlockSpec((shards, 1, rows, width), lambda j, chosen: (0, chosen[j], 0, 0))
            ],
            out_specs=pl.BlockSpec(
                (slabs, 1, 2, size, LANES), lambda j, chosen: (0, j, 0, 0, 0)
            ),
        ),
        out_shape=jax.ShapeDtypeStruct((slabs, count, 2, size, LANES), jnp.bfloat16),
        compiler_params=params(),
        cost_estimate=SMALL,
    )(chosen, grad_blocks)


def stat_kernel(
    base, source, entry, filled, left_stat, right_stat, left_gram, right_gram, *refs
):
    left_out, right_out = refs[-2:]
    full = filled[pl.program_id(0)] > 0
    left = left_gram[0, 0, 0].astype(jnp.float32)
    right = right_gram[0, 0, 0].astype(jnp.float32)
    left_out[0] = BETA_STAT * left_stat[0] + jnp.where(full, (1.0 - BETA_STAT) * left, 0.0)
    right_out[0] = BETA_STAT * right_stat[0] + jnp.where(full, (1.0 - BETA_STAT) * right, 0.0)


def refresh(left_stat, right_stat, received, base, source, entry, filled, earlier):
    slots, size, cols = left_stat.shape
    count = source.shape[0]
    own = pl.BlockSpec((1, size, cols), lambda r, base, source, entry, filled: (base[0] + r, 0, 0))
    gram = (1, 1, 1, size, cols)
    shape = jax.ShapeDtypeStruct(left_stat.shape, jnp.float32)
    return pl.pallas_call(
        stat_kernel,
        grid_spec=pltpu.PrefetchScalarGridSpec(
            num_scalar_prefetch=4,
            grid=(count,),
            in_specs=[
                own,
                own,
                pl.BlockSpec(
                    gram, lambda r, base, source, entry, filled: (source[r], entry[r], 0, 0, 0)
                ),
                pl.BlockSpec(
                    gram, lambda r, base, source, entry, filled: (source[r], entry[r], 1, 0, 0)
                ),
            ]
            + [pl.BlockSpec(memory_space=pl.ANY)] * len(earlier),
            out_specs=[own, own],
        ),
        out_shape=[shape, shape],
        input_output_aliases={8 + i: i for i in range(len(earlier))},
        compiler_params=params(),
        cost_estimate=SMALL,
    )(
        base.reshape(1), source, entry, filled, left_stat, right_stat, received, received, *earlier
    )


def left_product(left, grad):
    slabs, _, rows, _ = left.shape
    left_rows = jnp.concatenate([left[s, 0] for s in range(slabs)], axis=1)
    whole = grad[:, 0].reshape(grad.shape[0] * rows, grad.shape[3])
    return jnp.dot(left_rows, whole, preferred_element_type=jnp.float32).astype(jnp.bfloat16)


def precond_kernel(left, grad, right, out, total):
    slabs, _, rows, cols = left.shape
    parts = grad.shape[0]
    mixed = left_product(left, grad)
    total[...] = jnp.zeros_like(total)
    step = 2
    for start in range(0, slabs, step):
        columns = jnp.concatenate(
            [right[:, s, 0].reshape(parts * rows, cols) for s in range(start, start + step)], axis=1
        )
        piece = jnp.dot(mixed, columns, preferred_element_type=jnp.float32)
        out[0, :, start * cols : (start + step) * cols] = piece.astype(jnp.bfloat16)
        square = jnp.sum(piece * piece, axis=0, keepdims=True)
        total[0] += square[:, :cols] + square[:, cols:]


def tile_sources(mine, count, spread):
    found = {(mine, b): (0, spread * b) for b in range(count)}
    for hop in range(1, count):
        for i in range(count - hop):
            if mine + hop < count:
                found[mine + hop, (mine + hop + i) % count] = (hop, spread * i)
            if mine - hop >= 0:
                found[mine - hop, (mine - hop - i) % count] = (count - 1 + hop, spread * i)
    return found


def precond_tiles_kernel(me, left, grad, *refs):
    rights, out, total = refs[:-2], refs[-2], refs[-1]
    slabs, _, rows, cols = left.shape
    parts = grad.shape[0]
    spread = slabs // parts
    mixed = left_product(left, grad)
    total[...] = jnp.zeros_like(total)
    for mine in range(parts):

        @pl.when(me[0] == mine)
        def _(mine=mine):
            found = tile_sources(mine, parts, spread)
            for b in range(parts):
                piece = jnp.zeros((rows, spread * cols), jnp.float32)
                for a in range(parts):
                    turned = (a, b) not in found
                    array, first = found[(b, a) if turned else (a, b)]
                    tile = jnp.concatenate(
                        [rights[array][first + s, 0] for s in range(spread)], axis=1
                    )
                    piece += lax.dot_general(
                        mixed[:, a * rows : (a + 1) * rows],
                        tile,
                        (((1,), (1 if turned else 0,)), ((), ())),
                        preferred_element_type=jnp.float32,
                    )
                out[0, :, b * rows : (b + 1) * rows] = piece.astype(jnp.bfloat16)
                square = jnp.sum(piece * piece, axis=0, keepdims=True)
                total[0] += sum(square[:, s * cols : (s + 1) * cols] for s in range(spread))


def first_hop(right):
    slabs, per, rows, cols = right.shape
    count, me = lax.axis_size("shard"), lax.axis_index("shard")
    spread = slabs // count
    lane = jnp.arange(spread * (count - 1), dtype=jnp.int32)
    moved = []
    for sign in (1, -1):
        tiles = (me + sign * (lane // spread)) % count
        picked = reorder(right.reshape(slabs, per * rows, cols), tiles * spread + lane % spread)
        moved.append(picked.reshape(lane.shape[0], per, rows, cols))
    return hop(moved)


def hop(moved):
    count = lax.axis_size("shard")
    down = [(a, a - 1) for a in range(1, count)]
    up = [(a, a + 1) for a in range(count - 1)]
    return lax.ppermute(moved[0], "shard", down), lax.ppermute(moved[1], "shard", up)


def next_hop(moved, spread):
    return hop([part[: part.shape[0] - spread] for part in moved])


def precondition(left, start, grad_blocks, rights):
    shards, count, rows, width = grad_blocks.shape
    slabs, _, _, cols = left.shape
    size = shards * rows
    whole = len(rights) == 1
    if whole:
        right_specs = [pl.BlockSpec((shards, slabs, 1, rows, cols), lambda m, me: (0, 0, start + m, 0, 0))]
    else:
        right_specs = [
            pl.BlockSpec((right.shape[0], 1, rows, cols), lambda m, me: (0, start + m, 0, 0))
            for right in rights
        ]
    body = precond_tiles_kernel
    if whole:
        body = lambda me, *refs: precond_kernel(*refs)
    return pl.pallas_call(
        body,
        grid_spec=pltpu.PrefetchScalarGridSpec(
            num_scalar_prefetch=1,
            grid=(count,),
            in_specs=[
                pl.BlockSpec((slabs, 1, rows, cols), lambda m, me: (0, start + m, 0, 0)),
                pl.BlockSpec((shards, 1, rows, width), lambda m, me: (0, m, 0, 0)),
            ]
            + right_specs,
            out_specs=[
                pl.BlockSpec((1, rows, width), lambda m, me: (m, 0, 0)),
                pl.BlockSpec((1, 1, cols), lambda m, me: (m, 0, 0)),
            ],
        ),
        out_shape=[
            jax.ShapeDtypeStruct((count, rows, width), jnp.bfloat16),
            jax.ShapeDtypeStruct((count, 1, cols), jnp.float32),
        ],
        compiler_params=params(),
        cost_estimate=SMALL,
    )(lax.axis_index("shard").reshape(1), left, grad_blocks, *rights)


def update_kernel(scale, weights, precond, out):
    slabs = weights.shape[0]
    factor = scale[pl.program_id(0)]
    old = jnp.concatenate([weights[s, 0] for s in range(slabs)], axis=1).astype(jnp.float32)
    step = factor * precond[0].astype(jnp.float32) + DECAY_RATE * old
    out[0] = (old - LEARNING * step).astype(jnp.bfloat16)


def update(weights, start, precond, scale):
    slabs, _, rows, cols = weights.shape
    count = precond.shape[0]
    width = slabs * cols
    own = pl.BlockSpec((1, rows, width), lambda m, scale: (m, 0, 0))
    return pl.pallas_call(
        update_kernel,
        grid_spec=pltpu.PrefetchScalarGridSpec(
            num_scalar_prefetch=1,
            grid=(count,),
            in_specs=[
                pl.BlockSpec((slabs, 1, rows, cols), lambda m, scale: (0, start + m, 0, 0)),
                own,
            ],
            out_specs=own,
        ),
        out_shape=jax.ShapeDtypeStruct((count, rows, width), jnp.bfloat16),
        compiler_params=params(),
        cost_estimate=SMALL,
    )(scale, weights, precond)


def pair_kernel(picked, first, second, third, fourth, received, send_a, keep_a, send_b, keep_b):
    half = first.shape[1] // 2
    added = [
        (own[0].astype(jnp.float32) + received[u].astype(jnp.float32)).astype(jnp.bfloat16)
        for u, own in enumerate((first, second, third, fourth))
    ]
    for ref, chosen, start in (
        (send_a, (1, 3), 0),
        (keep_a, (0, 2), 0),
        (send_b, (2, 3), half),
        (keep_b, (0, 1), half),
    ):
        for i, u in enumerate(chosen):
            ref[i, 0] = added[u][start : start + half]


def add_pair(partials, received, picked):
    _, rows, width = partials.shape
    count = received.shape[0] // 4
    half = jax.ShapeDtypeStruct((2, count, rows // 2, width), partials.dtype)

    def own(u):
        return pl.BlockSpec((1, rows, width), lambda i, picked: (picked[4 * i + u], 0, 0))

    return pl.pallas_call(
        pair_kernel,
        grid_spec=pltpu.PrefetchScalarGridSpec(
            num_scalar_prefetch=1,
            grid=(count,),
            in_specs=[own(0), own(1), own(2), own(3)]
            + [pl.BlockSpec((4, rows, width), lambda i, picked: (i, 0, 0))],
            out_specs=[pl.BlockSpec((2, 1, rows // 2, width), lambda i, picked: (0, i, 0, 0))] * 4,
        ),
        out_shape=[half] * 4,
        compiler_params=params(),
        cost_estimate=SMALL,
    )(picked, partials, partials, partials, partials, received)


def add(one, two):
    return (one.astype(jnp.float32) + two.astype(jnp.float32)).astype(jnp.bfloat16)


def swap(array, bit):
    devices = lax.axis_size("tensor")
    return lax.ppermute(array, "tensor", [(t, t ^ bit) for t in range(devices)])


def swap_core(array):
    return lax.ppermute(array, "section", [(0, 1), (1, 0)])


def pick(picked):
    core = lax.axis_index("section")
    relative = jnp.arange(4, dtype=jnp.int32) ^ lax.axis_index("tensor")
    mine = jnp.take(picked, relative * 2 + core, axis=0).T.reshape(-1)
    other = jnp.take(picked, relative * 2 + 1 - core, axis=0).T.reshape(-1)
    return mine, other


def pair_sums(partials, sent, mine):
    return add_pair(partials, swap_core(sent), mine)


def first_sums(send_a, keep_a, send_b, keep_b):
    return add(keep_a, swap(send_a, 1)), add(keep_b, swap(send_b, 2))


def last_sums(sum_a, sum_b, beside=()):
    last_a, last_b = swap(sum_a[1], 2), swap(sum_b[1], 1)
    if beside:
        last_a, last_b, beside = lax.optimization_barrier((last_a, last_b, beside))
    return jnp.concatenate([add(sum_a[0], last_a), add(sum_b[0], last_b)], axis=1), beside


def gather_blocks(first, second, by_entry, early_work, finish):
    total = by_entry.size
    cut = first.shape[0]
    tensor, core = lax.axis_index("tensor"), lax.axis_index("section")
    x_first, y_second = swap(first, 1), swap(second, 2)
    y_first, x_second = swap(first, 2), swap(second, 1)
    x_first, y_second, early_work = lax.optimization_barrier((x_first, y_second, early_work))
    d_first, d_second = swap(x_first, 2), swap(y_second, 1)

    def targets(bits, core):
        places = [by_entry[(tensor ^ bit) * 2 + core] for bit in bits]
        return [piece for place in places for piece in (place[:cut], place[cut:])]

    near = [first, second, x_first, x_second, y_first, y_second]
    near_target = targets((0, 1, 2), core) + targets((0, 1, 2), 1 - core)
    near = near + [swap_core(piece) for piece in near]
    placed = place_blocks(near, jnp.concatenate(near_target), total, [])
    late_work = finish(early_work)
    d_first, d_second, placed, late_work = lax.optimization_barrier(
        (d_first, d_second, placed, late_work)
    )
    far = [d_first, d_second]
    far_target = targets((3,), core) + targets((3,), 1 - core)
    far = far + [swap_core(piece) for piece in far]
    return place_blocks(far, jnp.concatenate(far_target), total, [placed]), late_work


def shards(
    grad_parts,
    weights,
    adam_m,
    adam_v,
    left_stat,
    right_stat,
    left_root,
    right_root,
    block_owner,
    block_matrix,
    factors,
    factor_grad,
    factor_m,
    factor_v,
):
    capacity = left_stat.shape[0]
    blocks, rows, cols = weights.shape
    size = left_stat.shape[1]
    group = size // cols
    per = blocks // group
    sends = -(-capacity // group)
    owner_index = lax.axis_index("shard")
    group_index = lax.axis_index(GROUP)
    owner_count = lax.axis_size("shard")

    ids = jnp.arange(blocks, dtype=jnp.int32)
    owners = jnp.arange(owner_count, dtype=jnp.int32)
    loads = jnp.sum((block_owner[None, :] == owners[:, None]).astype(jnp.int32), axis=1)
    heavy = jnp.min(jnp.where(loads == jnp.max(loads), owners, owner_count))
    turn = (block_owner - heavy) % owner_count
    own_turn = (owner_index - heavy) % owner_count
    before = (turn[None, :] < turn[:, None]) | (
        (turn[None, :] == turn[:, None]) & (ids[None, :] < ids[:, None])
    )
    position = jnp.sum(before.astype(jnp.int32), axis=1)
    place = (position % group) * per + position // group
    order = jnp.sum(jnp.where(place[None, :] == ids[:, None], ids[None, :], 0), axis=1)

    first = jnp.sum((turn < own_turn).astype(jnp.int32))
    held = jnp.sum((turn == own_turn).astype(jnp.int32))
    early = sends - 1 if blocks - capacity <= group else 0
    is_heavy = own_turn == 0
    own_entry = (first - group_index + group - 1) // group

    def deal(tiles):
        return lax.all_to_all(
            tiles.reshape(group, per, rows, cols), GROUP, split_axis=0, concat_axis=0, tiled=True
        )

    by_entry = order.reshape(group, per)
    partials = grad_parts[0]
    cuts = [(0, early), (early, per)] if early else [(0, per)]
    orders = [pick(by_entry[:, a:b]) for a, b in cuts]
    right_dealt = deal(reorder(right_root, order))
    sent = [reorder(partials, other) for _, other in orders]
    right_dealt, sent[-1] = lax.optimization_barrier((right_dealt, sent[-1]))
    if early and owner_count == 4 and rows * owner_count == size:
        spread = group // owner_count
        near = first_hop(right_dealt)
        sums = first_sums(*pair_sums(partials, sent[0], orders[0][0]))
        pairs = pair_sums(partials, sent[1], orders[1][0])
        sums, near, pairs = lax.optimization_barrier((sums, near, pairs))
        summed, middle = last_sums(*sums, next_hop(near, spread))
        gradient = [summed]
        sums, far = lax.optimization_barrier((first_sums(*pairs), next_hop(middle, spread)))
        gradient.append(last_sums(*sums)[0])
        downs, ups = zip(near, middle, far)
        rights = [right_dealt, *downs, *ups]
    else:
        gradient = [
            last_sums(*first_sums(*pair_sums(partials, part, mine)))[0]
            for part, (mine, _) in zip(sent, orders)
        ]
        rights = [lax.all_gather(right_dealt, "shard", axis=0)]
    gradient = [lax.optimization_barrier(part) for part in gradient]
    grad_blocks = [lax.all_gather(part, "shard", axis=0) for part in gradient]
    left_dealt = deal(reorder(left_root, order))
    weights_sent = reorder(weights, order)
    tiles = jnp.concatenate(gradient, axis=0).reshape(per, rows, group, cols)
    tiles = deal(jnp.transpose(tiles, (2, 0, 1, 3)))

    if early:
        grad_blocks[0], left_dealt, weights_sent, tiles = lax.optimization_barrier(
            (grad_blocks[0], left_dealt, weights_sent, tiles)
        )
        slabs = grams(grad_blocks[0], jnp.arange(early, dtype=jnp.int32))
        slabs, left_dealt, tiles = lax.optimization_barrier((slabs, left_dealt, tiles))
        received = lax.all_to_all(slabs, GROUP, split_axis=0, concat_axis=0, tiled=True)
        received, weights_sent = lax.optimization_barrier((received, weights_sent))
    weights_dealt = deal(weights_sent)
    adam_m_new, adam_v_new, adam_total = adam(
        tiles.reshape(blocks, rows, cols), place, adam_m, adam_v
    )
    pieces = [precondition(left_dealt, 0, grad_blocks[0], rights)]
    if early:
        grad_blocks[1], adam_total, pieces[0] = lax.optimization_barrier(
            (grad_blocks[1], adam_total, pieces[0])
        )
        pieces.append(precondition(left_dealt, early, grad_blocks[1], rights))
    entry = jnp.where(is_heavy, early, own_entry) - early
    last_slabs = grams(grad_blocks[-1], jnp.clip(entry, 0, per - 1 - early).reshape(1))
    precond_total = jnp.concatenate([total for _, total in pieces], axis=0)

    matrix_range = jnp.arange(MATS, dtype=jnp.int32)
    onehot = (block_matrix[:, None] == matrix_range[None, :]).astype(jnp.float32)
    own_order = lax.dynamic_slice_in_dim(order, group_index * per, per)
    own_onehot = jnp.sum(
        jnp.where((own_order[:, None] == ids[None, :])[:, :, None], onehot[None, :, :], 0.0), axis=1
    )
    adam_part = jnp.sum(jnp.sum(adam_total, axis=(1, 2))[:, None] * onehot, axis=0)
    shampoo_part = jnp.sum(jnp.sum(precond_total, axis=(1, 2))[:, None] * own_onehot, axis=0)
    parts = jnp.pad(jnp.stack([adam_part, shampoo_part]), ((0, 6), (0, LANES - MATS)))
    if early:
        received, last_slabs, parts = lax.optimization_barrier((received, last_slabs, parts))
    devices = owner_count * group
    parts = lax.all_to_all(
        jnp.broadcast_to(parts[None], (devices,) + parts.shape), ALL, 0, 0, tiled=True
    )
    adam_norm, shampoo_norm = jnp.sum(parts, axis=0)[:2, :MATS]
    counts = jnp.sum(onehot, axis=0) * float(size * size)
    graft_scale = jnp.sqrt(adam_norm / (shampoo_norm + FLOOR_RATE * counts))
    block_scale = jnp.sum(own_onehot * graft_scale[None, :], axis=1)

    last = lax.all_to_all(last_slabs, GROUP, split_axis=0, concat_axis=0, tiled=True)
    updated = [
        update(weights_dealt, a, piece, block_scale[a:b])
        for (a, b), (piece, _) in zip(cuts, pieces)
    ]
    if len(updated) == 1:
        updated = [updated[0][: per // 2], updated[0][per // 2 :]]
    stats = ()
    if early:
        ranks = jnp.arange(early * group, dtype=jnp.int32)
        base = jnp.where(is_heavy, 0, capacity - early * group)
        filled = jnp.where(is_heavy, 1, 0) * jnp.ones_like(ranks)
        stats = refresh(
            left_stat, right_stat, received, base, ranks % group, ranks // group, filled, stats
        )
    base = jnp.where(is_heavy, early * group, 0)
    ranks = base + jnp.arange(capacity - early * group, dtype=jnp.int32)
    filled = (ranks < held).astype(jnp.int32)
    source = (first + ranks) % group
    nothing = jnp.zeros_like(ranks)
    finish = lambda earlier: refresh(
        left_stat, right_stat, last, base, source, nothing, filled, earlier
    )
    new_weights, (left_new, right_new) = gather_blocks(*updated, by_entry, stats, finish)

    factor_m_new, factor_v_new, factor_step = adam_direction(
        factor_grad.astype(jnp.float32), factor_m, factor_v
    )
    factors_new = factors - LEARNING * (factor_step + DECAY_RATE * factors)
    return (
        new_weights,
        adam_m_new,
        adam_v_new,
        left_new,
        right_new,
        factors_new,
        factor_m_new,
        factor_v_new,
    )


def solution(mesh):
    tile = P(None, "shard", GROUP)
    stat = P("shard", None, GROUP)
    factor = P("shard", GROUP)
    in_specs = (P(GROUP, None, "shard", None), tile, tile, tile, stat, stat, tile, tile, P(), P())
    out_specs = (P(None, "shard", None), tile, tile, stat, stat)
    return jax.shard_map(
        shards,
        mesh=mesh,
        in_specs=in_specs + (factor,) * 4,
        out_specs=out_specs + (factor,) * 3,
        check_vma=False,
    )
```

```python
import functools

import jax
import jax.numpy as jnp
from jax import lax
from jax.experimental import pallas as pl
from jax.experimental.pallas import tpu as pltpu
from jax.sharding import PartitionSpec as P

MATS = 5

BETA_ONE = 0.9
BETA_TWO = 0.95
BETA_STAT = 0.95
LEARNING = 0.1
DECAY_RATE = 0.1
EPSILON = 1e-08
FLOOR_RATE = 1e-06
CORRECT_ONE = 1.0 - 0.9**10
CORRECT_TWO = 1.0 - 0.95**10

GROUP = ("tensor", "section")
ALL = ("shard", "tensor", "section")
VMEM_LIMIT = 48 * 1024 * 1024
LANES = 128
SMALL = pl.CostEstimate(flops=0, bytes_accessed=0, transcendentals=0)


def params():
    return pltpu.CompilerParams(vmem_limit_bytes=VMEM_LIMIT)


def adam_direction(grad_float, moment, second):
    moment_new = BETA_ONE * moment + (1.0 - BETA_ONE) * grad_float
    second_new = BETA_TWO * second + (1.0 - BETA_TWO) * grad_float * grad_float
    direction = moment_new / CORRECT_ONE / (jnp.sqrt(second_new / CORRECT_TWO) + EPSILON)
    return (moment_new, second_new, direction)


def copy_blocks(pairs, held, arrived, left):
    into = [
        pltpu.make_async_copy(source, held.at[i], arrived.at[i])
        for i, (source, _) in enumerate(pairs)
    ]
    out_of = [
        pltpu.make_async_copy(held.at[i], target, left.at[i]) for i, (_, target) in enumerate(pairs)
    ]
    for copy in into:
        copy.start()
    for arrival, copy in zip(into, out_of):
        arrival.wait()
        copy.start()
    for copy in out_of:
        copy.wait()


def copy_scratch(count, tile, kind):
    return [
        pltpu.VMEM((count,) + tile, kind),
        pltpu.SemaphoreType.DMA((count,)),
        pltpu.SemaphoreType.DMA((count,)),
    ]


def reorder_kernel(order, blocks, out, held, arrived, left):
    pairs = [(blocks.at[order[i]], out.at[i]) for i in range(out.shape[0])]
    copy_blocks(pairs, held, arrived, left)


def reorder(blocks, order):
    count, tile = order.shape[0], blocks.shape[1:]
    return pl.pallas_call(
        reorder_kernel,
        grid_spec=pltpu.PrefetchScalarGridSpec(
            num_scalar_prefetch=1,
            grid=(1,),
            in_specs=[pl.BlockSpec(memory_space=pl.ANY)],
            out_specs=pl.BlockSpec(memory_space=pl.ANY),
            scratch_shapes=copy_scratch(count, tile, blocks.dtype),
        ),
        out_shape=jax.ShapeDtypeStruct((count,) + tile, blocks.dtype),
        compiler_params=params(),
        cost_estimate=SMALL,
    )(order, blocks)


def place_kernel(sources, target, *refs):
    out, held, arrived, left = refs[-4:]
    blocks = [ref.at[i] for ref in refs[:sources] for i in range(ref.shape[0])]
    pairs = [(block, out.at[target[i]]) for i, block in enumerate(blocks)]
    copy_blocks(pairs, held, arrived, left)


def place_blocks(arrays, target, total, earlier):
    tile, kind = arrays[0].shape[1:], arrays[0].dtype
    inputs = list(arrays) + list(earlier)
    return pl.pallas_call(
        functools.partial(place_kernel, len(arrays)),
        grid_spec=pltpu.PrefetchScalarGridSpec(
            num_scalar_prefetch=1,
            grid=(1,),
            in_specs=[pl.BlockSpec(memory_space=pl.ANY)] * len(inputs),
            out_specs=pl.BlockSpec(memory_space=pl.ANY),
            scratch_shapes=copy_scratch(target.shape[0], tile, kind),
        ),
        out_shape=jax.ShapeDtypeStruct((total,) + tile, kind),
        input_output_aliases={1 + len(arrays) + i: i for i in range(len(earlier))},
        compiler_params=params(),
        cost_estimate=SMALL,
    )(target, *inputs)


def adam_kernel(place, grad, moment, second, moment_out, second_out, total):
    moment_new, second_new, direction = adam_direction(
        grad[0].astype(jnp.float32), moment[0], second[0]
    )
    moment_out[0] = moment_new
    second_out[0] = second_new
    total[0] = jnp.sum(direction * direction, axis=0, keepdims=True)


def adam(grad_tiles, place, moment, second):
    count, rows, cols = moment.shape
    own = pl.BlockSpec((1, rows, cols), lambda i, place: (i, 0, 0))
    return pl.pallas_call(
        adam_kernel,
        grid_spec=pltpu.PrefetchScalarGridSpec(
            num_scalar_prefetch=1,
            grid=(count,),
            in_specs=[
                pl.BlockSpec((1, rows, cols), lambda i, place: (place[i], 0, 0)),
                own,
                own,
            ],
            out_specs=[own, own, pl.BlockSpec((1, 1, cols), lambda i, place: (i, 0, 0))],
        ),
        out_shape=[
            jax.ShapeDtypeStruct(moment.shape, jnp.float32),
            jax.ShapeDtypeStruct(moment.shape, jnp.float32),
            jax.ShapeDtypeStruct((count, 1, cols), jnp.float32),
        ],
        compiler_params=params(),
        cost_estimate=SMALL,
    )(place, grad_tiles, moment, second)


def gram_kernel(chosen, grad, out):
    parts, _, rows, width = grad.shape
    size = parts * rows
    whole = grad[:, 0].reshape(size, width)
    turned = whole.T
    step = 2 * LANES
    for start in range(0, size, step):
        left = lax.dot_general(
            whole,
            whole[start : start + step, :],
            (((1,), (1,)), ((), ())),
            preferred_element_type=jnp.float32,
        ).astype(jnp.bfloat16)
        right = lax.dot_general(
            turned,
            whole[:, start : start + step],
            (((1,), (0,)), ((), ())),
            preferred_element_type=jnp.float32,
        ).astype(jnp.bfloat16)
        for half in range(2):
            slab = start // LANES + half
            out[slab, 0, 0] = left[:, half * LANES : (half + 1) * LANES]
            out[slab, 0, 1] = right[:, half * LANES : (half + 1) * LANES]


def grams(grad_blocks, chosen):
    shards, per, rows, width = grad_blocks.shape
    size = shards * rows
    slabs = size // LANES
    count = chosen.shape[0]
    return pl.pallas_call(
        gram_kernel,
        grid_spec=pltpu.PrefetchScalarGridSpec(
            num_scalar_prefetch=1,
            grid=(count,),
            in_specs=[
                pl.BlockSpec((shards, 1, rows, width), lambda j, chosen: (0, chosen[j], 0, 0))
            ],
            out_specs=pl.BlockSpec(
                (slabs, 1, 2, size, LANES), lambda j, chosen: (0, j, 0, 0, 0)
            ),
        ),
        out_shape=jax.ShapeDtypeStruct((slabs, count, 2, size, LANES), jnp.bfloat16),
        compiler_params=params(),
        cost_estimate=SMALL,
    )(chosen, grad_blocks)


def stat_kernel(
    base, source, entry, filled, left_stat, right_stat, left_gram, right_gram, *refs
):
    left_out, right_out = refs[-2:]
    full = filled[pl.program_id(0)] > 0
    left = left_gram[0, 0, 0].astype(jnp.float32)
    right = right_gram[0, 0, 0].astype(jnp.float32)
    left_out[0] = BETA_STAT * left_stat[0] + jnp.where(full, (1.0 - BETA_STAT) * left, 0.0)
    right_out[0] = BETA_STAT * right_stat[0] + jnp.where(full, (1.0 - BETA_STAT) * right, 0.0)


def refresh(left_stat, right_stat, received, base, source, entry, filled, earlier):
    slots, size, cols = left_stat.shape
    count = source.shape[0]
    own = pl.BlockSpec((1, size, cols), lambda r, base, source, entry, filled: (base[0] + r, 0, 0))
    gram = (1, 1, 1, size, cols)
    shape = jax.ShapeDtypeStruct(left_stat.shape, jnp.float32)
    return pl.pallas_call(
        stat_kernel,
        grid_spec=pltpu.PrefetchScalarGridSpec(
            num_scalar_prefetch=4,
            grid=(count,),
            in_specs=[
                own,
                own,
                pl.BlockSpec(
                    gram, lambda r, base, source, entry, filled: (source[r], entry[r], 0, 0, 0)
                ),
                pl.BlockSpec(
                    gram, lambda r, base, source, entry, filled: (source[r], entry[r], 1, 0, 0)
                ),
            ]
            + [pl.BlockSpec(memory_space=pl.ANY)] * len(earlier),
            out_specs=[own, own],
        ),
        out_shape=[shape, shape],
        input_output_aliases={8 + i: i for i in range(len(earlier))},
        compiler_params=params(),
        cost_estimate=SMALL,
    )(
        base.reshape(1), source, entry, filled, left_stat, right_stat, received, received, *earlier
    )


def left_product(left, grad):
    slabs, _, rows, _ = left.shape
    left_rows = jnp.concatenate([left[s, 0] for s in range(slabs)], axis=1)
    whole = grad[:, 0].reshape(grad.shape[0] * rows, grad.shape[3])
    return jnp.dot(left_rows, whole, preferred_element_type=jnp.float32).astype(jnp.bfloat16)


def precond_kernel(left, grad, right, out, total):
    slabs, _, rows, cols = left.shape
    parts = grad.shape[0]
    mixed = left_product(left, grad)
    total[...] = jnp.zeros_like(total)
    step = 2
    for start in range(0, slabs, step):
        columns = jnp.concatenate(
            [right[:, s, 0].reshape(parts * rows, cols) for s in range(start, start + step)], axis=1
        )
        piece = jnp.dot(mixed, columns, preferred_element_type=jnp.float32)
        out[0, :, start * cols : (start + step) * cols] = piece.astype(jnp.bfloat16)
        square = jnp.sum(piece * piece, axis=0, keepdims=True)
        total[0] += square[:, :cols] + square[:, cols:]


def tile_sources(mine, count, spread):
    found = {(mine, b): (0, spread * b) for b in range(count)}
    for hop in range(1, count):
        for i in range(count - hop):
            if mine + hop < count:
                found[mine + hop, (mine + hop + i) % count] = (hop, spread * i)
            if mine - hop >= 0:
                found[mine - hop, (mine - hop - i) % count] = (count - 1 + hop, spread * i)
    return found


def precond_tiles_kernel(me, left, grad, *refs):
    rights, out, total = refs[:-2], refs[-2], refs[-1]
    slabs, _, rows, cols = left.shape
    parts = grad.shape[0]
    spread = slabs // parts
    mixed = left_product(left, grad)
    total[...] = jnp.zeros_like(total)
    for mine in range(parts):

        @pl.when(me[0] == mine)
        def _(mine=mine):
            found = tile_sources(mine, parts, spread)
            for b in range(parts):
                piece = jnp.zeros((rows, spread * cols), jnp.float32)
                for a in range(parts):
                    turned = (a, b) not in found
                    array, first = found[(b, a) if turned else (a, b)]
                    tile = jnp.concatenate(
                        [rights[array][first + s, 0] for s in range(spread)], axis=1
                    )
                    piece += lax.dot_general(
                        mixed[:, a * rows : (a + 1) * rows],
                        tile,
                        (((1,), (1 if turned else 0,)), ((), ())),
                        preferred_element_type=jnp.float32,
                    )
                out[0, :, b * rows : (b + 1) * rows] = piece.astype(jnp.bfloat16)
                square = jnp.sum(piece * piece, axis=0, keepdims=True)
                total[0] += sum(square[:, s * cols : (s + 1) * cols] for s in range(spread))


def first_hop(right):
    slabs, per, rows, cols = right.shape
    count, me = lax.axis_size("shard"), lax.axis_index("shard")
    spread = slabs // count
    lane = jnp.arange(spread * (count - 1), dtype=jnp.int32)
    moved = []
    for sign in (1, -1):
        tiles = (me + sign * (lane // spread)) % count
        picked = reorder(right.reshape(slabs, per * rows, cols), tiles * spread + lane % spread)
        moved.append(picked.reshape(lane.shape[0], per, rows, cols))
    return hop(moved)


def hop(moved):
    count = lax.axis_size("shard")
    down = [(a, a - 1) for a in range(1, count)]
    up = [(a, a + 1) for a in range(count - 1)]
    return lax.ppermute(moved[0], "shard", down), lax.ppermute(moved[1], "shard", up)


def next_hop(moved, spread):
    return hop([part[: part.shape[0] - spread] for part in moved])


def precondition(left, start, grad_blocks, rights):
    shards, count, rows, width = grad_blocks.shape
    slabs, _, _, cols = left.shape
    size = shards * rows
    whole = len(rights) == 1
    if whole:
        right_specs = [pl.BlockSpec((shards, slabs, 1, rows, cols), lambda m, me: (0, 0, start + m, 0, 0))]
    else:
        right_specs = [
            pl.BlockSpec((right.shape[0], 1, rows, cols), lambda m, me: (0, start + m, 0, 0))
            for right in rights
        ]
    body = precond_tiles_kernel
    if whole:
        body = lambda me, *refs: precond_kernel(*refs)
    return pl.pallas_call(
        body,
        grid_spec=pltpu.PrefetchScalarGridSpec(
            num_scalar_prefetch=1,
            grid=(count,),
            in_specs=[
                pl.BlockSpec((slabs, 1, rows, cols), lambda m, me: (0, start + m, 0, 0)),
                pl.BlockSpec((shards, 1, rows, width), lambda m, me: (0, m, 0, 0)),
            ]
            + right_specs,
            out_specs=[
                pl.BlockSpec((1, rows, width), lambda m, me: (m, 0, 0)),
                pl.BlockSpec((1, 1, cols), lambda m, me: (m, 0, 0)),
            ],
        ),
        out_shape=[
            jax.ShapeDtypeStruct((count, rows, width), jnp.bfloat16),
            jax.ShapeDtypeStruct((count, 1, cols), jnp.float32),
        ],
        compiler_params=params(),
        cost_estimate=SMALL,
    )(lax.axis_index("shard").reshape(1), left, grad_blocks, *rights)


def update_kernel(scale, weights, precond, out):
    slabs = weights.shape[0]
    factor = scale[pl.program_id(0)]
    old = jnp.concatenate([weights[s, 0] for s in range(slabs)], axis=1).astype(jnp.float32)
    step = factor * precond[0].astype(jnp.float32) + DECAY_RATE * old
    out[0] = (old - LEARNING * step).astype(jnp.bfloat16)


def update(weights, start, precond, scale):
    slabs, _, rows, cols = weights.shape
    count = precond.shape[0]
    width = slabs * cols
    own = pl.BlockSpec((1, rows, width), lambda m, scale: (m, 0, 0))
    return pl.pallas_call(
        update_kernel,
        grid_spec=pltpu.PrefetchScalarGridSpec(
            num_scalar_prefetch=1,
            grid=(count,),
            in_specs=[
                pl.BlockSpec((slabs, 1, rows, cols), lambda m, scale: (0, start + m, 0, 0)),
                own,
            ],
            out_specs=own,
        ),
        out_shape=jax.ShapeDtypeStruct((count, rows, width), jnp.bfloat16),
        compiler_params=params(),
        cost_estimate=SMALL,
    )(scale, weights, precond)


def pair_kernel(picked, first, second, third, fourth, received, send_a, keep_a, send_b, keep_b):
    half = first.shape[1] // 2
    added = [
        (own[0].astype(jnp.float32) + received[u].astype(jnp.float32)).astype(jnp.bfloat16)
        for u, own in enumerate((first, second, third, fourth))
    ]
    for ref, chosen, start in (
        (send_a, (1, 3), 0),
        (keep_a, (0, 2), 0),
        (send_b, (2, 3), half),
        (keep_b, (0, 1), half),
    ):
        for i, u in enumerate(chosen):
            ref[i, 0] = added[u][start : start + half]


def add_pair(partials, received, picked):
    _, rows, width = partials.shape
    count = received.shape[0] // 4
    half = jax.ShapeDtypeStruct((2, count, rows // 2, width), partials.dtype)

    def own(u):
        return pl.BlockSpec((1, rows, width), lambda i, picked: (picked[4 * i + u], 0, 0))

    return pl.pallas_call(
        pair_kernel,
        grid_spec=pltpu.PrefetchScalarGridSpec(
            num_scalar_prefetch=1,
            grid=(count,),
            in_specs=[own(0), own(1), own(2), own(3)]
            + [pl.BlockSpec((4, rows, width), lambda i, picked: (i, 0, 0))],
            out_specs=[pl.BlockSpec((2, 1, rows // 2, width), lambda i, picked: (0, i, 0, 0))] * 4,
        ),
        out_shape=[half] * 4,
        compiler_params=params(),
        cost_estimate=SMALL,
    )(picked, partials, partials, partials, partials, received)


def add(one, two):
    return (one.astype(jnp.float32) + two.astype(jnp.float32)).astype(jnp.bfloat16)


def swap(array, bit):
    devices = lax.axis_size("tensor")
    return lax.ppermute(array, "tensor", [(t, t ^ bit) for t in range(devices)])


def swap_core(array):
    return lax.ppermute(array, "section", [(0, 1), (1, 0)])


def pick(picked):
    core = lax.axis_index("section")
    relative = jnp.arange(4, dtype=jnp.int32) ^ lax.axis_index("tensor")
    mine = jnp.take(picked, relative * 2 + core, axis=0).T.reshape(-1)
    other = jnp.take(picked, relative * 2 + 1 - core, axis=0).T.reshape(-1)
    return mine, other


def first_sums(partials, sent, mine):
    received = swap_core(sent)
    send_a, keep_a, send_b, keep_b = add_pair(partials, received, mine)
    return add(keep_a, swap(send_a, 1)), add(keep_b, swap(send_b, 2))


def last_sums(sum_a, sum_b):
    last_a = add(sum_a[0], swap(sum_a[1], 2))
    last_b = add(sum_b[0], swap(sum_b[1], 1))
    return jnp.concatenate([last_a, last_b], axis=1)


def gather_blocks(first, second, by_entry, early_work, finish):
    total = by_entry.size
    cut = first.shape[0]
    tensor, core = lax.axis_index("tensor"), lax.axis_index("section")
    x_first, y_second = swap(first, 1), swap(second, 2)
    y_first, x_second = swap(first, 2), swap(second, 1)
    x_first, y_second, early_work = lax.optimization_barrier((x_first, y_second, early_work))
    d_first, d_second = swap(x_first, 2), swap(y_second, 1)

    def targets(bits, core):
        places = [by_entry[(tensor ^ bit) * 2 + core] for bit in bits]
        return [piece for place in places for piece in (place[:cut], place[cut:])]

    near = [first, second, x_first, x_second, y_first, y_second]
    near_target = targets((0, 1, 2), core) + targets((0, 1, 2), 1 - core)
    near = near + [swap_core(piece) for piece in near]
    placed = place_blocks(near, jnp.concatenate(near_target), total, [])
    late_work = finish(early_work)
    d_first, d_second, placed, late_work = lax.optimization_barrier(
        (d_first, d_second, placed, late_work)
    )
    far = [d_first, d_second]
    far_target = targets((3,), core) + targets((3,), 1 - core)
    far = far + [swap_core(piece) for piece in far]
    return place_blocks(far, jnp.concatenate(far_target), total, [placed]), late_work


def shards(
    grad_parts,
    weights,
    adam_m,
    adam_v,
    left_stat,
    right_stat,
    left_root,
    right_root,
    block_owner,
    block_matrix,
    factors,
    factor_grad,
    factor_m,
    factor_v,
):
    capacity = left_stat.shape[0]
    blocks, rows, cols = weights.shape
    size = left_stat.shape[1]
    group = size // cols
    per = blocks // group
    sends = -(-capacity // group)
    owner_index = lax.axis_index("shard")
    group_index = lax.axis_index(GROUP)
    owner_count = lax.axis_size("shard")

    ids = jnp.arange(blocks, dtype=jnp.int32)
    owners = jnp.arange(owner_count, dtype=jnp.int32)
    loads = jnp.sum((block_owner[None, :] == owners[:, None]).astype(jnp.int32), axis=1)
    heavy = jnp.min(jnp.where(loads == jnp.max(loads), owners, owner_count))
    turn = (block_owner - heavy) % owner_count
    own_turn = (owner_index - heavy) % owner_count
    before = (turn[None, :] < turn[:, None]) | (
        (turn[None, :] == turn[:, None]) & (ids[None, :] < ids[:, None])
    )
    position = jnp.sum(before.astype(jnp.int32), axis=1)
    place = (position % group) * per + position // group
    order = jnp.sum(jnp.where(place[None, :] == ids[:, None], ids[None, :], 0), axis=1)

    first = jnp.sum((turn < own_turn).astype(jnp.int32))
    held = jnp.sum((turn == own_turn).astype(jnp.int32))
    early = sends - 1 if blocks - capacity <= group else 0
    is_heavy = own_turn == 0
    own_entry = (first - group_index + group - 1) // group

    def deal(tiles):
        return lax.all_to_all(
            tiles.reshape(group, per, rows, cols), GROUP, split_axis=0, concat_axis=0, tiled=True
        )

    by_entry = order.reshape(group, per)
    partials = grad_parts[0]
    cuts = [(0, early), (early, per)] if early else [(0, per)]
    orders = [pick(by_entry[:, a:b]) for a, b in cuts]
    sent = [reorder(partials, other) for _, other in orders]
    sent[0], right_root = lax.optimization_barrier((sent[0], right_root))
    right_dealt = deal(reorder(right_root, order))
    right_dealt, sent[-1] = lax.optimization_barrier((right_dealt, sent[-1]))
    if early and owner_count == 4 and rows * owner_count == size:
        spread = group // owner_count
        near = first_hop(right_dealt)
        sums = first_sums(partials, sent[0], orders[0][0])
        sums, near = lax.optimization_barrier((sums, near))
        gradient = [last_sums(*sums)]
        middle = next_hop(near, spread)
        gradient.append(last_sums(*first_sums(partials, sent[1], orders[1][0])))
        rights = [near, middle]
    else:
        gradient = [
            last_sums(*first_sums(partials, part, mine)) for part, (mine, _) in zip(sent, orders)
        ]
        rights = [lax.all_gather(right_dealt, "shard", axis=0)]
    gradient = [lax.optimization_barrier(part) for part in gradient]
    grad_blocks = [lax.all_gather(part, "shard", axis=0) for part in gradient]
    left_dealt = deal(reorder(left_root, order))
    weights_dealt = deal(reorder(weights, order))
    tiles = jnp.concatenate(gradient, axis=0).reshape(per, rows, group, cols)
    tiles = deal(jnp.transpose(tiles, (2, 0, 1, 3)))

    if early:
        grad_blocks[0], left_dealt, weights_dealt, tiles, rights = lax.optimization_barrier(
            (grad_blocks[0], left_dealt, weights_dealt, tiles, rights)
        )
        if len(rights) == 2:
            downs, ups = zip(*rights, next_hop(rights[1], group // owner_count))
            rights = [right_dealt, *downs, *ups]
        slabs = grams(grad_blocks[0], jnp.arange(early, dtype=jnp.int32))
        slabs, left_dealt, tiles = lax.optimization_barrier((slabs, left_dealt, tiles))
        received = lax.all_to_all(slabs, GROUP, split_axis=0, concat_axis=0, tiled=True)
    adam_m_new, adam_v_new, adam_total = adam(
        tiles.reshape(blocks, rows, cols), place, adam_m, adam_v
    )
    pieces = [precondition(left_dealt, 0, grad_blocks[0], rights)]
    if early:
        grad_blocks[1], adam_total, pieces[0] = lax.optimization_barrier(
            (grad_blocks[1], adam_total, pieces[0])
        )
        pieces.append(precondition(left_dealt, early, grad_blocks[1], rights))
    entry = jnp.where(is_heavy, early, own_entry) - early
    last_slabs = grams(grad_blocks[-1], jnp.clip(entry, 0, per - 1 - early).reshape(1))
    precond_total = jnp.concatenate([total for _, total in pieces], axis=0)

    matrix_range = jnp.arange(MATS, dtype=jnp.int32)
    onehot = (block_matrix[:, None] == matrix_range[None, :]).astype(jnp.float32)
    own_order = lax.dynamic_slice_in_dim(order, group_index * per, per)
    own_onehot = jnp.sum(
        jnp.where((own_order[:, None] == ids[None, :])[:, :, None], onehot[None, :, :], 0.0), axis=1
    )
    adam_part = jnp.sum(jnp.sum(adam_total, axis=(1, 2))[:, None] * onehot, axis=0)
    shampoo_part = jnp.sum(jnp.sum(precond_total, axis=(1, 2))[:, None] * own_onehot, axis=0)
    parts = jnp.pad(jnp.stack([adam_part, shampoo_part]), ((0, 6), (0, LANES - MATS)))
    if early:
        received, last_slabs, parts = lax.optimization_barrier((received, last_slabs, parts))
    devices = owner_count * group
    parts = lax.all_to_all(
        jnp.broadcast_to(parts[None], (devices,) + parts.shape), ALL, 0, 0, tiled=True
    )
    adam_norm, shampoo_norm = jnp.sum(parts, axis=0)[:2, :MATS]
    counts = jnp.sum(onehot, axis=0) * float(size * size)
    graft_scale = jnp.sqrt(adam_norm / (shampoo_norm + FLOOR_RATE * counts))
    block_scale = jnp.sum(own_onehot * graft_scale[None, :], axis=1)

    last = lax.all_to_all(last_slabs, GROUP, split_axis=0, concat_axis=0, tiled=True)
    updated = [
        update(weights_dealt, a, piece, block_scale[a:b])
        for (a, b), (piece, _) in zip(cuts, pieces)
    ]
    if len(updated) == 1:
        updated = [updated[0][: per // 2], updated[0][per // 2 :]]
    stats = ()
    if early:
        ranks = jnp.arange(early * group, dtype=jnp.int32)
        base = jnp.where(is_heavy, 0, capacity - early * group)
        filled = jnp.where(is_heavy, 1, 0) * jnp.ones_like(ranks)
        stats = refresh(
            left_stat, right_stat, received, base, ranks % group, ranks // group, filled, stats
        )
    base = jnp.where(is_heavy, early * group, 0)
    ranks = base + jnp.arange(capacity - early * group, dtype=jnp.int32)
    filled = (ranks < held).astype(jnp.int32)
    source = (first + ranks) % group
    nothing = jnp.zeros_like(ranks)
    finish = lambda earlier: refresh(
        left_stat, right_stat, last, base, source, nothing, filled, earlier
    )
    new_weights, (left_new, right_new) = gather_blocks(*updated, by_entry, stats, finish)

    factor_m_new, factor_v_new, factor_step = adam_direction(
        factor_grad.astype(jnp.float32), factor_m, factor_v
    )
    factors_new = factors - LEARNING * (factor_step + DECAY_RATE * factors)
    return (
        new_weights,
        adam_m_new,
        adam_v_new,
        left_new,
        right_new,
        factors_new,
        factor_m_new,
        factor_v_new,
    )


def solution(mesh):
    tile = P(None, "shard", GROUP)
    stat = P("shard", None, GROUP)
    factor = P("shard", GROUP)
    in_specs = (P(GROUP, None, "shard", None), tile, tile, tile, stat, stat, tile, tile, P(), P())
    out_specs = (P(None, "shard", None), tile, tile, stat, stat)
    return jax.shard_map(
        shards,
        mesh=mesh,
        in_specs=in_specs + (factor,) * 4,
        out_specs=out_specs + (factor,) * 3,
        check_vma=False,
    )
```

```python
import functools

import jax
import jax.numpy as jnp
from jax import lax
from jax.experimental import pallas as pl
from jax.experimental.pallas import tpu as pltpu
from jax.sharding import PartitionSpec as P

MATS = 5

BETA_ONE = 0.9
BETA_TWO = 0.95
BETA_STAT = 0.95
LEARNING = 0.1
DECAY_RATE = 0.1
EPSILON = 1e-08
FLOOR_RATE = 1e-06
CORRECT_ONE = 1.0 - 0.9**10
CORRECT_TWO = 1.0 - 0.95**10

GROUP = ("tensor", "section")
ALL = ("shard", "tensor", "section")
VMEM_LIMIT = 48 * 1024 * 1024
LANES = 128
SMALL = pl.CostEstimate(flops=0, bytes_accessed=0, transcendentals=0)


def params():
    return pltpu.CompilerParams(vmem_limit_bytes=VMEM_LIMIT)


def adam_direction(grad_float, moment, second):
    moment_new = BETA_ONE * moment + (1.0 - BETA_ONE) * grad_float
    second_new = BETA_TWO * second + (1.0 - BETA_TWO) * grad_float * grad_float
    direction = moment_new / CORRECT_ONE / (jnp.sqrt(second_new / CORRECT_TWO) + EPSILON)
    return (moment_new, second_new, direction)


def copy_blocks(pairs, held, arrived, left):
    into = [
        pltpu.make_async_copy(source, held.at[i], arrived.at[i])
        for i, (source, _) in enumerate(pairs)
    ]
    out_of = [
        pltpu.make_async_copy(held.at[i], target, left.at[i]) for i, (_, target) in enumerate(pairs)
    ]
    for copy in into:
        copy.start()
    for arrival, copy in zip(into, out_of):
        arrival.wait()
        copy.start()
    for copy in out_of:
        copy.wait()


def copy_scratch(count, tile, kind):
    return [
        pltpu.VMEM((count,) + tile, kind),
        pltpu.SemaphoreType.DMA((count,)),
        pltpu.SemaphoreType.DMA((count,)),
    ]


def reorder_kernel(order, blocks, out, held, arrived, left):
    pairs = [(blocks.at[order[i]], out.at[i]) for i in range(out.shape[0])]
    copy_blocks(pairs, held, arrived, left)


def reorder(blocks, order):
    count, tile = order.shape[0], blocks.shape[1:]
    return pl.pallas_call(
        reorder_kernel,
        grid_spec=pltpu.PrefetchScalarGridSpec(
            num_scalar_prefetch=1,
            grid=(1,),
            in_specs=[pl.BlockSpec(memory_space=pl.ANY)],
            out_specs=pl.BlockSpec(memory_space=pl.ANY),
            scratch_shapes=copy_scratch(count, tile, blocks.dtype),
        ),
        out_shape=jax.ShapeDtypeStruct((count,) + tile, blocks.dtype),
        compiler_params=params(),
        cost_estimate=SMALL,
    )(order, blocks)


def place_kernel(sources, target, *refs):
    out, held, arrived, left = refs[-4:]
    blocks = [ref.at[i] for ref in refs[:sources] for i in range(ref.shape[0])]
    pairs = [(block, out.at[target[i]]) for i, block in enumerate(blocks)]
    copy_blocks(pairs, held, arrived, left)


def place_blocks(arrays, target, total, earlier):
    tile, kind = arrays[0].shape[1:], arrays[0].dtype
    inputs = list(arrays) + list(earlier)
    return pl.pallas_call(
        functools.partial(place_kernel, len(arrays)),
        grid_spec=pltpu.PrefetchScalarGridSpec(
            num_scalar_prefetch=1,
            grid=(1,),
            in_specs=[pl.BlockSpec(memory_space=pl.ANY)] * len(inputs),
            out_specs=pl.BlockSpec(memory_space=pl.ANY),
            scratch_shapes=copy_scratch(target.shape[0], tile, kind),
        ),
        out_shape=jax.ShapeDtypeStruct((total,) + tile, kind),
        input_output_aliases={1 + len(arrays) + i: i for i in range(len(earlier))},
        compiler_params=params(),
        cost_estimate=SMALL,
    )(target, *inputs)


def adam_kernel(place, grad, moment, second, moment_out, second_out, total):
    moment_new, second_new, direction = adam_direction(
        grad[0].astype(jnp.float32), moment[0], second[0]
    )
    moment_out[0] = moment_new
    second_out[0] = second_new
    total[0] = jnp.sum(direction * direction, axis=0, keepdims=True)


def adam(grad_tiles, place, moment, second):
    count, rows, cols = moment.shape
    own = pl.BlockSpec((1, rows, cols), lambda i, place: (i, 0, 0))
    return pl.pallas_call(
        adam_kernel,
        grid_spec=pltpu.PrefetchScalarGridSpec(
            num_scalar_prefetch=1,
            grid=(count,),
            in_specs=[
                pl.BlockSpec((1, rows, cols), lambda i, place: (place[i], 0, 0)),
                own,
                own,
            ],
            out_specs=[own, own, pl.BlockSpec((1, 1, cols), lambda i, place: (i, 0, 0))],
        ),
        out_shape=[
            jax.ShapeDtypeStruct(moment.shape, jnp.float32),
            jax.ShapeDtypeStruct(moment.shape, jnp.float32),
            jax.ShapeDtypeStruct((count, 1, cols), jnp.float32),
        ],
        compiler_params=params(),
        cost_estimate=SMALL,
    )(place, grad_tiles, moment, second)


def gram_kernel(chosen, grad, out):
    parts, _, rows, width = grad.shape
    size = parts * rows
    whole = grad[:, 0].reshape(size, width)
    turned = whole.T
    step = 2 * LANES
    for start in range(0, size, step):
        left = lax.dot_general(
            whole,
            whole[start : start + step, :],
            (((1,), (1,)), ((), ())),
            preferred_element_type=jnp.float32,
        ).astype(jnp.bfloat16)
        right = lax.dot_general(
            turned,
            whole[:, start : start + step],
            (((1,), (0,)), ((), ())),
            preferred_element_type=jnp.float32,
        ).astype(jnp.bfloat16)
        for half in range(2):
            slab = start // LANES + half
            out[slab, 0, 0] = left[:, half * LANES : (half + 1) * LANES]
            out[slab, 0, 1] = right[:, half * LANES : (half + 1) * LANES]


def grams(grad_blocks, chosen):
    shards, per, rows, width = grad_blocks.shape
    size = shards * rows
    slabs = size // LANES
    count = chosen.shape[0]
    return pl.pallas_call(
        gram_kernel,
        grid_spec=pltpu.PrefetchScalarGridSpec(
            num_scalar_prefetch=1,
            grid=(count,),
            in_specs=[
                pl.BlockSpec((shards, 1, rows, width), lambda j, chosen: (0, chosen[j], 0, 0))
            ],
            out_specs=pl.BlockSpec(
                (slabs, 1, 2, size, LANES), lambda j, chosen: (0, j, 0, 0, 0)
            ),
        ),
        out_shape=jax.ShapeDtypeStruct((slabs, count, 2, size, LANES), jnp.bfloat16),
        compiler_params=params(),
        cost_estimate=SMALL,
    )(chosen, grad_blocks)


def stat_kernel(
    base, source, entry, filled, left_stat, right_stat, left_gram, right_gram, *refs
):
    left_out, right_out = refs[-2:]
    full = filled[pl.program_id(0)] > 0
    left = left_gram[0, 0, 0].astype(jnp.float32)
    right = right_gram[0, 0, 0].astype(jnp.float32)
    left_out[0] = BETA_STAT * left_stat[0] + jnp.where(full, (1.0 - BETA_STAT) * left, 0.0)
    right_out[0] = BETA_STAT * right_stat[0] + jnp.where(full, (1.0 - BETA_STAT) * right, 0.0)


def refresh(left_stat, right_stat, received, base, source, entry, filled, earlier):
    slots, size, cols = left_stat.shape
    count = source.shape[0]
    own = pl.BlockSpec((1, size, cols), lambda r, base, source, entry, filled: (base[0] + r, 0, 0))
    gram = (1, 1, 1, size, cols)
    shape = jax.ShapeDtypeStruct(left_stat.shape, jnp.float32)
    return pl.pallas_call(
        stat_kernel,
        grid_spec=pltpu.PrefetchScalarGridSpec(
            num_scalar_prefetch=4,
            grid=(count,),
            in_specs=[
                own,
                own,
                pl.BlockSpec(
                    gram, lambda r, base, source, entry, filled: (source[r], entry[r], 0, 0, 0)
                ),
                pl.BlockSpec(
                    gram, lambda r, base, source, entry, filled: (source[r], entry[r], 1, 0, 0)
                ),
            ]
            + [pl.BlockSpec(memory_space=pl.ANY)] * len(earlier),
            out_specs=[own, own],
        ),
        out_shape=[shape, shape],
        input_output_aliases={8 + i: i for i in range(len(earlier))},
        compiler_params=params(),
        cost_estimate=SMALL,
    )(
        base.reshape(1), source, entry, filled, left_stat, right_stat, received, received, *earlier
    )


def left_product(left, grad):
    slabs, _, rows, _ = left.shape
    left_rows = jnp.concatenate([left[s, 0] for s in range(slabs)], axis=1)
    whole = grad[:, 0].reshape(grad.shape[0] * rows, grad.shape[3])
    return jnp.dot(left_rows, whole, preferred_element_type=jnp.float32).astype(jnp.bfloat16)


def precond_kernel(left, grad, right, out, total):
    slabs, _, rows, cols = left.shape
    parts = grad.shape[0]
    mixed = left_product(left, grad)
    total[...] = jnp.zeros_like(total)
    step = 2
    for start in range(0, slabs, step):
        columns = jnp.concatenate(
            [right[:, s, 0].reshape(parts * rows, cols) for s in range(start, start + step)], axis=1
        )
        piece = jnp.dot(mixed, columns, preferred_element_type=jnp.float32)
        out[0, :, start * cols : (start + step) * cols] = piece.astype(jnp.bfloat16)
        square = jnp.sum(piece * piece, axis=0, keepdims=True)
        total[0] += square[:, :cols] + square[:, cols:]


def tile_sources(mine, count, spread):
    found = {(mine, b): (0, spread * b) for b in range(count)}
    for hop in range(1, count):
        for i in range(count - hop):
            if mine + hop < count:
                found[mine + hop, (mine + hop + i) % count] = (hop, spread * i)
            if mine - hop >= 0:
                found[mine - hop, (mine - hop - i) % count] = (count - 1 + hop, spread * i)
    return found


def precond_tiles_kernel(me, left, grad, *refs):
    rights, out, total = refs[:-2], refs[-2], refs[-1]
    slabs, _, rows, cols = left.shape
    parts = grad.shape[0]
    spread = slabs // parts
    mixed = left_product(left, grad)
    total[...] = jnp.zeros_like(total)
    for mine in range(parts):

        @pl.when(me[0] == mine)
        def _(mine=mine):
            found = tile_sources(mine, parts, spread)
            for b in range(parts):
                piece = jnp.zeros((rows, spread * cols), jnp.float32)
                for a in range(parts):
                    turned = (a, b) not in found
                    array, first = found[(b, a) if turned else (a, b)]
                    tile = jnp.concatenate(
                        [rights[array][first + s, 0] for s in range(spread)], axis=1
                    )
                    piece += lax.dot_general(
                        mixed[:, a * rows : (a + 1) * rows],
                        tile,
                        (((1,), (1 if turned else 0,)), ((), ())),
                        preferred_element_type=jnp.float32,
                    )
                out[0, :, b * rows : (b + 1) * rows] = piece.astype(jnp.bfloat16)
                square = jnp.sum(piece * piece, axis=0, keepdims=True)
                total[0] += sum(square[:, s * cols : (s + 1) * cols] for s in range(spread))


def first_hop(right):
    slabs, per, rows, cols = right.shape
    count, me = lax.axis_size("shard"), lax.axis_index("shard")
    spread = slabs // count
    lane = jnp.arange(spread * (count - 1), dtype=jnp.int32)
    moved = []
    for sign in (1, -1):
        tiles = (me + sign * (lane // spread)) % count
        picked = reorder(right.reshape(slabs, per * rows, cols), tiles * spread + lane % spread)
        moved.append(picked.reshape(lane.shape[0], per, rows, cols))
    return hop(moved)


def hop(moved):
    count = lax.axis_size("shard")
    down = [(a, a - 1) for a in range(1, count)]
    up = [(a, a + 1) for a in range(count - 1)]
    return lax.ppermute(moved[0], "shard", down), lax.ppermute(moved[1], "shard", up)


def next_hop(moved, spread):
    return hop([part[: part.shape[0] - spread] for part in moved])


def precondition(left, start, grad_blocks, rights):
    shards, count, rows, width = grad_blocks.shape
    slabs, _, _, cols = left.shape
    size = shards * rows
    whole = len(rights) == 1
    if whole:
        right_specs = [pl.BlockSpec((shards, slabs, 1, rows, cols), lambda m, me: (0, 0, start + m, 0, 0))]
    else:
        right_specs = [
            pl.BlockSpec((right.shape[0], 1, rows, cols), lambda m, me: (0, start + m, 0, 0))
            for right in rights
        ]
    body = precond_tiles_kernel
    if whole:
        body = lambda me, *refs: precond_kernel(*refs)
    return pl.pallas_call(
        body,
        grid_spec=pltpu.PrefetchScalarGridSpec(
            num_scalar_prefetch=1,
            grid=(count,),
            in_specs=[
                pl.BlockSpec((slabs, 1, rows, cols), lambda m, me: (0, start + m, 0, 0)),
                pl.BlockSpec((shards, 1, rows, width), lambda m, me: (0, m, 0, 0)),
            ]
            + right_specs,
            out_specs=[
                pl.BlockSpec((1, rows, width), lambda m, me: (m, 0, 0)),
                pl.BlockSpec((1, 1, cols), lambda m, me: (m, 0, 0)),
            ],
        ),
        out_shape=[
            jax.ShapeDtypeStruct((count, rows, width), jnp.bfloat16),
            jax.ShapeDtypeStruct((count, 1, cols), jnp.float32),
        ],
        compiler_params=params(),
        cost_estimate=SMALL,
    )(lax.axis_index("shard").reshape(1), left, grad_blocks, *rights)


def update_kernel(me, scale, precond, *refs):
    weights, out = refs[:-1], refs[-1]
    factor = scale[pl.program_id(0)]
    cols = weights[0].shape[2]
    for k, slab in enumerate(weights):
        here = pl.ds(pl.multiple_of((me[0] ^ k) * cols, cols), cols)
        old = slab[0].astype(jnp.float32)
        step = factor * precond[0, :, here].astype(jnp.float32) + DECAY_RATE * old
        out[0, :, here] = (old - LEARNING * step).astype(jnp.bfloat16)


def update(weights, start, precond, scale, me):
    count, rows, width = precond.shape
    cols = weights[0].shape[2]
    own = pl.BlockSpec((1, rows, width), lambda m, me, scale: (m, 0, 0))
    return pl.pallas_call(
        update_kernel,
        grid_spec=pltpu.PrefetchScalarGridSpec(
            num_scalar_prefetch=2,
            grid=(count,),
            in_specs=[own]
            + [pl.BlockSpec((1, rows, cols), lambda m, me, scale: (0, start + m, 0))]
            * len(weights),
            out_specs=own,
        ),
        out_shape=jax.ShapeDtypeStruct((count, rows, width), jnp.bfloat16),
        compiler_params=params(),
        cost_estimate=SMALL,
    )(me.reshape(1), scale, precond, *weights)


def pair_kernel(picked, first, second, third, fourth, received, send_a, keep_a, send_b, keep_b):
    half = first.shape[1] // 2
    added = [
        (own[0].astype(jnp.float32) + received[u].astype(jnp.float32)).astype(jnp.bfloat16)
        for u, own in enumerate((first, second, third, fourth))
    ]
    for ref, chosen, start in (
        (send_a, (1, 3), 0),
        (keep_a, (0, 2), 0),
        (send_b, (2, 3), half),
        (keep_b, (0, 1), half),
    ):
        for i, u in enumerate(chosen):
            ref[i, 0] = added[u][start : start + half]


def add_pair(partials, received, picked):
    _, rows, width = partials.shape
    count = received.shape[0] // 4
    half = jax.ShapeDtypeStruct((2, count, rows // 2, width), partials.dtype)

    def own(u):
        return pl.BlockSpec((1, rows, width), lambda i, picked: (picked[4 * i + u], 0, 0))

    return pl.pallas_call(
        pair_kernel,
        grid_spec=pltpu.PrefetchScalarGridSpec(
            num_scalar_prefetch=1,
            grid=(count,),
            in_specs=[own(0), own(1), own(2), own(3)]
            + [pl.BlockSpec((4, rows, width), lambda i, picked: (i, 0, 0))],
            out_specs=[pl.BlockSpec((2, 1, rows // 2, width), lambda i, picked: (0, i, 0, 0))] * 4,
        ),
        out_shape=[half] * 4,
        compiler_params=params(),
        cost_estimate=SMALL,
    )(picked, partials, partials, partials, partials, received)


def add(one, two):
    return (one.astype(jnp.float32) + two.astype(jnp.float32)).astype(jnp.bfloat16)


def swap(array, bit):
    devices = lax.axis_size("tensor")
    return lax.ppermute(array, "tensor", [(t, t ^ bit) for t in range(devices)])


def swap_core(array):
    return lax.ppermute(array, "section", [(0, 1), (1, 0)])


def pick(picked):
    core = lax.axis_index("section")
    relative = jnp.arange(4, dtype=jnp.int32) ^ lax.axis_index("tensor")
    mine = jnp.take(picked, relative * 2 + core, axis=0).T.reshape(-1)
    other = jnp.take(picked, relative * 2 + 1 - core, axis=0).T.reshape(-1)
    return mine, other


def first_sums(partials, sent, mine):
    received = swap_core(sent)
    send_a, keep_a, send_b, keep_b = add_pair(partials, received, mine)
    return add(keep_a, swap(send_a, 1)), add(keep_b, swap(send_b, 2))


def last_sums(sum_a, sum_b):
    last_a = add(sum_a[0], swap(sum_a[1], 2))
    last_b = add(sum_b[0], swap(sum_b[1], 1))
    return jnp.concatenate([last_a, last_b], axis=1)


def gather_blocks(first, second, by_entry, early_work, finish):
    total = by_entry.size
    cut = first.shape[0]
    tensor, core = lax.axis_index("tensor"), lax.axis_index("section")
    x_first, y_second = swap(first, 1), swap(second, 2)
    y_first, x_second = swap(first, 2), swap(second, 1)
    x_first, y_second, early_work = lax.optimization_barrier((x_first, y_second, early_work))
    d_first, d_second = swap(x_first, 2), swap(y_second, 1)

    def targets(bits, core):
        places = [by_entry[(tensor ^ bit) * 2 + core] for bit in bits]
        return [piece for place in places for piece in (place[:cut], place[cut:])]

    near = [first, second, x_first, x_second, y_first, y_second]
    near_target = targets((0, 1, 2), core) + targets((0, 1, 2), 1 - core)
    near = near + [swap_core(piece) for piece in near]
    placed = place_blocks(near, jnp.concatenate(near_target), total, [])
    late_work = finish(early_work)
    d_first, d_second, placed, late_work = lax.optimization_barrier(
        (d_first, d_second, placed, late_work)
    )
    far = [d_first, d_second]
    far_target = targets((3,), core) + targets((3,), 1 - core)
    far = far + [swap_core(piece) for piece in far]
    return place_blocks(far, jnp.concatenate(far_target), total, [placed]), late_work


def shards(
    grad_parts,
    weights,
    adam_m,
    adam_v,
    left_stat,
    right_stat,
    left_root,
    right_root,
    block_owner,
    block_matrix,
    factors,
    factor_grad,
    factor_m,
    factor_v,
):
    capacity = left_stat.shape[0]
    blocks, rows, cols = weights.shape
    size = left_stat.shape[1]
    group = size // cols
    per = blocks // group
    sends = -(-capacity // group)
    owner_index = lax.axis_index("shard")
    group_index = lax.axis_index(GROUP)
    owner_count = lax.axis_size("shard")

    ids = jnp.arange(blocks, dtype=jnp.int32)
    owners = jnp.arange(owner_count, dtype=jnp.int32)
    loads = jnp.sum((block_owner[None, :] == owners[:, None]).astype(jnp.int32), axis=1)
    heavy = jnp.min(jnp.where(loads == jnp.max(loads), owners, owner_count))
    turn = (block_owner - heavy) % owner_count
    own_turn = (owner_index - heavy) % owner_count
    before = (turn[None, :] < turn[:, None]) | (
        (turn[None, :] == turn[:, None]) & (ids[None, :] < ids[:, None])
    )
    position = jnp.sum(before.astype(jnp.int32), axis=1)
    place = (position % group) * per + position // group
    order = jnp.sum(jnp.where(place[None, :] == ids[:, None], ids[None, :], 0), axis=1)

    first = jnp.sum((turn < own_turn).astype(jnp.int32))
    held = jnp.sum((turn == own_turn).astype(jnp.int32))
    early = sends - 1 if blocks - capacity <= group else 0
    is_heavy = own_turn == 0
    own_entry = (first - group_index + group - 1) // group

    def deal(tiles):
        return lax.all_to_all(
            tiles.reshape(group, per, rows, cols), GROUP, split_axis=0, concat_axis=0, tiled=True
        )

    by_entry = order.reshape(group, per)
    partials = grad_parts[0]
    cuts = [(0, early), (early, per)] if early else [(0, per)]
    orders = [pick(by_entry[:, a:b]) for a, b in cuts]
    sent = [reorder(partials, other) for _, other in orders]
    sent[0], right_root = lax.optimization_barrier((sent[0], right_root))
    right_dealt = deal(reorder(right_root, order))
    right_dealt, sent[-1] = lax.optimization_barrier((right_dealt, sent[-1]))
    if early and owner_count == 4 and rows * owner_count == size:
        spread = group // owner_count
        near = first_hop(right_dealt)
        sums = first_sums(partials, sent[0], orders[0][0])
        sums, near = lax.optimization_barrier((sums, near))
        gradient = [last_sums(*sums)]
        middle = next_hop(near, spread)
        gradient.append(last_sums(*first_sums(partials, sent[1], orders[1][0])))
        rights = [near, middle]
    else:
        gradient = [
            last_sums(*first_sums(partials, part, mine)) for part, (mine, _) in zip(sent, orders)
        ]
        rights = [lax.all_gather(right_dealt, "shard", axis=0)]
    gradient = [lax.optimization_barrier(part) for part in gradient]
    grad_blocks = [lax.all_gather(part, "shard", axis=0) for part in gradient]
    left_dealt = deal(reorder(left_root, order))
    partners = jnp.arange(group, dtype=jnp.int32) ^ group_index
    weights_sent = reorder(weights, by_entry[partners].reshape(-1))
    tiles = jnp.concatenate(gradient, axis=0).reshape(per, rows, group, cols)
    tiles = deal(jnp.transpose(tiles, (2, 0, 1, 3)))

    if early:
        grad_blocks[0], left_dealt, weights_sent, tiles, rights = lax.optimization_barrier(
            (grad_blocks[0], left_dealt, weights_sent, tiles, rights)
        )
        if len(rights) == 2:
            downs, ups = zip(*rights, next_hop(rights[1], group // owner_count))
            rights = [right_dealt, *downs, *ups]
        slabs = grams(grad_blocks[0], jnp.arange(early, dtype=jnp.int32))
        slabs, left_dealt, tiles, weights_sent = lax.optimization_barrier(
            (slabs, left_dealt, tiles, weights_sent)
        )
        received = lax.all_to_all(slabs, GROUP, split_axis=0, concat_axis=0, tiled=True)
    adam_m_new, adam_v_new, adam_total = adam(
        tiles.reshape(blocks, rows, cols), place, adam_m, adam_v
    )
    away = weights_sent.reshape(group, per * rows, cols)
    away = [away[:1]] + [
        lax.ppermute(away[k : k + 1], GROUP, [(g, g ^ k) for g in range(group)])
        for k in range(1, group)
    ]
    pieces = [precondition(left_dealt, 0, grad_blocks[0], rights)]
    if early:
        grad_blocks[1], adam_total, pieces[0], away = lax.optimization_barrier(
            (grad_blocks[1], adam_total, pieces[0], away)
        )
    if early:
        pieces.append(precondition(left_dealt, early, grad_blocks[1], rights))
    entry = jnp.where(is_heavy, early, own_entry) - early
    last_slabs = grams(grad_blocks[-1], jnp.clip(entry, 0, per - 1 - early).reshape(1))
    precond_total = jnp.concatenate([total for _, total in pieces], axis=0)

    matrix_range = jnp.arange(MATS, dtype=jnp.int32)
    onehot = (block_matrix[:, None] == matrix_range[None, :]).astype(jnp.float32)
    own_order = lax.dynamic_slice_in_dim(order, group_index * per, per)
    own_onehot = jnp.sum(
        jnp.where((own_order[:, None] == ids[None, :])[:, :, None], onehot[None, :, :], 0.0), axis=1
    )
    adam_part = jnp.sum(jnp.sum(adam_total, axis=(1, 2))[:, None] * onehot, axis=0)
    shampoo_part = jnp.sum(jnp.sum(precond_total, axis=(1, 2))[:, None] * own_onehot, axis=0)
    parts = jnp.pad(jnp.stack([adam_part, shampoo_part]), ((0, 6), (0, LANES - MATS)))
    if early:
        received, last_slabs, parts = lax.optimization_barrier((received, last_slabs, parts))
    devices = owner_count * group
    parts = lax.all_to_all(
        jnp.broadcast_to(parts[None], (devices,) + parts.shape), ALL, 0, 0, tiled=True
    )
    adam_norm, shampoo_norm = jnp.sum(parts, axis=0)[:2, :MATS]
    counts = jnp.sum(onehot, axis=0) * float(size * size)
    graft_scale = jnp.sqrt(adam_norm / (shampoo_norm + FLOOR_RATE * counts))
    block_scale = jnp.sum(own_onehot * graft_scale[None, :], axis=1)

    last = lax.all_to_all(last_slabs, GROUP, split_axis=0, concat_axis=0, tiled=True)
    updated = [
        update(away, a, piece, block_scale[a:b], group_index)
        for (a, b), (piece, _) in zip(cuts, pieces)
    ]
    if len(updated) == 1:
        updated = [updated[0][: per // 2], updated[0][per // 2 :]]
    stats = ()
    if early:
        ranks = jnp.arange(early * group, dtype=jnp.int32)
        base = jnp.where(is_heavy, 0, capacity - early * group)
        filled = jnp.where(is_heavy, 1, 0) * jnp.ones_like(ranks)
        stats = refresh(
            left_stat, right_stat, received, base, ranks % group, ranks // group, filled, stats
        )
    base = jnp.where(is_heavy, early * group, 0)
    ranks = base + jnp.arange(capacity - early * group, dtype=jnp.int32)
    filled = (ranks < held).astype(jnp.int32)
    source = (first + ranks) % group
    nothing = jnp.zeros_like(ranks)
    finish = lambda earlier: refresh(
        left_stat, right_stat, last, base, source, nothing, filled, earlier
    )
    new_weights, (left_new, right_new) = gather_blocks(*updated, by_entry, stats, finish)

    factor_m_new, factor_v_new, factor_step = adam_direction(
        factor_grad.astype(jnp.float32), factor_m, factor_v
    )
    factors_new = factors - LEARNING * (factor_step + DECAY_RATE * factors)
    return (
        new_weights,
        adam_m_new,
        adam_v_new,
        left_new,
        right_new,
        factors_new,
        factor_m_new,
        factor_v_new,
    )


def solution(mesh):
    tile = P(None, "shard", GROUP)
    stat = P("shard", None, GROUP)
    factor = P("shard", GROUP)
    in_specs = (P(GROUP, None, "shard", None), tile, tile, tile, stat, stat, tile, tile, P(), P())
    out_specs = (P(None, "shard", None), tile, tile, stat, stat)
    return jax.shard_map(
        shards,
        mesh=mesh,
        in_specs=in_specs + (factor,) * 4,
        out_specs=out_specs + (factor,) * 3,
        check_vma=False,
    )
```

```python
import functools

import jax
import jax.numpy as jnp
from jax import lax
from jax.experimental import pallas as pl
from jax.experimental.pallas import tpu as pltpu
from jax.sharding import PartitionSpec as P

MATS = 5

BETA_ONE = 0.9
BETA_TWO = 0.95
BETA_STAT = 0.95
LEARNING = 0.1
DECAY_RATE = 0.1
EPSILON = 1e-08
FLOOR_RATE = 1e-06
CORRECT_ONE = 1.0 - 0.9**10
CORRECT_TWO = 1.0 - 0.95**10

GROUP = ("tensor", "section")
ALL = ("shard", "tensor", "section")
VMEM_LIMIT = 48 * 1024 * 1024
LANES = 128
SMALL = pl.CostEstimate(flops=0, bytes_accessed=0, transcendentals=0)


def params():
    return pltpu.CompilerParams(vmem_limit_bytes=VMEM_LIMIT)


def adam_direction(grad_float, moment, second):
    moment_new = BETA_ONE * moment + (1.0 - BETA_ONE) * grad_float
    second_new = BETA_TWO * second + (1.0 - BETA_TWO) * grad_float * grad_float
    direction = moment_new / CORRECT_ONE / (jnp.sqrt(second_new / CORRECT_TWO) + EPSILON)
    return (moment_new, second_new, direction)


def copy_blocks(pairs, held, arrived, left):
    into = [
        pltpu.make_async_copy(source, held.at[i], arrived.at[i])
        for i, (source, _) in enumerate(pairs)
    ]
    out_of = [
        pltpu.make_async_copy(held.at[i], target, left.at[i]) for i, (_, target) in enumerate(pairs)
    ]
    for copy in into:
        copy.start()
    for arrival, copy in zip(into, out_of):
        arrival.wait()
        copy.start()
    for copy in out_of:
        copy.wait()


def copy_scratch(count, tile, kind):
    return [
        pltpu.VMEM((count,) + tile, kind),
        pltpu.SemaphoreType.DMA((count,)),
        pltpu.SemaphoreType.DMA((count,)),
    ]


def reorder_kernel(order, blocks, out, held, arrived, left):
    pairs = [(blocks.at[order[i]], out.at[i]) for i in range(out.shape[0])]
    copy_blocks(pairs, held, arrived, left)


def reorder(blocks, order):
    count, tile = order.shape[0], blocks.shape[1:]
    return pl.pallas_call(
        reorder_kernel,
        grid_spec=pltpu.PrefetchScalarGridSpec(
            num_scalar_prefetch=1,
            grid=(1,),
            in_specs=[pl.BlockSpec(memory_space=pl.ANY)],
            out_specs=pl.BlockSpec(memory_space=pl.ANY),
            scratch_shapes=copy_scratch(count, tile, blocks.dtype),
        ),
        out_shape=jax.ShapeDtypeStruct((count,) + tile, blocks.dtype),
        compiler_params=params(),
        cost_estimate=SMALL,
    )(order, blocks)


def place_kernel(sources, target, *refs):
    out, held, arrived, left = refs[-4:]
    blocks = [ref.at[i] for ref in refs[:sources] for i in range(ref.shape[0])]
    pairs = [(block, out.at[target[i]]) for i, block in enumerate(blocks)]
    copy_blocks(pairs, held, arrived, left)


def place_blocks(arrays, target, total, earlier):
    tile, kind = arrays[0].shape[1:], arrays[0].dtype
    inputs = list(arrays) + list(earlier)
    return pl.pallas_call(
        functools.partial(place_kernel, len(arrays)),
        grid_spec=pltpu.PrefetchScalarGridSpec(
            num_scalar_prefetch=1,
            grid=(1,),
            in_specs=[pl.BlockSpec(memory_space=pl.ANY)] * len(inputs),
            out_specs=pl.BlockSpec(memory_space=pl.ANY),
            scratch_shapes=copy_scratch(target.shape[0], tile, kind),
        ),
        out_shape=jax.ShapeDtypeStruct((total,) + tile, kind),
        input_output_aliases={1 + len(arrays) + i: i for i in range(len(earlier))},
        compiler_params=params(),
        cost_estimate=SMALL,
    )(target, *inputs)


def adam_kernel(place, grad, moment, second, moment_out, second_out, total):
    moment_new, second_new, direction = adam_direction(
        grad[0].astype(jnp.float32), moment[0], second[0]
    )
    moment_out[0] = moment_new
    second_out[0] = second_new
    total[0] = jnp.sum(direction * direction, axis=0, keepdims=True)


def adam(grad_tiles, place, moment, second):
    count, rows, cols = moment.shape
    own = pl.BlockSpec((1, rows, cols), lambda i, place: (i, 0, 0))
    return pl.pallas_call(
        adam_kernel,
        grid_spec=pltpu.PrefetchScalarGridSpec(
            num_scalar_prefetch=1,
            grid=(count,),
            in_specs=[
                pl.BlockSpec((1, rows, cols), lambda i, place: (place[i], 0, 0)),
                own,
                own,
            ],
            out_specs=[own, own, pl.BlockSpec((1, 1, cols), lambda i, place: (i, 0, 0))],
        ),
        out_shape=[
            jax.ShapeDtypeStruct(moment.shape, jnp.float32),
            jax.ShapeDtypeStruct(moment.shape, jnp.float32),
            jax.ShapeDtypeStruct((count, 1, cols), jnp.float32),
        ],
        compiler_params=params(),
        cost_estimate=SMALL,
    )(place, grad_tiles, moment, second)


def gram_kernel(chosen, grad, out):
    parts, _, rows, width = grad.shape
    size = parts * rows
    whole = grad[:, 0].reshape(size, width)
    turned = whole.T
    step = 2 * LANES
    for start in range(0, size, step):
        left = lax.dot_general(
            whole,
            whole[start : start + step, :],
            (((1,), (1,)), ((), ())),
            preferred_element_type=jnp.float32,
        ).astype(jnp.bfloat16)
        right = lax.dot_general(
            turned,
            whole[:, start : start + step],
            (((1,), (0,)), ((), ())),
            preferred_element_type=jnp.float32,
        ).astype(jnp.bfloat16)
        for half in range(2):
            slab = start // LANES + half
            out[slab, 0, 0] = left[:, half * LANES : (half + 1) * LANES]
            out[slab, 0, 1] = right[:, half * LANES : (half + 1) * LANES]


def grams(grad_blocks, chosen):
    shards, per, rows, width = grad_blocks.shape
    size = shards * rows
    slabs = size // LANES
    count = chosen.shape[0]
    return pl.pallas_call(
        gram_kernel,
        grid_spec=pltpu.PrefetchScalarGridSpec(
            num_scalar_prefetch=1,
            grid=(count,),
            in_specs=[
                pl.BlockSpec((shards, 1, rows, width), lambda j, chosen: (0, chosen[j], 0, 0))
            ],
            out_specs=pl.BlockSpec(
                (slabs, 1, 2, size, LANES), lambda j, chosen: (0, j, 0, 0, 0)
            ),
        ),
        out_shape=jax.ShapeDtypeStruct((slabs, count, 2, size, LANES), jnp.bfloat16),
        compiler_params=params(),
        cost_estimate=SMALL,
    )(chosen, grad_blocks)


def stat_kernel(
    base, source, entry, filled, left_stat, right_stat, left_gram, right_gram, *refs
):
    left_out, right_out = refs[-2:]
    full = filled[pl.program_id(0)] > 0
    left = left_gram[0, 0, 0].astype(jnp.float32)
    right = right_gram[0, 0, 0].astype(jnp.float32)
    left_out[0] = BETA_STAT * left_stat[0] + jnp.where(full, (1.0 - BETA_STAT) * left, 0.0)
    right_out[0] = BETA_STAT * right_stat[0] + jnp.where(full, (1.0 - BETA_STAT) * right, 0.0)


def refresh(left_stat, right_stat, received, base, source, entry, filled, earlier):
    slots, size, cols = left_stat.shape
    count = source.shape[0]
    own = pl.BlockSpec((1, size, cols), lambda r, base, source, entry, filled: (base[0] + r, 0, 0))
    gram = (1, 1, 1, size, cols)
    shape = jax.ShapeDtypeStruct(left_stat.shape, jnp.float32)
    return pl.pallas_call(
        stat_kernel,
        grid_spec=pltpu.PrefetchScalarGridSpec(
            num_scalar_prefetch=4,
            grid=(count,),
            in_specs=[
                own,
                own,
                pl.BlockSpec(
                    gram, lambda r, base, source, entry, filled: (source[r], entry[r], 0, 0, 0)
                ),
                pl.BlockSpec(
                    gram, lambda r, base, source, entry, filled: (source[r], entry[r], 1, 0, 0)
                ),
            ]
            + [pl.BlockSpec(memory_space=pl.ANY)] * len(earlier),
            out_specs=[own, own],
        ),
        out_shape=[shape, shape],
        input_output_aliases={8 + i: i for i in range(len(earlier))},
        compiler_params=params(),
        cost_estimate=SMALL,
    )(
        base.reshape(1), source, entry, filled, left_stat, right_stat, received, received, *earlier
    )


def left_product(left, grad):
    slabs, _, rows, _ = left.shape
    left_rows = jnp.concatenate([left[s, 0] for s in range(slabs)], axis=1)
    whole = grad[:, 0].reshape(grad.shape[0] * rows, grad.shape[3])
    return jnp.dot(left_rows, whole, preferred_element_type=jnp.float32).astype(jnp.bfloat16)


def precond_kernel(left, grad, right, out, total):
    slabs, _, rows, cols = left.shape
    parts = grad.shape[0]
    mixed = left_product(left, grad)
    total[...] = jnp.zeros_like(total)
    step = 2
    for start in range(0, slabs, step):
        columns = jnp.concatenate(
            [right[:, s, 0].reshape(parts * rows, cols) for s in range(start, start + step)], axis=1
        )
        piece = jnp.dot(mixed, columns, preferred_element_type=jnp.float32)
        out[0, :, start * cols : (start + step) * cols] = piece.astype(jnp.bfloat16)
        square = jnp.sum(piece * piece, axis=0, keepdims=True)
        total[0] += square[:, :cols] + square[:, cols:]


def tile_sources(mine, count, spread):
    found = {(mine, b): (0, spread * b) for b in range(count)}
    for hop in range(1, count):
        for i in range(count - hop):
            if mine + hop < count:
                found[mine + hop, (mine + hop + i) % count] = (hop, spread * i)
            if mine - hop >= 0:
                found[mine - hop, (mine - hop - i) % count] = (count - 1 + hop, spread * i)
    return found


def precond_tiles_kernel(me, left, grad, *refs):
    rights, out, total = refs[:-2], refs[-2], refs[-1]
    slabs, _, rows, cols = left.shape
    parts = grad.shape[0]
    spread = slabs // parts
    mixed = left_product(left, grad)
    total[...] = jnp.zeros_like(total)
    for mine in range(parts):

        @pl.when(me[0] == mine)
        def _(mine=mine):
            found = tile_sources(mine, parts, spread)
            for b in range(parts):
                piece = jnp.zeros((rows, spread * cols), jnp.float32)
                for a in range(parts):
                    turned = (a, b) not in found
                    array, first = found[(b, a) if turned else (a, b)]
                    tile = jnp.concatenate(
                        [rights[array][first + s, 0] for s in range(spread)], axis=1
                    )
                    piece += lax.dot_general(
                        mixed[:, a * rows : (a + 1) * rows],
                        tile,
                        (((1,), (1 if turned else 0,)), ((), ())),
                        preferred_element_type=jnp.float32,
                    )
                out[0, :, b * rows : (b + 1) * rows] = piece.astype(jnp.bfloat16)
                square = jnp.sum(piece * piece, axis=0, keepdims=True)
                total[0] += sum(square[:, s * cols : (s + 1) * cols] for s in range(spread))


def first_hop(right):
    slabs, per, rows, cols = right.shape
    count, me = lax.axis_size("shard"), lax.axis_index("shard")
    spread = slabs // count
    lane = jnp.arange(spread * (count - 1), dtype=jnp.int32)
    moved = []
    for sign in (1, -1):
        tiles = (me + sign * (lane // spread)) % count
        picked = reorder(right.reshape(slabs, per * rows, cols), tiles * spread + lane % spread)
        moved.append(picked.reshape(lane.shape[0], per, rows, cols))
    return hop(moved)


def hop(moved):
    count = lax.axis_size("shard")
    down = [(a, a - 1) for a in range(1, count)]
    up = [(a, a + 1) for a in range(count - 1)]
    return lax.ppermute(moved[0], "shard", down), lax.ppermute(moved[1], "shard", up)


def next_hop(moved, spread):
    return hop([part[: part.shape[0] - spread] for part in moved])


def precondition(left, start, grad_blocks, rights):
    shards, count, rows, width = grad_blocks.shape
    slabs, _, _, cols = left.shape
    size = shards * rows
    whole = len(rights) == 1
    if whole:
        right_specs = [pl.BlockSpec((shards, slabs, 1, rows, cols), lambda m, me: (0, 0, start + m, 0, 0))]
    else:
        right_specs = [
            pl.BlockSpec((right.shape[0], 1, rows, cols), lambda m, me: (0, start + m, 0, 0))
            for right in rights
        ]
    body = precond_tiles_kernel
    if whole:
        body = lambda me, *refs: precond_kernel(*refs)
    return pl.pallas_call(
        body,
        grid_spec=pltpu.PrefetchScalarGridSpec(
            num_scalar_prefetch=1,
            grid=(count,),
            in_specs=[
                pl.BlockSpec((slabs, 1, rows, cols), lambda m, me: (0, start + m, 0, 0)),
                pl.BlockSpec((shards, 1, rows, width), lambda m, me: (0, m, 0, 0)),
            ]
            + right_specs,
            out_specs=[
                pl.BlockSpec((1, rows, width), lambda m, me: (m, 0, 0)),
                pl.BlockSpec((1, 1, cols), lambda m, me: (m, 0, 0)),
            ],
        ),
        out_shape=[
            jax.ShapeDtypeStruct((count, rows, width), jnp.bfloat16),
            jax.ShapeDtypeStruct((count, 1, cols), jnp.float32),
        ],
        compiler_params=params(),
        cost_estimate=SMALL,
    )(lax.axis_index("shard").reshape(1), left, grad_blocks, *rights)


def update_kernel(me, scale, precond, *refs):
    weights, out = refs[:-1], refs[-1]
    factor = scale[pl.program_id(0)]
    cols = weights[0].shape[2]
    for k, slab in enumerate(weights):
        here = pl.ds(pl.multiple_of((me[0] ^ k) * cols, cols), cols)
        old = slab[0].astype(jnp.float32)
        step = factor * precond[0, :, here].astype(jnp.float32) + DECAY_RATE * old
        out[0, :, here] = (old - LEARNING * step).astype(jnp.bfloat16)


def update(weights, start, precond, scale, me):
    count, rows, width = precond.shape
    cols = weights[0].shape[2]
    own = pl.BlockSpec((1, rows, width), lambda m, me, scale: (m, 0, 0))
    return pl.pallas_call(
        update_kernel,
        grid_spec=pltpu.PrefetchScalarGridSpec(
            num_scalar_prefetch=2,
            grid=(count,),
            in_specs=[own]
            + [pl.BlockSpec((1, rows, cols), lambda m, me, scale: (0, start + m, 0))]
            * len(weights),
            out_specs=own,
        ),
        out_shape=jax.ShapeDtypeStruct((count, rows, width), jnp.bfloat16),
        compiler_params=params(),
        cost_estimate=SMALL,
    )(me.reshape(1), scale, precond, *weights)


def pair_kernel(picked, first, second, third, fourth, received, send_a, keep_a, send_b, keep_b):
    half = first.shape[1] // 2
    added = [
        (own[0].astype(jnp.float32) + received[u].astype(jnp.float32)).astype(jnp.bfloat16)
        for u, own in enumerate((first, second, third, fourth))
    ]
    for ref, chosen, start in (
        (send_a, (1, 3), 0),
        (keep_a, (0, 2), 0),
        (send_b, (2, 3), half),
        (keep_b, (0, 1), half),
    ):
        for i, u in enumerate(chosen):
            ref[i, 0] = added[u][start : start + half]


def add_pair(partials, received, picked):
    _, rows, width = partials.shape
    count = received.shape[0] // 4
    half = jax.ShapeDtypeStruct((2, count, rows // 2, width), partials.dtype)

    def own(u):
        return pl.BlockSpec((1, rows, width), lambda i, picked: (picked[4 * i + u], 0, 0))

    return pl.pallas_call(
        pair_kernel,
        grid_spec=pltpu.PrefetchScalarGridSpec(
            num_scalar_prefetch=1,
            grid=(count,),
            in_specs=[own(0), own(1), own(2), own(3)]
            + [pl.BlockSpec((4, rows, width), lambda i, picked: (i, 0, 0))],
            out_specs=[pl.BlockSpec((2, 1, rows // 2, width), lambda i, picked: (0, i, 0, 0))] * 4,
        ),
        out_shape=[half] * 4,
        compiler_params=params(),
        cost_estimate=SMALL,
    )(picked, partials, partials, partials, partials, received)


def add(one, two):
    return (one.astype(jnp.float32) + two.astype(jnp.float32)).astype(jnp.bfloat16)


def swap(array, bit):
    devices = lax.axis_size("tensor")
    return lax.ppermute(array, "tensor", [(t, t ^ bit) for t in range(devices)])


def swap_core(array):
    return lax.ppermute(array, "section", [(0, 1), (1, 0)])


def pick(picked):
    core = lax.axis_index("section")
    relative = jnp.arange(4, dtype=jnp.int32) ^ lax.axis_index("tensor")
    mine = jnp.take(picked, relative * 2 + core, axis=0).T.reshape(-1)
    other = jnp.take(picked, relative * 2 + 1 - core, axis=0).T.reshape(-1)
    return mine, other


def first_sums(partials, sent, mine):
    received = swap_core(sent)
    send_a, keep_a, send_b, keep_b = add_pair(partials, received, mine)
    return add(keep_a, swap(send_a, 1)), add(keep_b, swap(send_b, 2))


def last_sums(sum_a, sum_b):
    last_a = add(sum_a[0], swap(sum_a[1], 2))
    last_b = add(sum_b[0], swap(sum_b[1], 1))
    return jnp.concatenate([last_a, last_b], axis=1)


def gather_blocks(first, second, by_entry, early_work, finish):
    total = by_entry.size
    cut = first.shape[0]
    tensor, core = lax.axis_index("tensor"), lax.axis_index("section")
    x_first, y_second = swap(first, 1), swap(second, 2)
    y_first, x_second = swap(first, 2), swap(second, 1)
    x_first, y_second, early_work = lax.optimization_barrier((x_first, y_second, early_work))
    d_first, d_second = swap(x_first, 2), swap(y_second, 1)

    def targets(bits, core):
        places = [by_entry[(tensor ^ bit) * 2 + core] for bit in bits]
        return [piece for place in places for piece in (place[:cut], place[cut:])]

    near = [first, second, x_first, x_second, y_first, y_second]
    near_target = targets((0, 1, 2), core) + targets((0, 1, 2), 1 - core)
    near = near + [swap_core(piece) for piece in near]
    placed = place_blocks(near, jnp.concatenate(near_target), total, [])
    late_work = finish(early_work)
    d_first, d_second, placed, late_work = lax.optimization_barrier(
        (d_first, d_second, placed, late_work)
    )
    far = [d_first, d_second]
    far_target = targets((3,), core) + targets((3,), 1 - core)
    far = far + [swap_core(piece) for piece in far]
    return place_blocks(far, jnp.concatenate(far_target), total, [placed]), late_work


def shards(
    grad_parts,
    weights,
    adam_m,
    adam_v,
    left_stat,
    right_stat,
    left_root,
    right_root,
    block_owner,
    block_matrix,
    factors,
    factor_grad,
    factor_m,
    factor_v,
):
    capacity = left_stat.shape[0]
    blocks, rows, cols = weights.shape
    size = left_stat.shape[1]
    group = size // cols
    per = blocks // group
    sends = -(-capacity // group)
    owner_index = lax.axis_index("shard")
    group_index = lax.axis_index(GROUP)
    owner_count = lax.axis_size("shard")

    ids = jnp.arange(blocks, dtype=jnp.int32)
    owners = jnp.arange(owner_count, dtype=jnp.int32)
    loads = jnp.sum((block_owner[None, :] == owners[:, None]).astype(jnp.int32), axis=1)
    heavy = jnp.min(jnp.where(loads == jnp.max(loads), owners, owner_count))
    turn = (block_owner - heavy) % owner_count
    own_turn = (owner_index - heavy) % owner_count
    before = (turn[None, :] < turn[:, None]) | (
        (turn[None, :] == turn[:, None]) & (ids[None, :] < ids[:, None])
    )
    position = jnp.sum(before.astype(jnp.int32), axis=1)
    place = (position % group) * per + position // group
    order = jnp.sum(jnp.where(place[None, :] == ids[:, None], ids[None, :], 0), axis=1)

    first = jnp.sum((turn < own_turn).astype(jnp.int32))
    held = jnp.sum((turn == own_turn).astype(jnp.int32))
    early = sends - 1 if blocks - capacity <= group else 0
    is_heavy = own_turn == 0
    own_entry = (first - group_index + group - 1) // group

    def deal(tiles):
        return lax.all_to_all(
            tiles.reshape(group, per, rows, cols), GROUP, split_axis=0, concat_axis=0, tiled=True
        )

    by_entry = order.reshape(group, per)
    partials = grad_parts[0]
    cuts = [(0, early), (early, per)] if early else [(0, per)]
    orders = [pick(by_entry[:, a:b]) for a, b in cuts]
    sent = [reorder(partials, other) for _, other in orders]
    sent[0], right_root = lax.optimization_barrier((sent[0], right_root))
    right_dealt = deal(reorder(right_root, order))
    right_dealt, sent[-1] = lax.optimization_barrier((right_dealt, sent[-1]))
    if early and owner_count == 4 and rows * owner_count == size:
        spread = group // owner_count
        near = first_hop(right_dealt)
        sums = first_sums(partials, sent[0], orders[0][0])
        sums, near = lax.optimization_barrier((sums, near))
        gradient = [last_sums(*sums)]
        middle = next_hop(near, spread)
        gradient.append(last_sums(*first_sums(partials, sent[1], orders[1][0])))
        rights = [near, middle]
    else:
        gradient = [
            last_sums(*first_sums(partials, part, mine)) for part, (mine, _) in zip(sent, orders)
        ]
        rights = [lax.all_gather(right_dealt, "shard", axis=0)]
    gradient = [lax.optimization_barrier(part) for part in gradient]
    grad_blocks = [lax.all_gather(part, "shard", axis=0) for part in gradient]
    left_dealt = deal(reorder(left_root, order))
    partners = jnp.arange(group, dtype=jnp.int32) ^ group_index
    weights_sent = reorder(weights, by_entry[partners].reshape(-1))
    tiles = jnp.concatenate(gradient, axis=0).reshape(per, rows, group, cols)
    tiles = deal(jnp.transpose(tiles, (2, 0, 1, 3)))

    if early:
        grad_blocks[0], left_dealt, weights_sent, tiles, rights = lax.optimization_barrier(
            (grad_blocks[0], left_dealt, weights_sent, tiles, rights)
        )
        if len(rights) == 2:
            downs, ups = zip(*rights, next_hop(rights[1], group // owner_count))
            rights = [right_dealt, *downs, *ups]
        slabs = grams(grad_blocks[0], jnp.arange(early, dtype=jnp.int32))
        slabs, left_dealt, tiles, weights_sent = lax.optimization_barrier(
            (slabs, left_dealt, tiles, weights_sent)
        )
        received = lax.all_to_all(slabs, GROUP, split_axis=0, concat_axis=0, tiled=True)
    adam_m_new, adam_v_new, adam_total = adam(
        tiles.reshape(blocks, rows, cols), place, adam_m, adam_v
    )
    pieces = [precondition(left_dealt, 0, grad_blocks[0], rights)]
    adam_total, pieces[0], weights_sent = lax.optimization_barrier(
        (adam_total, pieces[0], weights_sent)
    )
    away = weights_sent.reshape(group, per * rows, cols)
    away = [away[:1]] + [
        lax.ppermute(away[k : k + 1], GROUP, [(g, g ^ k) for g in range(group)])
        for k in range(1, group)
    ]
    if early:
        grad_blocks[1], adam_total, pieces[0] = lax.optimization_barrier(
            (grad_blocks[1], adam_total, pieces[0])
        )
        pieces.append(precondition(left_dealt, early, grad_blocks[1], rights))
    entry = jnp.where(is_heavy, early, own_entry) - early
    last_slabs = grams(grad_blocks[-1], jnp.clip(entry, 0, per - 1 - early).reshape(1))
    precond_total = jnp.concatenate([total for _, total in pieces], axis=0)

    matrix_range = jnp.arange(MATS, dtype=jnp.int32)
    onehot = (block_matrix[:, None] == matrix_range[None, :]).astype(jnp.float32)
    own_order = lax.dynamic_slice_in_dim(order, group_index * per, per)
    own_onehot = jnp.sum(
        jnp.where((own_order[:, None] == ids[None, :])[:, :, None], onehot[None, :, :], 0.0), axis=1
    )
    adam_part = jnp.sum(jnp.sum(adam_total, axis=(1, 2))[:, None] * onehot, axis=0)
    shampoo_part = jnp.sum(jnp.sum(precond_total, axis=(1, 2))[:, None] * own_onehot, axis=0)
    parts = jnp.pad(jnp.stack([adam_part, shampoo_part]), ((0, 6), (0, LANES - MATS)))
    if early:
        received, last_slabs, parts, away = lax.optimization_barrier(
            (received, last_slabs, parts, away)
        )
    devices = owner_count * group
    parts = lax.all_to_all(
        jnp.broadcast_to(parts[None], (devices,) + parts.shape), ALL, 0, 0, tiled=True
    )
    adam_norm, shampoo_norm = jnp.sum(parts, axis=0)[:2, :MATS]
    counts = jnp.sum(onehot, axis=0) * float(size * size)
    graft_scale = jnp.sqrt(adam_norm / (shampoo_norm + FLOOR_RATE * counts))
    block_scale = jnp.sum(own_onehot * graft_scale[None, :], axis=1)

    last = lax.all_to_all(last_slabs, GROUP, split_axis=0, concat_axis=0, tiled=True)
    updated = [
        update(away, a, piece, block_scale[a:b], group_index)
        for (a, b), (piece, _) in zip(cuts, pieces)
    ]
    if len(updated) == 1:
        updated = [updated[0][: per // 2], updated[0][per // 2 :]]
    stats = ()
    if early:
        ranks = jnp.arange(early * group, dtype=jnp.int32)
        base = jnp.where(is_heavy, 0, capacity - early * group)
        filled = jnp.where(is_heavy, 1, 0) * jnp.ones_like(ranks)
        stats = refresh(
            left_stat, right_stat, received, base, ranks % group, ranks // group, filled, stats
        )
    base = jnp.where(is_heavy, early * group, 0)
    ranks = base + jnp.arange(capacity - early * group, dtype=jnp.int32)
    filled = (ranks < held).astype(jnp.int32)
    source = (first + ranks) % group
    nothing = jnp.zeros_like(ranks)
    finish = lambda earlier: refresh(
        left_stat, right_stat, last, base, source, nothing, filled, earlier
    )
    new_weights, (left_new, right_new) = gather_blocks(*updated, by_entry, stats, finish)

    factor_m_new, factor_v_new, factor_step = adam_direction(
        factor_grad.astype(jnp.float32), factor_m, factor_v
    )
    factors_new = factors - LEARNING * (factor_step + DECAY_RATE * factors)
    return (
        new_weights,
        adam_m_new,
        adam_v_new,
        left_new,
        right_new,
        factors_new,
        factor_m_new,
        factor_v_new,
    )


def solution(mesh):
    tile = P(None, "shard", GROUP)
    stat = P("shard", None, GROUP)
    factor = P("shard", GROUP)
    in_specs = (P(GROUP, None, "shard", None), tile, tile, tile, stat, stat, tile, tile, P(), P())
    out_specs = (P(None, "shard", None), tile, tile, stat, stat)
    return jax.shard_map(
        shards,
        mesh=mesh,
        in_specs=in_specs + (factor,) * 4,
        out_specs=out_specs + (factor,) * 3,
        check_vma=False,
    )
```
